128 devices in a mesh: dp: 8 (over z_hi, x), fsdp: 16 (over z_lo, y, core).
Axes of the slice: x: 4, y: 4, z: 4 (z_hi: 2, z_lo: 2; z = z_hi * 2 + z_lo), core: 2. Of those that a mesh axis runs over, the one named last changes fastest.
Arguments:
- tokens: bfloat16 [32768, 1152], P(('dp', 'fsdp')), may hold values from -6 to 6
- segments: int32 [128, 256], P(('dp', 'fsdp')), may hold values from 0 to 3, never falling along the last dimension, each value on 1 to 128 neighbouring positions
- attn_gain: bfloat16 [1152], P(('dp', 'fsdp')), may hold values from 0.5 to 1.5
- w_query: bfloat16 [1152, 1152], P(('dp', 'fsdp')), may hold values from -0.1875 to 0.1875
- w_key: bfloat16 [1152, 384], P(('dp', 'fsdp')), may hold values from -0.1875 to 0.1875
- w_value: bfloat16 [1152, 384], P(('dp', 'fsdp')), may hold values from -0.1875 to 0.1875
- w_out: bfloat16 [1152, 1152], P(('dp', 'fsdp')), may hold values from -0.75 to 0.75
- mlp_gain: bfloat16 [1152], P(('dp', 'fsdp')), may hold values from 0.5 to 1.5
- w_gate: bfloat16 [1152, 3072], P(('dp', 'fsdp')), may hold values from -0.1875 to 0.1875
- w_up: bfloat16 [1152, 3072], P(('dp', 'fsdp')), may hold values from -0.1875 to 0.1875
- w_down: bfloat16 [3072, 1152], P(('dp', 'fsdp')), may hold values from -0.15625 to 0.15625
- cotangent: bfloat16 [32768, 1152], P(('dp', 'fsdp')), may hold values from -6 to 6
Outputs:
- output: bfloat16 [32768, 1152], P(('dp', 'fsdp'))
- grad_input: float32 [32768, 1152], P(('dp', 'fsdp'))
- grad_attn_gain: float32 [1152], P(('dp', 'fsdp'))
- grad_w_query: float32 [1152, 1152], P(('dp', 'fsdp'))
- grad_w_key: float32 [1152, 384], P(('dp', 'fsdp'))
- grad_w_value: float32 [1152, 384], P(('dp', 'fsdp'))
- grad_w_out: float32 [1152, 1152], P(('dp', 'fsdp'))
- grad_mlp_gain: float32 [1152], P(('dp', 'fsdp'))
- grad_w_gate: float32 [1152, 3072], P(('dp', 'fsdp'))
- grad_w_up: float32 [1152, 3072], P(('dp', 'fsdp'))
- grad_w_down: float32 [3072, 1152], P(('dp', 'fsdp'))
The draws below stay inside these ranges and needn't reach their ends.
Inputs may be any that keep to these rules, and one draw needn't show every extreme that they name: `segments`: in each row of 256 tokens the ids never fall; a run of equal ids is one document of at most 128 tokens.
All inputs are finite; a program needn't handle non-finite values.
Results may differ from the reference program's by a relative error of at most 0.03.
Values may be sent and summed in bfloat16 or wider, within the bound.
No kernel may reach another device: no remote copies, remote signals or barrier semaphores. Data moves between devices by JAX's collectives and lax.ppermute only.
A program may use at most 192 MiB of HBM per device.

```python
import math
import jax
import jax.numpy as jnp
import numpy as np
from jax import lax

D = 1152
HEADS = 18
KV_HEADS = 6
HEAD = 64
FF = 3072
TOK_DEV = 256
DOCS = 4
KV = 384
SEQS = 128
TOKENS = 32768


def shard_levels(rng, dims, split, least, high):
    gain = 1.0
    for axis_at, shards_of in split:
        draws = jax.random.uniform(jax.random.fold_in(jax.random.fold_in(rng, 6), axis_at), (shards_of,), jnp.float32, least / len(split), high / len(split))
        gain = gain * jnp.repeat(jnp.exp(draws), dims[axis_at] // shards_of).reshape((-1,) + (1,) * (len(dims) - 1 - axis_at))
    return gain


def length_profile(amount, total, bound, slope):
    portions = [(1 << 20) // math.isqrt(standing ** slope) + 1 for standing in range(2, amount + 1)]
    surplus, given = total - bound - (amount - 1), [1] * (amount - 1)
    while surplus > 0:
        candidates = [i for i in range(amount - 1) if given[i] < bound]
        pool, budget = sum([portions[i] for i in candidates]), surplus
        for i in candidates:
            more = min(bound - given[i], max(1, budget * portions[i] // pool), surplus)
            given[i] = given[i] + more
            surplus = surplus - more
    return np.array([bound] + given)


def uneven(own_key, amount, total, reach, slope):
    if amount == 2:
        one = jax.random.randint(own_key, (), max(1, total - reach), min(reach, total - 1) + 1)
        return jnp.stack([one, total - one])
    tallies = jnp.asarray(length_profile(amount, total, reach, slope), jnp.int32)
    twos = (amount - 1) // 2
    giver, sink = tallies[1:1 + 2 * twos:2], tallies[2:2 + 2 * twos:2]
    margin = jnp.minimum(giver - 1, reach - sink)
    shifted = jax.random.randint(jax.random.fold_in(own_key, 1), (twos,), 0, 1 << 20) % (margin + 1)
    tallies = tallies.at[1:1 + 2 * twos:2].set(giver - shifted).at[2:2 + 2 * twos:2].set(sink + shifted)
    return tallies[jax.random.permutation(jax.random.fold_in(own_key, 2), amount)]


def centred(own_key, extent, spread, most, shards=(), kind=jnp.bfloat16):
    entries = jax.random.normal(own_key, extent, jnp.float32) * spread
    if len(shards) > 0:
        entries = shard_levels(own_key, extent, shards, -0.22, 0.18) * entries
    return jnp.clip(entries, min=-most, max=most).astype(kind)


def setup_inputs(seed: int = 0) -> dict:
    keys = jax.random.split(jax.random.key(seed), 13)
    return {
        "tokens": centred(keys[0], (TOKENS, D), 1.0, 6.0, ((0, 128),)),
        "segments": jax.vmap(lambda own: jnp.searchsorted(jnp.cumsum(uneven(own, DOCS, TOK_DEV, TOK_DEV // 2, 0)), jnp.arange(TOK_DEV), side="right"))(jax.random.split(keys[1], SEQS)).reshape((SEQS, TOK_DEV)).astype(jnp.int32),
        "attn_gain": jnp.clip(1.0 + 0.1 * jax.random.normal(keys[2], (D,), jnp.float32), 0.5, 1.5).astype(jnp.bfloat16),
        "w_query": centred(keys[3], (D, D), D ** -0.5, 0.1875, ((0, 128),)),
        "w_key": centred(keys[4], (D, KV), D ** -0.5, 0.1875, ((0, 128),)),
        "w_value": centred(keys[5], (D, KV), D ** -0.5, 0.1875, ((0, 128),)),
        "w_out": centred(keys[6], (D, D), (D // 16) ** -0.5, 0.75, ((0, 128),)),
        "mlp_gain": jnp.clip(1.0 + 0.1 * jax.random.normal(keys[7], (D,), jnp.float32), 0.5, 1.5).astype(jnp.bfloat16),
        "w_gate": centred(keys[8], (D, FF), D ** -0.5, 0.1875, ((0, 128),)),
        "w_up": centred(keys[9], (D, FF), D ** -0.5, 0.1875, ((0, 128),)),
        "w_down": centred(keys[10], (FF, D), (FF // 2) ** -0.5, 0.15625, ((0, 128),)),
        "cotangent": centred(keys[11], (TOKENS, D), 1.0, 6.0, ((0, 128),)),
    }


EPS = 1e-05
THETA = 10000.0

@jax.custom_vjp
def low(v):
    return lax.optimization_barrier(v.astype(jnp.bfloat16)).astype(jnp.float32)

@jax.custom_vjp
def low_back(v):
    return v

def low_keep(v):
    return (low(v), None)

def low_pass(kept, grad):
    return (grad,)

def back_keep(v):
    return (v, None)

def back_low(kept, grad):
    return (low(grad),)
low.defvjp(low_keep, low_pass)
low_back.defvjp(back_keep, back_low)

def product(left, right):
    return jnp.dot(left, right, precision=lax.Precision.HIGHEST, preferred_element_type=jnp.float32)

def norm_scale(values):
    return lax.rsqrt(lax.optimization_barrier(jnp.mean(values * values, axis=-1, keepdims=True)) + EPS)

def scaled_norm(values, gain_vec):
    return values * norm_scale(values) * gain_vec

def swish_product(gate_in, up_in):
    return gate_in * jax.nn.sigmoid(gate_in) * up_in

def rotate(values, cos_table, sin_table):
    half_size = values.shape[-1] // 2
    first_half = values[..., :half_size]
    second_half = values[..., half_size:]
    return jnp.concatenate([first_half * cos_table - second_half * sin_table, second_half * cos_table + first_half * sin_table], axis=-1)

def row_tables(segment_row, head_size):
    length = segment_row.shape[0]
    places = jnp.arange(length, dtype=jnp.int32)
    same_doc = segment_row[:, None] == segment_row[None, :]
    starts = lax.optimization_barrier(jnp.min(jnp.where(same_doc, places[None, :], length), axis=1))
    offsets = (places - starts).astype(jnp.float32)
    frequency = jnp.exp(jnp.arange(head_size // 2, dtype=jnp.float32) * (-2.0 * math.log(THETA) / head_size))
    angles = offsets[:, None] * frequency[None, :]
    allowed = same_doc & (places[:, None] >= places[None, :])
    return (jnp.cos(angles)[:, None, :], jnp.sin(angles)[:, None, :], allowed)

def attend(pieces):
    queries, keys_rot, values, allowed = pieces
    group_size = HEADS // KV_HEADS
    keys_all = jnp.repeat(keys_rot, group_size, axis=1)
    values_all = jnp.repeat(values, group_size, axis=1)
    raw_scores = low_back(jnp.einsum('qhd,khd->hqk', queries, keys_all, precision=lax.Precision.HIGHEST))
    scores = jnp.where(allowed[None], raw_scores * HEAD ** (-0.5), -1e+30)
    largest = lax.optimization_barrier(jnp.max(scores, axis=-1, keepdims=True))
    weights = jnp.exp(scores - largest)
    attn_probs = low(weights / lax.optimization_barrier(jnp.sum(weights, axis=-1, keepdims=True)))
    return jnp.einsum('hqk,khd->qhd', attn_probs, values_all, precision=lax.Precision.HIGHEST)

def layer_forward(hidden, params, cos_table, sin_table, allowed):
    attn_gain, w_query, w_key, w_value, w_out, mlp_gain, w_gate, w_up, w_down = params
    batch_rows = allowed.shape[0]
    length = allowed.shape[1]
    normed = low(scaled_norm(hidden, attn_gain))
    queries = low_back(product(normed, w_query)).reshape(batch_rows, length, HEADS, HEAD)
    keys_rot = low_back(product(normed, w_key)).reshape(batch_rows, length, KV_HEADS, HEAD)
    values = low(low_back(product(normed, w_value))).reshape(batch_rows, length, KV_HEADS, HEAD)
    queries = low(rotate(queries, cos_table, sin_table))
    keys_rot = low(rotate(keys_rot, cos_table, sin_table))
    mixed = lax.map(jax.checkpoint(attend), (queries, keys_rot, values, allowed))
    mixed = low(low_back(mixed.reshape(batch_rows * length, HEADS * HEAD)))
    middle = hidden + low_back(product(mixed, w_out))
    normed_two = low(scaled_norm(middle, mlp_gain))
    gate_pre = low_back(product(normed_two, w_gate))
    up_pre = low_back(product(normed_two, w_up))
    activated = low(swish_product(gate_pre, up_pre))
    return middle + low_back(product(activated, w_down))

def reference(tokens, segments, attn_gain, w_query, w_key, w_value, w_out, mlp_gain, w_gate, w_up, w_down, cotangent):
    cos_table, sin_table, allowed = jax.vmap(lambda segment_row: row_tables(segment_row, HEAD))(segments)
    group_rows = math.gcd(SEQS, max(1, 4096 // TOK_DEV))
    blocks = SEQS // group_rows
    params = tuple((weight.astype(jnp.float32) for weight in (attn_gain, w_query, w_key, w_value, w_out, mlp_gain, w_gate, w_up, w_down)))
    hidden = tokens.astype(jnp.float32).reshape(blocks, group_rows * TOK_DEV, D)
    incoming = cotangent.astype(jnp.float32).reshape(blocks, group_rows * TOK_DEV, D)
    cos_table = cos_table.reshape(blocks, group_rows, TOK_DEV, 1, HEAD // 2)
    sin_table = sin_table.reshape(blocks, group_rows, TOK_DEV, 1, HEAD // 2)
    allowed = allowed.reshape(blocks, group_rows, TOK_DEV, TOK_DEV)

    def one_block(totals, pieces):
        rows_in, rows_back, cos_rows, sin_rows, allowed_rows = pieces

        def forward(values_in, weights_in):
            return layer_forward(values_in, weights_in, cos_rows, sin_rows, allowed_rows)
        result, pullback = jax.vjp(forward, rows_in, params)
        grad_rows, grad_params = pullback(rows_back)
        totals = jax.tree.map(lambda left, right: left + right, totals, grad_params)
        return (totals, (result.astype(jnp.bfloat16), grad_rows))
    totals, (outputs, grad_rows) = lax.scan(one_block, jax.tree.map(jnp.zeros_like, params), (hidden, incoming, cos_table, sin_table, allowed))
    return (outputs.reshape(TOKENS, D), grad_rows.reshape(TOKENS, D), totals[0], totals[1], totals[2], totals[3], totals[4], totals[5], totals[6], totals[7], totals[8])
```

```python
import math

import jax
import jax.numpy as jnp
import numpy as np
from jax import lax
from jax.sharding import Mesh
from jax.sharding import PartitionSpec as P

D = 1152
HEADS = 18
KV_HEADS = 6
HEAD = 64
FF = 3072
TOK = 256
EPS = 1e-05
THETA = 10000.0

SHAPE = (2, 4, 2, 4, 2)
AXES = ("z_hi", "x", "z_lo", "y", "core")
BF = jnp.bfloat16
F32 = jnp.float32


def device_pairs(move):
    pairs = []
    for i in range(128):
        zh, x, zl, y, c = (int(v) for v in np.unravel_index(i, SHAPE))
        x, y, z, c = move(x, y, zh * 2 + zl, c)
        x, y, z = x % 4, y % 4, z % 4
        pairs.append((i, int(np.ravel_multi_index((z // 2, x, z % 2, y, c), SHAPE))))
    return pairs


RINGS = {
    "x": device_pairs(lambda x, y, z, c: (x + 1 - 2 * c, y, z, c)),
    "y": device_pairs(lambda x, y, z, c: (x, y + 1 - 2 * c, z, c)),
    "z": device_pairs(lambda x, y, z, c: (x, y, z + 1 - 2 * c, c)),
}
CORES = device_pairs(lambda x, y, z, c: (x, y, z, 1 - c))
TRADE = device_pairs(lambda x, y, z, c: (x, y, c * 2 + z % 2, z // 2))


def send(value, pairs):
    return lax.ppermute(value, AXES, pairs)


def swap(value):
    return send(value, CORES)


def dot(a, b):
    return jnp.dot(a, b, preferred_element_type=F32)


def dot_t(a, b):
    return lax.dot_general(a, b, (((1,), (1,)), ((), ())), preferred_element_type=F32)


def t_dot(a, b):
    return lax.dot_general(a, b, (((0,), (0,)), ((), ())), preferred_element_type=F32)


SHIFTS = {
    axis: [device_pairs(lambda x, y, z, c, n=n: (
        x - (1 - 2 * c) * n * (axis == "x"), y - (1 - 2 * c) * n * (axis == "y"),
        z - (1 - 2 * c) * n * (axis == "z"), c)) for n in range(4)]
    for axis in ("x", "y", "z")
}


class Lockstep:
    def __init__(self):
        self.last = ()

    def __call__(self, values, pairs):
        tied = lax.optimization_barrier((*values, *self.last))
        sent = [send(v, p) for v, p in zip(tied, pairs)]
        self.last = lax.optimization_barrier(tuple(sent))
        return list(self.last)

    def gather(self, blocks, axes):
        held = [[b] for b in blocks]
        for _ in range(3):
            arrived = self([h[-1] for h in held], [RINGS[a] for a in axes])
            for h, block in zip(held, arrived):
                h.append(block)
        return held

    def scatter(self, makers, axes, last_f32=False):
        parts = [make(1).astype(BF) for make in makers]
        for step in (2, 3, 0):
            arrived = self(parts, [RINGS[a] for a in axes])
            parts = [make(step) + a.astype(F32) for make, a in zip(makers, arrived)]
            if step != 0 or not last_f32:
                parts = [p.astype(BF) for p in parts]
        return parts


def place(blocks, at, sign):
    out = jnp.zeros((4, *blocks[0].shape), blocks[0].dtype)
    for step, block in enumerate(blocks):
        out = lax.dynamic_update_index_in_dim(out, block, (at - sign * step) % 4, 0)
    return out


def row_tables(segment_row):
    places = jnp.arange(TOK, dtype=jnp.int32)
    same_doc = segment_row[:, None] == segment_row[None, :]
    starts = jnp.min(jnp.where(same_doc, places[None, :], TOK), axis=1)
    offsets = (places - starts).astype(F32)
    frequency = jnp.exp(jnp.arange(HEAD // 2, dtype=F32) * (-2.0 * math.log(THETA) / HEAD))
    angles = offsets[:, None] * frequency[None, :]
    allowed = same_doc & (places[:, None] >= places[None, :])
    return jnp.cos(angles), jnp.sin(angles), allowed


def rotate(values, cos_table, sin_table):
    first, second = values[..., : HEAD // 2], values[..., HEAD // 2 :]
    return jnp.concatenate(
        [first * cos_table - second * sin_table, second * cos_table + first * sin_table], axis=-1
    )


def unrotate(grads, cos_table, sin_table):
    return rotate(grads, cos_table, -sin_table)


def norm_scale(values):
    return lax.rsqrt(jnp.mean(values * values, axis=-1, keepdims=True) + EPS)


def body(
    tokens, segments, attn_gain, w_query, w_key, w_value, w_out, mlp_gain, w_gate, w_up, w_down,
    cotangent,
):
    core = lax.axis_index("core")
    at = {
        "x": lax.axis_index("x"),
        "y": lax.axis_index("y"),
        "z": lax.axis_index("z_hi") * 2 + lax.axis_index("z_lo"),
    }
    sign = 1 - 2 * core
    first = core == 0

    def halves(w):
        n = w.shape[1] // 2
        low, high = w[:, :n], w[:, n:]
        return jnp.where(first, low, high), jnp.where(first, high, low)

    pairs = [halves(w) for w in (w_gate, w_query, w_up, w_key, w_value)]
    gain_pair = jnp.stack([attn_gain, mlp_gain], axis=1)

    def columns(parts):
        gate, query, up, key, value = parts
        return jnp.concatenate(
            [gate, query[:, :512], up, query[:, 512:], key, value, gain_pair], axis=1
        )

    kept, given = columns([p[0] for p in pairs]), columns([p[1] for p in pairs])
    step = Lockstep()
    given, traded = step(
        [given, jnp.concatenate([w_out, w_down], axis=0)], [CORES, TRADE]
    )
    rows = jnp.concatenate([jnp.where(first, kept, given), jnp.where(first, given, kept)], axis=0)

    tokens_all = jnp.concatenate([tokens, swap(tokens)], axis=0)
    cot = jnp.concatenate([cotangent, swap(cotangent)], axis=0)
    seg_other = swap(segments.astype(F32)).astype(jnp.int32)

    order_a, order_b, order_c = ("x", "z", "y"), ("y", "x", "z"), ("z", "y", "x")

    def natural(order):
        k = jnp.arange(D, dtype=jnp.int32)
        r, t = k % 18, k // 18
        c = {}
        for level, axis in enumerate(order):
            c[axis] = (at[axis] - sign * ((t // 4**level) % 4)) % 4
        chip = (((c["z"] // 2) * 4 + c["x"]) * 2 + c["z"] % 2) * 4 + c["y"]
        return chip * 18 + r

    def natural_out():
        k = jnp.arange(576, dtype=jnp.int32)
        r, t = k % 9, k // 9
        c = {}
        for level, axis in enumerate(order_c):
            c[axis] = (at[axis] - sign * ((t // 4**level) % 4)) % 4
        return (((c["x"] * 2 + c["z"] % 2) * 4 + c["y"]) * 2 + c["z"] // 2) * 9 + r

    def one_hot(index):
        n = index.shape[0]
        return (jnp.arange(n, dtype=jnp.int32)[:, None] == index[None, :]).astype(BF)

    perm_a, perm_b, perm_c = one_hot(natural(order_a)), one_hot(natural(order_b)), one_hot(natural_out())

    one, two, three = zip(order_a, order_b, order_c)
    ha, hb, hc = step.gather([rows[:, :2048], rows[:, 2048:], traded], one)
    c_out = jnp.concatenate([h[:9] for h in hc], axis=0)
    c_down = place([h[9:] for h in hc], at["z"], sign).reshape(2, 2, 24, D)
    c_down = jnp.transpose(c_down, (1, 0, 2, 3)).reshape(96, D)
    ha, hb, hc = step.gather(
        [jnp.concatenate(ha, axis=0), jnp.concatenate(hb, axis=0),
         jnp.concatenate([c_out, c_down], axis=0)], two
    )
    b_a, b_b = lax.optimization_barrier(
        (jnp.concatenate(ha, axis=0), jnp.concatenate(hb, axis=0))
    )
    b_out = jnp.concatenate([h[:36] for h in hc], axis=0)
    b_down = place([h[36:].reshape(2, 48, D) for h in hc], at["y"], sign)
    b_down = jnp.transpose(b_down, (1, 0, 2, 3)).reshape(384, D)
    b_out, b_down = lax.optimization_barrier((b_out, b_down))
    ha, hb, hc = step.gather([b_a[:, 1536:], b_b[:, 1536:], b_out], three)
    wq_a, w_b, w_o = (jnp.concatenate(h, axis=0) for h in (ha, hb, hc))
    ha, hb, hc = step.gather([b_a[:, :1536], b_b[:, :1536], b_down], three)
    wg, wu = (jnp.concatenate(h, axis=0) for h in (ha, hb))
    wd = place(hc, at["x"], sign).reshape(1536, D)
    gains = lax.dot_general(
        w_b[:, 448:], perm_b, (((0,), (1,)), ((), ())), preferred_element_type=F32
    )
    w_b = w_b[:, :448]

    tables = [row_tables(segments[0]), row_tables(seg_other[0])]
    cos_table = jnp.stack([t[0] for t in tables])[:, :, None, :]
    sin_table = jnp.stack([t[1] for t in tables])[:, :, None, :]
    allowed = jnp.stack([t[2] for t in tables])[:, None, None]

    x = tokens_all.astype(F32)
    r1 = norm_scale(x)
    normed = (x * r1 * gains[0]).astype(BF)
    normed_a, normed_b = dot(normed, perm_a).astype(BF), dot(normed, perm_b).astype(BF)
    pre_a, pre_b = dot(normed_a, wq_a), dot(normed_b, w_b)
    q_pre = jnp.concatenate([pre_a, pre_b[:, :64]], axis=1).reshape(2, TOK, 9, HEAD)
    k_pre = pre_b[:, 64:256].reshape(2, TOK, 3, HEAD)
    values = pre_b[:, 256:].astype(BF).reshape(2, TOK, 3, HEAD)
    queries = rotate(q_pre, cos_table, sin_table).astype(BF).reshape(2, TOK, 3, 3, HEAD)
    keys = rotate(k_pre, cos_table, sin_table).astype(BF)
    raw = jnp.einsum("bqkgd,bskd->bkgqs", queries, keys, preferred_element_type=F32)
    scores = jnp.where(allowed, raw * HEAD ** (-0.5), -1e30)
    largest = jnp.max(scores, axis=-1, keepdims=True)
    weights = jnp.exp(scores - largest)
    probs_full = weights / jnp.sum(weights, axis=-1, keepdims=True)
    probs = probs_full.astype(BF)
    mixed = jnp.einsum("bkgqs,bskd->bqkgd", probs, values, preferred_element_type=F32)
    mixed = mixed.reshape(2 * TOK, 576).astype(BF)
    mixed_c = dot(mixed, perm_c).astype(BF)
    part = dot(mixed_c, w_o)
    other = swap(part.astype(BF)).astype(F32)
    middle = x + part + jnp.concatenate([other[TOK:], other[:TOK]], axis=0)

    r2 = norm_scale(middle)
    normed_two = (middle * r2 * gains[1]).astype(BF)
    two_a, two_b = dot(normed_two, perm_a).astype(BF), dot(normed_two, perm_b).astype(BF)
    gate_pre, up_pre = dot(two_a, wg), dot(two_b, wu)
    sig = jax.nn.sigmoid(gate_pre)
    activated = (gate_pre * sig * up_pre).astype(BF)
    part = dot(activated, wd)
    output = (middle[:TOK] + part[:TOK] + swap(part[TOK:].astype(BF)).astype(F32)).astype(BF)
    d_act = dot_t(cot, wd)
    d_gate = (d_act * up_pre * sig * (1 + gate_pre * (1 - sig))).astype(BF)
    d_up = (d_act * gate_pre * sig).astype(BF)

    two_at, two_bt = t_dot(perm_a, normed_two.T).astype(BF), t_dot(perm_b, normed_two.T).astype(BF)
    def down_block(s):
        start = ((at["x"] - sign * s) % 4) * 384
        return t_dot(lax.dynamic_slice_in_dim(activated, start, 384, 1), cot)

    g_gate, g_up, g_down = step.scatter(
        [
            lambda s: dot(two_at[288 * s : 288 * s + 288], d_gate),
            lambda s: dot(two_bt[288 * s : 288 * s + 288], d_up),
            down_block,
        ],
        three,
    )

    d_two_a, d_two_b = dot_t(d_gate, wg).astype(BF), dot_t(d_up, wu).astype(BF)
    part = dot_t(d_two_a, perm_a) + dot_t(d_two_b, perm_b)
    other = swap(part.astype(BF)).astype(F32)
    d_two = part + jnp.concatenate([other[TOK:], other[:TOK]], axis=0)
    g_mlp_gain = jnp.sum((d_two * middle * r2)[:TOK], axis=0)
    e2 = d_two * gains[1]
    d_middle = cot.astype(F32) + r2 * (
        e2 - middle * r2 * r2 * jnp.mean(middle * e2, axis=-1, keepdims=True)
    )
    d_branch = d_middle.astype(BF)

    mixed_ct = t_dot(perm_c, mixed.T).astype(BF)
    d_mixed = dot_t(dot_t(d_branch, w_o).astype(BF), perm_c).astype(BF)
    d_mixed = d_mixed.reshape(2, TOK, 3, 3, HEAD)
    d_probs = jnp.einsum("bqkgd,bskd->bkgqs", d_mixed, values, preferred_element_type=F32)
    d_values = jnp.einsum("bkgqs,bqkgd->bskd", probs, d_mixed, preferred_element_type=F32)
    row_dot = jnp.sum(probs_full * d_probs, axis=-1, keepdims=True)
    d_raw = (probs_full * (d_probs - row_dot) * HEAD ** (-0.5)).astype(BF)
    d_queries = jnp.einsum("bkgqs,bskd->bqkgd", d_raw, keys, preferred_element_type=F32)
    d_keys = jnp.einsum("bkgqs,bqkgd->bskd", d_raw, queries, preferred_element_type=F32)
    d_q = unrotate(d_queries.reshape(2, TOK, 9, HEAD), cos_table, sin_table)
    d_q = d_q.reshape(2 * TOK, 576).astype(BF)
    d_k = unrotate(d_keys, cos_table, sin_table).reshape(2 * TOK, 192).astype(BF)
    d_v = d_values.reshape(2 * TOK, 192).astype(BF)
    d_qa = d_q[:, :512]
    d_qb = jnp.concatenate([d_q[:, 512:], d_k, d_v], axis=1)

    normed_at, normed_bt = t_dot(perm_a, normed.T).astype(BF), t_dot(perm_b, normed.T).astype(BF)
    g_qa, g_qb, g_out = step.scatter(
        [
            lambda s: dot(normed_at[288 * s : 288 * s + 288], d_qa),
            lambda s: dot(normed_bt[288 * s : 288 * s + 288], d_qb),
            lambda s: dot(mixed_ct[144 * s : 144 * s + 144], d_branch),
        ],
        three,
    )

    d_one_a, d_one_b = dot_t(d_qa, wq_a).astype(BF), dot_t(d_qb, w_b).astype(BF)
    part = dot_t(d_one_a, perm_a) + dot_t(d_one_b, perm_b)
    d_normed = part[:TOK] + swap(part[TOK:].astype(BF)).astype(F32)
    x_own, r_own = x[:TOK], r1[:TOK]
    g_attn_gain = jnp.sum(d_normed * x_own * r_own, axis=0)
    e1 = d_normed * gains[0]
    grad_input = d_middle[:TOK] + r_own * (
        e1 - x_own * r_own * r_own * jnp.mean(x_own * e1, axis=-1, keepdims=True)
    )

    g_gains = jnp.stack([g_attn_gain, g_mlp_gain])
    upper = g_gains.astype(BF)
    lower = (g_gains - upper.astype(F32)).astype(BF)
    g_gains = dot(upper, perm_b) + dot(lower, perm_b)
    for axis in reversed(order_b):
        n = g_gains.shape[1] // 4
        g_gains = sum(
            [send(g_gains[:, n * s : n * s + n], SHIFTS[axis][s]) for s in (1, 2, 3)], g_gains[:, :n]
        )

    held_a, held_b = (g_gate, g_qa), (g_up, g_qb)

    def rows_of(held, n):
        return lambda s: jnp.concatenate([h[n * s : n * s + n] for h in held], axis=1).astype(F32)

    def y_block(s):
        y = (at["y"] - sign * s) % 4
        down = lax.dynamic_index_in_dim(g_down.reshape(2, 4, 48, D), y, 1, False).reshape(96, D)
        return jnp.concatenate([g_out[36 * s : 36 * s + 36], down], axis=0).astype(F32)

    s_a, s_b, s_c = step.scatter([rows_of(held_a, 72), rows_of(held_b, 72), y_block], two)

    def z_block(s):
        z = (at["z"] - sign * s) % 4
        down = s_c[36:].reshape(4, 24, D)
        down = lax.dynamic_index_in_dim(down, (z % 2) * 2 + z // 2, 0, False)
        return jnp.concatenate([s_c[9 * s : 9 * s + 9], down], axis=0).astype(F32)

    s_a, s_b, g_od = step.scatter([rows_of((s_a,), 18), rows_of((s_b,), 18), z_block], one, True)

    g_rows = jnp.concatenate([s_a, s_b], axis=1)
    mine = jnp.where(first, g_rows[:9], g_rows[9:])
    theirs = jnp.where(first, g_rows[9:], g_rows[:9]).astype(BF)
    gain_mine = jnp.where(first, g_gains[:, :9], g_gains[:, 9:])
    gain_theirs = jnp.where(first, g_gains[:, 9:], g_gains[:, :9])
    theirs, gain_theirs, g_od = step(
        [theirs, gain_theirs, g_od.astype(BF)], [CORES, CORES, TRADE]
    )
    g_gains = gain_mine + gain_theirs
    g_od, theirs = g_od.astype(F32), theirs.astype(F32)
    low, high = jnp.where(first, mine, theirs), jnp.where(first, theirs, mine)

    def joined(*cuts):
        return jnp.concatenate([h[:, a:b] for h in (low, high) for a, b in cuts], axis=1)

    g_g, g_u = joined((0, 1536)), joined((2048, 3584))
    g_q = joined((1536, 2048), (3584, 3648))
    g_k, g_v = joined((3648, 3840)), joined((3840, 4032))
    return (
        output, grad_input, g_gains[0], g_q, g_k, g_v, g_od[:9], g_gains[1], g_g, g_u, g_od[9:],
    )


def solution(mesh):
    fine = Mesh(mesh.devices.reshape(SHAPE), AXES)
    rows, vector = P(AXES, None), P(AXES)
    return jax.shard_map(
        body,
        mesh=fine,
        in_specs=(rows, rows, vector, rows, rows, rows, rows, vector, rows, rows, rows, rows),
        out_specs=(rows, rows, vector, rows, rows, rows, rows, vector, rows, rows, rows),
        check_vma=False,
    )
```

```python
import functools
import math

import jax
import jax.numpy as jnp
import numpy as np
from jax import lax
from jax.experimental import pallas as pl
from jax.experimental.pallas import tpu as pltpu
from jax.sharding import Mesh
from jax.sharding import PartitionSpec as P

D = 1152
HEADS = 18
KV_HEADS = 6
HEAD = 64
FF = 3072
DP = 1280
TOK = 256
EPS = 1e-05
THETA = 10000.0

SHAPE = (2, 4, 2, 4, 2)
AXES = ("z_hi", "x", "z_lo", "y", "core")
BF = jnp.bfloat16
F32 = jnp.float32


def device_pairs(move):
    pairs = []
    for i in range(128):
        zh, x, zl, y, c = (int(v) for v in np.unravel_index(i, SHAPE))
        x, y, z, c = move(x, y, zh * 2 + zl, c)
        x, y, z = x % 4, y % 4, z % 4
        pairs.append((i, int(np.ravel_multi_index((z // 2, x, z % 2, y, c), SHAPE))))
    return pairs


RINGS = {
    "x": device_pairs(lambda x, y, z, c: (x + 1 - 2 * c, y, z, c)),
    "y": device_pairs(lambda x, y, z, c: (x, y + 1 - 2 * c, z, c)),
    "z": device_pairs(lambda x, y, z, c: (x, y, z + 1 - 2 * c, c)),
}
CORES = device_pairs(lambda x, y, z, c: (x, y, z, 1 - c))
TRADE = device_pairs(lambda x, y, z, c: (x, y, c * 2 + z % 2, z // 2))


def send(value, pairs):
    return lax.ppermute(value, AXES, pairs)


def swap(value):
    return send(value, CORES)


def dot(a, b):
    return jnp.dot(a, b, preferred_element_type=F32)


def dot_t(a, b):
    return lax.dot_general(a, b, (((1,), (1,)), ((), ())), preferred_element_type=F32)


def t_dot(a, b):
    return lax.dot_general(a, b, (((0,), (0,)), ((), ())), preferred_element_type=F32)


def shift(axis, n):
    return device_pairs(lambda x, y, z, c: (
        x + n * (axis == "x"), y + n * (axis == "y"), z + n * (axis == "z"), c))


STRAIGHT = {axis: {n: shift(axis, n) for n in (1, 2, 3)} for axis in ("x", "y", "z")}


def params(mib):
    return pltpu.CompilerParams(vmem_limit_bytes=mib * 2**20)


ANY = pl.BlockSpec(memory_space=pl.ANY)
SMEM = pl.BlockSpec(memory_space=pltpu.SMEM)


def shaped(rows, columns, dtype):
    return jax.ShapeDtypeStruct((rows, columns), dtype)


def cost(flops, arrays):
    return pl.CostEstimate(
        flops=flops,
        bytes_accessed=sum(math.prod(a.shape) * a.dtype.itemsize for a in arrays),
        transcendentals=0,
    )


def low_lanes(shape):
    return lax.broadcasted_iota(jnp.int32, shape, 1) % 128 < 64


def turn(v, cos, sin):
    ahead = lax.broadcasted_iota(jnp.int32, v.shape, 1) % 64 < 32
    return v * cos + jnp.where(ahead, pltpu.roll(v, 96, 1), pltpu.roll(v, 32, 1)) * sin


def stack_kernel(*refs):
    *blocks, out = refs
    blocks = [b[...].astype(F32) for b in blocks]
    spare = out.shape[0] - sum(b.shape[0] for b in blocks)
    if spare:
        blocks.append(jnp.zeros((spare, out.shape[1]), F32))
    out[...] = jnp.concatenate(blocks, axis=0).astype(out.dtype)


def stack_rows(blocks, rows=72):
    return pl.pallas_call(
        stack_kernel,
        out_shape=shaped(rows, blocks[0].shape[1], blocks[0].dtype),
        compiler_params=params(8),
    )(*blocks)


def attention_kernel(
    tok_own, tok_other, w, perm, left, right, cos, sin, bias,
    normed_p, turned, k_lo, k_hi, v_lo, v_hi, probs, mixed, w_o, gains, part, part_low,
    gathered, pre,
):
    gathered[...] = dot(perm[...], w[:, 896:1024]).T
    gains[...] = gathered[64:72, :]
    for b, tok in enumerate((tok_own, tok_other)):
        rows = slice(b * TOK, b * TOK + TOK)
        x = tok[...].astype(F32)
        r1 = lax.rsqrt(jnp.mean(x * x, axis=1, keepdims=True) + EPS)
        normed = (x * r1 * gains[0:1, :]).astype(BF)
        normed_p[rows, :] = dot(normed, perm[...]).astype(BF)
    w_o[:, :640] = dot(left[...], w[:, 1024:1664]).astype(BF)
    w_o[:, 640:] = dot(right[...], w[:, 1024:1536]).astype(BF)

    def one_row(b, carry):
        rows = pl.ds(pl.multiple_of(b * TOK, TOK), TOK)
        pre[...] = dot(normed_p[rows, :], w[:, :1024])
        for j in range(6):
            lanes = slice(128 * j, 128 * j + 128)
            turned[rows, lanes] = turn(pre[:, lanes], cos[rows, :], sin[rows, :]).astype(BF)
        low = low_lanes((TOK, 128))
        zero = jnp.zeros((TOK, 128), F32)

        def both(value, half, to_low, to_high, kv):
            value = jnp.where(low if half == 0 else ~low, value, zero)
            moved = pltpu.roll(value, 64, 1)
            pair = (value, moved) if half == 0 else (moved, value)
            lanes = slice(128 * kv, 128 * kv + 128)
            to_low[rows, lanes], to_high[rows, lanes] = pair[0].astype(BF), pair[1].astype(BF)

        for kv, (j, half) in enumerate(((4, 1), (5, 0), (5, 1))):
            lanes = slice(128 * j, 128 * j + 128)
            both(turned[rows, lanes].astype(F32), half, k_lo, k_hi, kv)
        for kv, (j, half) in enumerate(((6, 0), (6, 1), (7, 0))):
            both(pre[:, 128 * j : 128 * j + 128], half, v_lo, v_hi, kv)
        for j in range(5):
            lanes = slice(128 * j, 128 * j + 128)
            total = None
            for h in (2 * j, 2 * j + 1):
                if h == 9:
                    continue
                kv = slice(128 * (h // 3), 128 * (h // 3) + 128)
                k_ref, v_ref = (k_lo, v_lo) if h % 2 == 0 else (k_hi, v_hi)
                s = dot_t(turned[rows, lanes], k_ref[rows, kv]) * HEAD ** (-0.5) + bias[rows, :]
                e = jnp.exp(s - jnp.max(s, axis=1, keepdims=True))
                p = (e * (1.0 / jnp.sum(e, axis=1, keepdims=True))).astype(BF)
                probs[h, rows, :] = p
                got = dot(p, v_ref[rows, kv])
                total = got if total is None else total + got
            mixed[rows, lanes] = total.astype(BF)
        for n in range(3):
            lanes = slice(384 * n, 384 * n + 384)
            got = dot(mixed[rows, :], w_o[:, lanes])
            part[rows, lanes] = got
            part_low[rows, lanes] = got.astype(BF)
        return carry

    lax.fori_loop(0, 2, one_row, 0)


def attention_forward(*args):
    outs = [
        shaped(512, DP, BF), shaped(512, 768, BF), *[shaped(512, 384, BF)] * 4,
        jax.ShapeDtypeStruct((9, 512, 256), BF), shaped(512, 640, BF), shaped(640, D, BF),
        shaped(8, D, F32), shaped(512, D, F32), shaped(512, D, BF),
    ]
    return pl.pallas_call(
        attention_kernel,
        out_shape=outs,
        scratch_shapes=[pltpu.VMEM((128, D), F32), pltpu.VMEM((TOK, 1024), F32)],
        compiler_params=params(40),
        cost_estimate=cost(6 * 10**9, [*args, *outs]),
    )(*args)


def feed_kernel(
    at, tok_own, tok_other, part, other, cot_own, cot_other, gains, perm_a, perm_b, *refs
):
    gate_blocks, up_blocks, down_blocks = refs[:4], refs[4:8], refs[8:12]
    (
        middle, act, d_gate, d_up, two_at, two_bt, out_own, out_send, d_two, d_two_low, mlp_row,
        wg, wu, wd, cot, n2, n2_a, n2_b, d_a, d_b, sems,
    ) = refs[12:]
    copies = []
    for s in range(4):
        row = lax.rem(at[0] - at[1] * s + 4, 4) * 384
        copies.append([
            pltpu.make_async_copy(gate_blocks[s], wg.at[pl.ds(288 * s, 288), :], sems.at[0, s]),
            pltpu.make_async_copy(up_blocks[s], wu.at[pl.ds(288 * s, 288), :], sems.at[1, s]),
            pltpu.make_async_copy(
                down_blocks[s], wd.at[pl.ds(pl.multiple_of(row, 384), 384), :], sems.at[2, s]
            ),
        ])
    for group in copies:
        for c in group:
            c.start()
    for b, (tok, c) in enumerate(((tok_own, cot_own), (tok_other, cot_other))):
        rows, swapped = slice(b * TOK, b * TOK + TOK), slice((1 - b) * TOK, (2 - b) * TOK)
        value = tok[...].astype(F32) + part[rows, :] + other[swapped, :].astype(F32)
        middle[rows, :] = value
        r2 = lax.rsqrt(jnp.mean(value * value, axis=1, keepdims=True) + EPS)
        n2[rows, :] = (value * r2 * gains[1:2, :]).astype(BF)
        cot[rows, :] = c[...]
    for n in range(3):
        lanes = slice(384 * n, 384 * n + 384)
        n2_a[:, lanes] = dot(n2[...], perm_a[:, lanes]).astype(BF)
        n2_b[:, lanes] = dot(n2[...], perm_b[:, lanes]).astype(BF)
    for group in copies:
        for c in group:
            c.wait()

    def columns(i, carry):
        lanes = pl.ds(pl.multiple_of(i * 256, 256), 256)
        gate, up = dot(n2_a[...], wg[:, lanes]), dot(n2_b[...], wu[:, lanes])
        d_act = dot_t(cot[...], wd[lanes, :])
        sig = 1.0 / (1.0 + jnp.exp(-gate))
        swish = gate * sig
        act[:, lanes] = (swish * up).astype(BF)
        d_up[:, lanes] = (d_act * swish).astype(BF)
        d_gate[:, lanes] = (d_act * up * sig * (1.0 + gate * (1.0 - sig))).astype(BF)
        return carry

    lax.fori_loop(0, 6, columns, 0)
    two_at[...] = n2_a[...].T
    two_bt[...] = n2_b[...].T

    def back(i, carry):
        lanes = pl.ds(pl.multiple_of(i * 384, 384), 384)
        got = dot(act[...], wd[:, lanes])
        out_own[:, lanes] = middle[:TOK, lanes] + got[:TOK]
        out_send[:, lanes] = got[TOK:].astype(BF)
        d_a[:, lanes] = dot_t(d_gate[...], wg[lanes, :]).astype(BF)
        d_b[:, lanes] = dot_t(d_up[...], wu[lanes, :]).astype(BF)
        return carry

    lax.fori_loop(0, 3, back, 0)

    def unmix(i, carry):
        lanes = pl.ds(pl.multiple_of(i * 384, 384), 384)
        got = dot_t(d_a[...], perm_a[lanes, :]) + dot_t(d_b[...], perm_b[lanes, :])
        d_two[:, lanes] = got
        d_two_low[:, lanes] = got.astype(BF)
        return carry

    lax.fori_loop(0, 3, unmix, 0)
    total = jnp.zeros((1, D), F32)
    for b in range(2):
        rows = slice(b * TOK, b * TOK + TOK)
        value = middle[rows, :]
        r2 = lax.rsqrt(jnp.mean(value * value, axis=1, keepdims=True) + EPS)
        total = total + jnp.sum(d_two[rows, :] * value * r2, axis=0, keepdims=True)
    mlp_row[...] = jnp.broadcast_to(total, (8, D))


def feed_forward_and_back(*args):
    outs = [
        shaped(512, D, F32), *[shaped(512, 1536, BF)] * 3, *[shaped(D, 512, BF)] * 2,
        shaped(TOK, D, F32), shaped(TOK, D, BF), shaped(512, D, F32), shaped(512, D, BF),
        shaped(8, D, F32),
    ]
    return pl.pallas_call(
        feed_kernel,
        out_shape=outs,
        in_specs=[SMEM] + [pl.BlockSpec(memory_space=pltpu.VMEM)] * 9 + [ANY] * 12,
        scratch_shapes=[
            pltpu.VMEM((D, 1536), BF), pltpu.VMEM((D, 1536), BF), pltpu.VMEM((1536, D), BF),
            *[pltpu.VMEM((512, D), BF)] * 6, pltpu.SemaphoreType.DMA((3, 4)),
        ],
        compiler_params=params(58),
        cost_estimate=cost(16 * 10**9, [*args, *outs]),
    )(*args)


def grads_kernel(s, at, two_at, two_bt, d_gate, d_up, act, cot_own, cot_other, *outs):
    rows = slice(288 * s, 288 * s + 288)
    outs[0][...] = dot(two_at[rows, :], d_gate[...]).astype(BF)
    outs[1][...] = dot(two_bt[rows, :], d_up[...]).astype(BF)
    start = pl.multiple_of(lax.rem(at[0] - at[1] * s + 4, 4) * 384, 384)
    lanes = pl.ds(start, 384)
    got = t_dot(act[:TOK, lanes], cot_own[...]) + t_dot(act[TOK:, lanes], cot_other[...])
    outs[2][...] = got.astype(BF)


def feed_grads(s, *args):
    outs = [shaped(288, 1536, BF), shaped(288, 1536, BF), shaped(384, D, BF)]
    return pl.pallas_call(
        functools.partial(grads_kernel, s),
        out_shape=outs,
        in_specs=[SMEM] + [pl.BlockSpec(memory_space=pltpu.VMEM)] * (len(args) - 1),
        compiler_params=params(22),
        cost_estimate=cost(14 * 10**8, [*args, *outs]),
    )(*args)


def added(parts, arrived):
    return [(p.astype(F32) + a.astype(F32)).astype(BF) for p, a in zip(parts, arrived)]


def attention_back_kernel(
    tok_own, tok_other, cot_own, cot_other, middle, d_two, other, gains, mlp_row, w, perm,
    left_t, right_t, cos, sin, normed_p, turned, k_lo, k_hi, v_lo, v_hi, probs, mixed, w_o,
    grads, d_middle, part_own, part_send,
    d_branch, d_mixed, d_pre, d_qkv, d_p, g_out, rows_of_gains,
):
    toks = (tok_own, tok_other)
    for b, c in enumerate((cot_own, cot_other)):
        rows, swapped = slice(b * TOK, b * TOK + TOK), slice((1 - b) * TOK, (2 - b) * TOK)
        value = middle[rows, :]
        r2 = lax.rsqrt(jnp.mean(value * value, axis=1, keepdims=True) + EPS)
        e2 = gains[1:2, :] * (d_two[rows, :] + other[swapped, :].astype(F32))
        got = c[...].astype(F32) + r2 * (
            e2 - value * (r2 * r2 * jnp.mean(value * e2, axis=1, keepdims=True))
        )
        if b == 0:
            d_middle[...] = got
        d_branch[rows, :] = got.astype(BF)
    d_mixed[...] = dot_t(d_branch[...], w_o[...]).astype(BF)

    def one_row(b, carry):
        rows = pl.ds(pl.multiple_of(b * TOK, TOK), TOK)
        d_k = {}
        d_v = {}
        for j in range(5):
            lanes = slice(128 * j, 128 * j + 128)
            q_pair, d_pair = turned[rows, lanes], d_mixed[rows, lanes]
            total = None
            for h in (2 * j, 2 * j + 1):
                if h == 9:
                    continue
                kv, half = h // 3, h % 2
                at_kv = slice(128 * kv, 128 * kv + 128)
                k_ref, v_ref = (k_lo, v_lo) if half == 0 else (k_hi, v_hi)
                p = probs[h, rows, :]
                p32 = p.astype(F32)
                d_probs = dot_t(d_pair, v_ref[rows, at_kv])
                row_dot = jnp.sum(p32 * d_probs, axis=1, keepdims=True)
                d_raw = (p32 * (d_probs - row_dot) * HEAD ** (-0.5)).astype(BF)
                got = dot(d_raw, k_ref[rows, at_kv])
                total = got if total is None else total + got
                for sums, value in ((d_k, t_dot(d_raw, q_pair)), (d_v, t_dot(p, d_pair))):
                    sums[kv, half] = value if (kv, half) not in sums else sums[kv, half] + value
            d_pre[:, lanes] = total
        low = low_lanes((TOK, 128))

        def collected(sums, kv, half):
            return sums[kv, half] + pltpu.roll(sums[kv, 1 - half], 64, 1)

        d_pre[:, 512:640] = jnp.where(low, d_pre[:, 512:640], collected(d_k, 0, 1))
        d_pre[:, 640:768] = jnp.where(low, collected(d_k, 1, 0), collected(d_k, 2, 1))
        for j in range(6):
            lanes = slice(128 * j, 128 * j + 128)
            d_qkv[rows, lanes] = turn(d_pre[:, lanes], cos[rows, :], -sin[rows, :]).astype(BF)
        d_qkv[rows, 768:896] = jnp.where(low, collected(d_v, 0, 0), collected(d_v, 1, 1)).astype(BF)
        d_qkv[rows, 896:1024] = jnp.where(low, collected(d_v, 2, 0), 0.0).astype(BF)
        return carry

    lax.fori_loop(0, 2, one_row, 0)

    total = jnp.zeros((1, D), F32)
    for b, tok in enumerate(toks):
        rows = slice(b * TOK, b * TOK + TOK)
        d_p[...] = dot_t(d_qkv[rows, :], w[:, :1024]).astype(BF)
        x = tok[...].astype(F32)
        r1 = lax.rsqrt(jnp.mean(x * x, axis=1, keepdims=True) + EPS)
        got = dot_t(d_p[...], perm[...])
        total = total + jnp.sum(got * x * r1, axis=0, keepdims=True)
        if b == 0:
            part_own[...] = got
        else:
            part_send[...] = got.astype(BF)
    which = lax.broadcasted_iota(jnp.int32, (128, D), 0)
    rows_of_gains[...] = jnp.where(
        which == 64, total, jnp.where(which == 65, mlp_row[0:1, :], 0.0)
    ).astype(BF)
    gain_columns = dot(rows_of_gains[...], perm[...]).T

    def qkv_grads(i, carry):
        lanes = pl.ds(pl.multiple_of(i * 256, 256), 256)
        grads[:, lanes] = t_dot(normed_p[...], d_qkv[:, lanes]).astype(BF)
        return carry

    lax.fori_loop(0, 4, qkv_grads, 0)
    grads[:, 896:1024] = (grads[:, 896:1024].astype(F32) + gain_columns).astype(BF)
    g_out[...] = t_dot(mixed[...], d_branch[...]).astype(BF)
    grads[:, 1024:1536] = (
        dot(left_t[...], g_out[:, :512]) + dot(right_t[...], g_out[:, 640:])
    ).astype(BF)
    grads[:, 1536:] = dot(left_t[...], g_out[:, 512:640]).astype(BF)


def attention_backward(*args):
    outs = [shaped(DP, 1664, BF), shaped(TOK, D, F32), shaped(TOK, D, F32), shaped(TOK, D, BF)]
    return pl.pallas_call(
        attention_back_kernel,
        out_shape=outs,
        scratch_shapes=[
            pltpu.VMEM((512, D), BF), pltpu.VMEM((512, 640), BF), pltpu.VMEM((TOK, 768), F32),
            pltpu.VMEM((512, 1024), BF), pltpu.VMEM((TOK, DP), BF), pltpu.VMEM((640, D), BF),
            pltpu.VMEM((128, D), BF),
        ],
        compiler_params=params(48),
        cost_estimate=cost(9 * 10**9, [*args, *outs]),
    )(*args)


class Lockstep:
    def __init__(self):
        self.last = ()

    def after(self, *values):
        self.last = (*self.last, *values)

    def __call__(self, values, pairs, late=(), late_pairs=()):
        tied = lax.optimization_barrier((*values, *self.last))
        sent = [send(v, p) for v, p in zip(tied, pairs)]
        sent += [send(v, p) for v, p in zip(late, late_pairs)]
        self.last = lax.optimization_barrier(tuple(sent))
        return list(self.last)

    def gather(self, blocks, axes, more=(), more_pairs=()):
        values = [b for b in blocks for _ in range(3)]
        pairs = [STRAIGHT[a][n] for a in axes for n in (1, 2, 3)]
        got = self([*values, *more], [*pairs, *more_pairs])
        rings = [[b, *got[3 * i : 3 * i + 3]] for i, b in enumerate(blocks)]
        return rings, got[3 * len(blocks) :]

    def scatter(self, makers, axes, more=(), more_pairs=()):
        values = [make(s).astype(BF) for make in makers for s in (1, 2, 3)]
        pairs = [STRAIGHT[a][4 - s] for a in axes for s in (1, 2, 3)]
        got = self([*values, *more], [*pairs, *more_pairs])
        sums = [
            sum([g.astype(F32) for g in got[3 * i : 3 * i + 3]], make(0).astype(F32))
            for i, make in enumerate(makers)
        ]
        return sums, got[3 * len(makers) :]


def place(blocks, at, sign):
    out = jnp.zeros((4, *blocks[0].shape), blocks[0].dtype)
    for step, block in enumerate(blocks):
        out = lax.dynamic_update_index_in_dim(out, block, (at - sign * step) % 4, 0)
    return out


def row_tables(segment_row):
    places = jnp.arange(TOK, dtype=jnp.int32)
    same_doc = segment_row[:, None] == segment_row[None, :]
    starts = jnp.min(jnp.where(same_doc, places[None, :], TOK), axis=1)
    offsets = (places - starts).astype(F32)
    lane = jnp.arange(128, dtype=jnp.int32)
    frequency = jnp.exp((lane % 32).astype(F32) * (-2.0 * math.log(THETA) / HEAD))
    angles = offsets[:, None] * frequency[None, :]
    side = jnp.where(lane % 64 < 32, -1.0, 1.0)
    allowed = same_doc & (places[:, None] >= places[None, :])
    return jnp.cos(angles), jnp.sin(angles) * side, jnp.where(allowed, 0.0, -1e30).astype(F32)


def body(
    tokens, segments, attn_gain, w_query, w_key, w_value, w_out, mlp_gain, w_gate, w_up, w_down,
    cotangent,
):
    core = lax.axis_index("core")
    at = {
        "x": lax.axis_index("x"),
        "y": lax.axis_index("y"),
        "z": lax.axis_index("z_hi") * 2 + lax.axis_index("z_lo"),
    }
    sign = 1 - 2 * core
    first = core == 0

    def halves(w):
        n = w.shape[1] // 2
        low, high = w[:, :n], w[:, n:]
        return jnp.where(first, low, high), jnp.where(first, high, low)

    pairs = [halves(w) for w in (w_gate, w_query, w_up, w_key, w_value)]
    gain_pair = jnp.stack([attn_gain, mlp_gain], axis=1)

    def columns(parts):
        gate, query, up, key, value = parts
        return jnp.concatenate([gate, up, query, key, value, gain_pair], axis=1)

    kept, given = columns([p[0] for p in pairs]), columns([p[1] for p in pairs])
    step = Lockstep()
    given, traded = step(
        [given, jnp.concatenate([w_out, w_down], axis=0)], [CORES, TRADE]
    )
    rows = jnp.concatenate([jnp.where(first, kept, given), jnp.where(first, given, kept)], axis=0)


    order_a, order_b, order_c = ("x", "z", "y"), ("y", "x", "z"), ("z", "y", "x")

    def natural(order):
        k = jnp.arange(D, dtype=jnp.int32)
        r, t = k % 18, k // 18
        c = {}
        for level, axis in enumerate(order):
            c[axis] = (at[axis] - (sign if level == 2 else 1) * ((t // 4**level) % 4)) % 4
        chip = (((c["z"] // 2) * 4 + c["x"]) * 2 + c["z"] % 2) * 4 + c["y"]
        return chip * 18 + r

    one, two, three = zip(order_a, order_b, order_c)
    out_rows = traded[:9]
    attn_rows = jnp.concatenate(
        [rows[:, 3072:], jnp.zeros((18, 62), BF),
         jnp.concatenate([out_rows[:, :640], jnp.pad(out_rows[:, 640:], ((0, 0), (0, 128)))], axis=0)],
        axis=1,
    )
    (ha, hb, hc), got = step.gather(
        [rows[:, :1536], rows[:, 1536:3072], traded[9:]], one,
        [attn_rows] * 3, [STRAIGHT["z"][n] for n in (1, 2, 3)],
    )
    w_attn = stack_rows([attn_rows, *got], 80)
    w_attn = lax.all_gather(w_attn, ("x", "y"), axis=0, tiled=True)
    down = place(hc, at["z"], 1).reshape(2, 2, 24, D)
    down = jnp.transpose(down, (1, 0, 2, 3)).reshape(96, D)
    (ha, hb, hc), (tok_other, cot_other, seg_other) = step.gather(
        [stack_rows(ha), stack_rows(hb), down], two,
        [tokens, cotangent, segments.astype(F32)], [CORES] * 3,
    )
    seg_other = seg_other.astype(jnp.int32)
    tables = [row_tables(segments[0]), row_tables(seg_other[0])]
    cos, sin, bias = (jnp.concatenate(t, axis=0) for t in zip(*tables))

    rows_a, rows_b = natural(order_a), natural(order_b)

    k = jnp.arange(DP, dtype=jnp.int32)
    x_at, y_at, r, s = k // 320, (k // 80) % 4, (k % 80) % 18, (k % 80) // 18
    z = (at["z"] - s) % 4
    source = (((z // 2 * 4 + x_at) * 2 + z % 2) * 4 + y_at) * 18 + r
    source = jnp.where(s < 4, source, -1)
    e = ((x_at * 2 + z % 2) * 4 + y_at) * 2 + z // 2
    e_at = jnp.arange(640, dtype=jnp.int32)
    to_left = jnp.where((r < 9) & (s < 4), e * 9 + r, -1)
    to_right = jnp.where((r >= 9) & (s < 4), e * 9 + r - 9, -1)
    rows_a, rows_b, source, to_left, to_right, *_ = lax.optimization_barrier(
        (rows_a, rows_b, source, to_left, to_right, *step.last)
    )
    d_at = jnp.arange(D, dtype=jnp.int32)[:, None]
    perm_a, perm_b, perm = ((d_at == i[None, :]).astype(BF) for i in (rows_a, rows_b, source))
    left, left_t = ((e_at[:, None] == to_left[None, :]).astype(BF), (to_left[:, None] == e_at[None, :]).astype(BF))
    right, right_t = ((e_at[:, None] == to_right[None, :]).astype(BF), (to_right[:, None] == e_at[None, :]).astype(BF))

    ring = [RINGS[a] for a in three]
    down = place([h.reshape(2, 48, D) for h in hc], at["y"], 1)
    down = jnp.transpose(down, (1, 0, 2, 3)).reshape(384, D)
    held = [[jnp.concatenate(ha, axis=0), jnp.concatenate(hb, axis=0), down]]
    held.append(step(held[-1], ring))
    (
        normed_p, turned, k_lo, k_hi, v_lo, v_hi, probs, mixed, w_o, gains, part, part_low,
    ) = attention_forward(tokens, tok_other, w_attn, perm, left, right, cos, sin, bias)
    *arrived, part_other = step(held[-1], ring, [part_low], [CORES])
    held.append(arrived)
    held.append(step(held[-1], ring))
    ha, hb, hc = zip(*held)

    where = jnp.stack([at["x"], sign]).astype(jnp.int32)
    (
        middle, act, d_gate, d_up, two_at, two_bt, out_own, out_send, d_two, d_two_low, mlp_row,
    ) = feed_forward_and_back(
        where, tokens, tok_other, part, part_other, cotangent, cot_other, gains, perm_a, perm_b,
        *ha, *hb, *hc,
    )
    arrays = (where, two_at, two_bt, d_gate, d_up, act, cotangent, cot_other)
    parts = feed_grads(1, *arrays)

    g_attn, d_middle, part_own, part_send = attention_backward(
        tokens, tok_other, cotangent, cot_other, middle, d_two, swap(d_two_low), gains, mlp_row,
        w_attn, perm, left_t, right_t, cos, sin, normed_p, turned, k_lo, k_hi, v_lo, v_hi, probs,
        mixed, w_o,
    )
    *arrived, part_other = step(parts, ring, [part_send], [CORES])
    arrived = step(added(feed_grads(2, *arrays), arrived), ring)
    arrived = step(added(feed_grads(3, *arrays), arrived), ring)
    g_gate, g_up, g_down = added(feed_grads(0, *arrays), arrived)
    g_attn = lax.psum_scatter(g_attn, "x", scatter_dimension=0, tiled=True)
    g_attn_x = g_attn
    g_attn = lax.psum_scatter(g_attn, "y", scatter_dimension=0, tiled=True)

    output = (out_own + swap(out_send).astype(F32)).astype(BF)
    d_normed = part_own + part_other.astype(F32)
    x_own = tokens.astype(F32)
    r_own = lax.rsqrt(jnp.mean(x_own * x_own, axis=-1, keepdims=True) + EPS)
    e1 = d_normed * gains[0]
    grad_input = d_middle + r_own * (
        e1 - x_own * r_own * r_own * jnp.mean(x_own * e1, axis=-1, keepdims=True)
    )

    def rows_of(held, n):
        return lambda s: held[n * s : n * s + n]

    def y_block(s):
        down = g_down.reshape(2, 4, 48, D)
        return lax.dynamic_index_in_dim(down, (at["y"] - s) % 4, 1, False).reshape(96, D)

    (g_gate, g_up, g_down), _ = step.scatter([rows_of(g_gate, 72), rows_of(g_up, 72), y_block], two)

    def z_block(s):
        z = (at["z"] - s) % 4
        down = g_down.reshape(4, 24, D)
        return lax.dynamic_index_in_dim(down, (z % 2) * 2 + z // 2, 0, False)

    step.after(g_attn_x)
    (g_gate, g_up, g_down), _ = step.scatter([rows_of(g_gate, 18), rows_of(g_up, 18), z_block], one)
    got = step([g_attn[18 * s : 18 * s + 18] for s in (1, 2, 3)], [STRAIGHT["z"][4 - s] for s in (1, 2, 3)])
    g_attn = sum([g.astype(F32) for g in got], g_attn[:18].astype(F32))

    g_out = jnp.concatenate([g_attn[:9, 1024:], g_attn[9:, 1024:1536]], axis=1)
    g_rows = jnp.concatenate([g_gate, g_up, g_attn[:, :962]], axis=1)
    mine = jnp.where(first, g_rows[:9], g_rows[9:])
    theirs = jnp.where(first, g_rows[9:], g_rows[:9]).astype(BF)
    theirs, g_od = step(
        [theirs, jnp.concatenate([g_out, g_down], axis=0).astype(BF)], [CORES, TRADE]
    )
    g_od, theirs = g_od.astype(F32), theirs.astype(F32)
    low, high = jnp.where(first, mine, theirs), jnp.where(first, theirs, mine)
    g_gains = (low[:, 4032:] + high[:, 4032:]).T

    def joined(*cuts):
        return jnp.concatenate([h[:, a:b] for h in (low, high) for a, b in cuts], axis=1)

    g_g, g_u = joined((0, 1536)), joined((1536, 3072))
    g_q, g_k, g_v = joined((3072, 3648)), joined((3648, 3840)), joined((3840, 4032))
    return (
        output, grad_input, g_gains[0], g_q, g_k, g_v, g_od[:9], g_gains[1], g_g, g_u, g_od[9:],
    )


def solution(mesh):
    fine = Mesh(mesh.devices.reshape(SHAPE), AXES)
    rows, vector = P(AXES, None), P(AXES)
    return jax.shard_map(
        body,
        mesh=fine,
        in_specs=(rows, rows, vector, rows, rows, rows, rows, vector, rows, rows, rows, rows),
        out_specs=(rows, rows, vector, rows, rows, rows, rows, vector, rows, rows, rows),
        check_vma=False,
    )
```

```python
import functools
import math

import jax
import jax.numpy as jnp
import numpy as np
from jax import lax
from jax.experimental import pallas as pl
from jax.experimental.pallas import tpu as pltpu
from jax.sharding import Mesh
from jax.sharding import PartitionSpec as P

D = 1152
HEADS = 18
KV_HEADS = 6
HEAD = 64
FF = 3072
DP = 1280
TOK = 256
EPS = 1e-05
THETA = 10000.0

SHAPE = (2, 4, 2, 4, 2)
AXES = ("z_hi", "x", "z_lo", "y", "core")
BF = jnp.bfloat16
F32 = jnp.float32


def device_pairs(move):
    pairs = []
    for i in range(128):
        zh, x, zl, y, c = (int(v) for v in np.unravel_index(i, SHAPE))
        x, y, z, c = move(x, y, zh * 2 + zl, c)
        x, y, z = x % 4, y % 4, z % 4
        pairs.append((i, int(np.ravel_multi_index((z // 2, x, z % 2, y, c), SHAPE))))
    return pairs


RINGS = {
    "x": device_pairs(lambda x, y, z, c: (x + 1 - 2 * c, y, z, c)),
    "y": device_pairs(lambda x, y, z, c: (x, y + 1 - 2 * c, z, c)),
    "z": device_pairs(lambda x, y, z, c: (x, y, z + 1 - 2 * c, c)),
}
CORES = device_pairs(lambda x, y, z, c: (x, y, z, 1 - c))
TRADE = device_pairs(lambda x, y, z, c: (x, y, c * 2 + z % 2, z // 2))


def lines(*axes):
    index = np.arange(128).reshape(SHAPE)
    groups = []
    for core, axis in enumerate(axes):
        along = np.moveaxis(index[..., core], AXES.index(axis), -1)
        groups += along.reshape(-1, 4).tolist()
    return groups


LINES = {("x", "y"): lines("x", "y"), ("y", "x"): lines("y", "x")}


def send(value, pairs):
    return lax.ppermute(value, AXES, pairs)


def swap(value):
    return send(value, CORES)


def dot(a, b):
    return jnp.dot(a, b, preferred_element_type=F32)


def dot_t(a, b):
    return lax.dot_general(a, b, (((1,), (1,)), ((), ())), preferred_element_type=F32)


def t_dot(a, b):
    return lax.dot_general(a, b, (((0,), (0,)), ((), ())), preferred_element_type=F32)


def shift(axis, n):
    return device_pairs(lambda x, y, z, c: (
        x + n * (axis == "x"), y + n * (axis == "y"), z + n * (axis == "z"), c))


def signed(axis, n):
    return device_pairs(lambda x, y, z, c: (
        x + n * (1 - 2 * c) * (axis == "x"), y + n * (1 - 2 * c) * (axis == "y"),
        z + n * (1 - 2 * c) * (axis == "z"), c))


SIGNED = {axis: {n: signed(axis, n) for n in (1, 2, 3)} for axis in ("x", "y", "z")}
STRAIGHT = {axis: {n: shift(axis, n) for n in (1, 2, 3)} for axis in ("x", "y", "z")}


def params(mib):
    return pltpu.CompilerParams(vmem_limit_bytes=mib * 2**20)


ANY = pl.BlockSpec(memory_space=pl.ANY)
SMEM = pl.BlockSpec(memory_space=pltpu.SMEM)


def shaped(rows, columns, dtype):
    return jax.ShapeDtypeStruct((rows, columns), dtype)


def cost(flops, arrays):
    return pl.CostEstimate(
        flops=flops,
        bytes_accessed=sum(math.prod(a.shape) * a.dtype.itemsize for a in arrays),
        transcendentals=0,
    )


def low_lanes(shape):
    return lax.broadcasted_iota(jnp.int32, shape, 1) % 128 < 64


def turn(v, cos, sin):
    ahead = lax.broadcasted_iota(jnp.int32, v.shape, 1) % 64 < 32
    return v * cos + jnp.where(ahead, pltpu.roll(v, 96, 1), pltpu.roll(v, 32, 1)) * sin


def stack_kernel(*refs):
    *blocks, out = refs
    blocks = [b[...].astype(F32) for b in blocks]
    spare = out.shape[0] - sum(b.shape[0] for b in blocks)
    if spare:
        blocks.append(jnp.zeros((spare, out.shape[1]), F32))
    out[...] = jnp.concatenate(blocks, axis=0).astype(out.dtype)


def stack_rows(blocks, rows=72):
    return pl.pallas_call(
        stack_kernel,
        out_shape=shaped(rows, blocks[0].shape[1], blocks[0].dtype),
        compiler_params=params(8),
    )(*blocks)


def heads_kernel(
    tok_own, tok_other, w, perm, left, right, cos, sin,
    normed_p, turned, k_lo, k_hi, v_lo, v_hi, w_o, gains, gathered, pre,
):
    gathered[...] = dot(perm[...], w[:, 896:1024]).T
    gains[...] = gathered[64:72, :]
    for b, tok in enumerate((tok_own, tok_other)):
        rows = slice(b * TOK, b * TOK + TOK)
        x = tok[...].astype(F32)
        r1 = lax.rsqrt(jnp.mean(x * x, axis=1, keepdims=True) + EPS)
        normed = (x * r1 * gains[0:1, :]).astype(BF)
        normed_p[rows, :] = dot(normed, perm[...]).astype(BF)
    w_o[:, :640] = dot(left[...], w[:, 1024:1664]).astype(BF)
    w_o[:, 640:] = dot(right[...], w[:, 1024:1536]).astype(BF)

    def one_row(b, carry):
        rows = pl.ds(pl.multiple_of(b * TOK, TOK), TOK)
        pre[...] = dot(normed_p[rows, :], w[:, :1024])
        for j in range(6):
            lanes = slice(128 * j, 128 * j + 128)
            turned[rows, lanes] = turn(pre[:, lanes], cos[rows, :], sin[rows, :]).astype(BF)
        low = low_lanes((TOK, 128))
        zero = jnp.zeros((TOK, 128), F32)

        def both(value, half, to_low, to_high, kv):
            value = jnp.where(low if half == 0 else ~low, value, zero)
            moved = pltpu.roll(value, 64, 1)
            pair = (value, moved) if half == 0 else (moved, value)
            lanes = slice(128 * kv, 128 * kv + 128)
            to_low[rows, lanes], to_high[rows, lanes] = pair[0].astype(BF), pair[1].astype(BF)

        for kv, (j, half) in enumerate(((4, 1), (5, 0), (5, 1))):
            lanes = slice(128 * j, 128 * j + 128)
            both(turned[rows, lanes].astype(F32), half, k_lo, k_hi, kv)
        for kv, (j, half) in enumerate(((6, 0), (6, 1), (7, 0))):
            both(pre[:, 128 * j : 128 * j + 128], half, v_lo, v_hi, kv)
        return carry

    lax.fori_loop(0, 2, one_row, 0)


def attention_heads(*args):
    outs = [
        shaped(512, DP, BF), shaped(512, 768, BF), *[shaped(512, 384, BF)] * 4, shaped(640, D, BF),
        shaped(8, D, F32),
    ]
    return pl.pallas_call(
        heads_kernel,
        out_shape=outs,
        scratch_shapes=[pltpu.VMEM((128, D), F32), pltpu.VMEM((TOK, 1024), F32)],
        compiler_params=params(32),
        cost_estimate=cost(5 * 10**9, [*args, *outs]),
    )(*args)


def attention_kernel(
    turned, k_lo, k_hi, v_lo, v_hi, w_o, bias, probs, mixed, part, part_low
):
    def one_row(b, carry):
        rows = pl.ds(pl.multiple_of(b * TOK, TOK), TOK)
        for j in range(5):
            lanes = slice(128 * j, 128 * j + 128)
            total = None
            for h in (2 * j, 2 * j + 1):
                if h == 9:
                    continue
                kv = slice(128 * (h // 3), 128 * (h // 3) + 128)
                k_ref, v_ref = (k_lo, v_lo) if h % 2 == 0 else (k_hi, v_hi)
                s = dot_t(turned[rows, lanes], k_ref[rows, kv]) * HEAD ** (-0.5) + bias[rows, :]
                e = jnp.exp(s - jnp.max(s, axis=1, keepdims=True))
                p = (e * (1.0 / jnp.sum(e, axis=1, keepdims=True))).astype(BF)
                probs[h, rows, :] = p
                got = dot(p, v_ref[rows, kv])
                total = got if total is None else total + got
            mixed[rows, lanes] = total.astype(BF)
        for n in range(3):
            lanes = slice(384 * n, 384 * n + 384)
            got = dot(mixed[rows, :], w_o[:, lanes])
            part[rows, lanes] = got
            part_low[rows, lanes] = got.astype(BF)
        return carry

    lax.fori_loop(0, 2, one_row, 0)


def attention_forward(*args):
    outs = [
        jax.ShapeDtypeStruct((9, 512, 256), BF), shaped(512, 640, BF), shaped(512, D, F32),
        shaped(512, D, BF),
    ]
    return pl.pallas_call(
        attention_kernel,
        out_shape=outs,
        compiler_params=params(20),
        cost_estimate=cost(3 * 10**9, [*args, *outs]),
    )(*args)


class Moves:
    def __init__(self, sems):
        self.sems, self.count, self.open = sems, 0, {}

    def start(self, name, source, to):
        copy = pltpu.make_async_copy(source, to, self.sems.at[self.count])
        copy.start()
        self.count += 1
        self.open.setdefault(name, []).append(copy)

    def wait(self, *names):
        for name in names or tuple(self.open):
            for copy in self.open.pop(name):
                copy.wait()


def down_lanes(at, s):
    return pl.ds(pl.multiple_of(lax.rem(at[0] - at[1] * s + 4, 4) * 384, 384), 384)


def feed_kernel(
    at, gains, tok_own, tok_other, part, other, cot_own, cot_other, perm_a_in, perm_b_in, *refs
):
    blocks = refs[:12]
    mlp_row, middle_out, out_own, out_send, d_two_out = refs[12:17]
    kept, grads = refs[17:22], refs[22:28]
    (
        tok, middle, near, cot, wg, wu, wd, perm_a, perm_b, n2, n2_a, n2_b, two_at, two_bt,
        act, d_gate, d_up, wide, tall, own, low, d_two, sems, grad_sems,
    ) = refs[28:]
    moves = Moves(sems)
    for b, (t, c) in enumerate(((tok_own, cot_own), (tok_other, cot_other))):
        moves.start("rows", t, tok.at[pl.ds(b * TOK, TOK), :])
    moves.start("rows", part, middle)
    moves.start("rows", other, near)
    moves.start("perms", perm_a_in, perm_a)
    moves.start("perms", perm_b_in, perm_b)
    for s in range(4):
        moves.start("weights", blocks[s], wg.at[pl.ds(288 * s, 288), :])
        moves.start("weights", blocks[4 + s], wu.at[pl.ds(288 * s, 288), :])
        moves.start("weights", blocks[8 + s], wd.at[down_lanes(at, s), :])
    moves.start("weights", cot_own, cot.at[pl.ds(0, TOK), :])
    moves.start("weights", cot_other, cot.at[pl.ds(TOK, TOK), :])
    moves.wait("rows")
    for b in range(2):
        rows, swapped = slice(b * TOK, b * TOK + TOK), slice((1 - b) * TOK, (2 - b) * TOK)
        value = tok[rows, :].astype(F32) + middle[rows, :] + near[swapped, :].astype(F32)
        middle[rows, :] = value
        r2 = lax.rsqrt(jnp.mean(value * value, axis=1, keepdims=True) + EPS)
        n2[rows, :] = (value * r2 * gains[1:2, :]).astype(BF)
    moves.start("middle", middle, middle_out)
    moves.wait("perms")
    for n in range(3):
        lanes = slice(384 * n, 384 * n + 384)
        n2_a[:, lanes] = dot(n2[...], perm_a[:, lanes]).astype(BF)
        n2_b[:, lanes] = dot(n2[...], perm_b[:, lanes]).astype(BF)
    two_at[...] = n2_a[...].T
    two_bt[...] = n2_b[...].T
    moves.start("kept", two_at, kept[0])
    moves.start("kept", two_bt, kept[1])
    moves.wait("weights")

    def grad_copies(k, i):
        lanes = pl.ds(pl.multiple_of(i * 256, 256), 256)
        slot = lax.rem(i, 2)
        return [
            pltpu.make_async_copy(
                wide.at[k, slot, pl.ds(288 * s, 288), :], grads[2 * k + s].at[:, lanes],
                grad_sems.at[k, slot, s],
            )
            for s in range(2)
        ]

    def columns(i, carry):
        lanes = pl.ds(pl.multiple_of(i * 256, 256), 256)
        gate, up = dot(n2_a[...], wg[:, lanes]), dot(n2_b[...], wu[:, lanes])
        d_act = dot_t(cot[...], wd[lanes, :])
        sig = 1.0 / (1.0 + jnp.exp(-gate))
        swish = gate * sig
        act[:, lanes] = (swish * up).astype(BF)
        d_up[:, lanes] = (d_act * swish).astype(BF)
        d_gate[:, lanes] = (d_act * up * sig * (1.0 + gate * (1.0 - sig))).astype(BF)

        @pl.when(i >= 2)
        def _():
            for k in range(2):
                for c in grad_copies(k, i - 2):
                    c.wait()

        slot = lax.rem(i, 2)
        wide[0, slot] = dot(two_at[288:864, :], d_gate[:, lanes]).astype(BF)
        wide[1, slot] = dot(two_bt[288:864, :], d_up[:, lanes]).astype(BF)
        for k in range(2):
            for c in grad_copies(k, i):
                c.start()
        return carry

    lax.fori_loop(0, 6, columns, 0)
    for to, value in zip(kept[2:], (d_gate, d_up, act)):
        moves.start("kept", value, to)
    for s in (1, 2):
        tall[s - 1] = t_dot(act[:, down_lanes(at, s)], cot[...]).astype(BF)
        moves.start("down", tall.at[s - 1], grads[3 + s])

    def back(i, carry):
        lanes = pl.ds(pl.multiple_of(i * 384, 384), 384)
        n2_a[:, lanes] = dot_t(d_gate[...], wg[lanes, :]).astype(BF)
        n2_b[:, lanes] = dot_t(d_up[...], wu[lanes, :]).astype(BF)
        got = dot(act[...], wd[:, lanes])
        own[:, lanes] = middle[:TOK, lanes] + got[:TOK]
        low[:, lanes] = got[TOK:].astype(BF)
        return carry

    lax.fori_loop(0, 3, back, 0)
    moves.start("out", own, out_own)
    moves.start("out", low, out_send)
    value = middle[...]
    r2 = lax.rsqrt(jnp.mean(value * value, axis=1, keepdims=True) + EPS)

    def unmix(i, carry):
        lanes = pl.ds(pl.multiple_of(i * 384, 384), 384)
        got = dot_t(n2_a[...], perm_a[lanes, :]) + dot_t(n2_b[...], perm_b[lanes, :])
        d_two[:, lanes] = got.astype(BF)
        total = jnp.sum(got * middle[:, lanes] * r2, axis=0, keepdims=True)
        mlp_row[:, lanes] = jnp.broadcast_to(total, (8, 384))
        return carry

    lax.fori_loop(0, 3, unmix, 0)
    moves.start("two", d_two, d_two_out)
    for i in (4, 5):
        for k in range(2):
            for c in grad_copies(k, i):
                c.wait()
    moves.wait()


VMEM = pl.BlockSpec(memory_space=pltpu.VMEM)


def feed_forward_and_back(*args):
    outs = [
        shaped(8, D, F32), shaped(512, D, F32), shaped(TOK, D, F32), shaped(TOK, D, BF),
        shaped(512, D, BF), *[shaped(D, 512, BF)] * 2, *[shaped(512, 1536, BF)] * 3,
        *[shaped(288, 1536, BF)] * 4, *[shaped(384, D, BF)] * 2,
    ]
    return pl.pallas_call(
        feed_kernel,
        out_shape=outs,
        in_specs=[SMEM, VMEM] + [ANY] * 20,
        out_specs=[VMEM] + [ANY] * 15,
        scratch_shapes=[
            pltpu.VMEM((512, D), BF), pltpu.VMEM((512, D), F32), *[pltpu.VMEM((512, D), BF)] * 2,
            pltpu.VMEM((D, 1536), BF), pltpu.VMEM((D, 1536), BF), pltpu.VMEM((1536, D), BF),
            *[pltpu.VMEM((D, D), BF)] * 2, *[pltpu.VMEM((512, D), BF)] * 3,
            *[pltpu.VMEM((D, 512), BF)] * 2, *[pltpu.VMEM((512, 1536), BF)] * 3,
            pltpu.VMEM((2, 2, 576, 256), BF), pltpu.VMEM((2, 384, D), BF),
            pltpu.VMEM((TOK, D), F32), pltpu.VMEM((TOK, D), BF), pltpu.VMEM((512, D), BF),
            pltpu.SemaphoreType.DMA((40,)), pltpu.SemaphoreType.DMA((2, 2, 2)),
        ],
        compiler_params=params(56),
        cost_estimate=cost(23 * 10**9, [*args, *outs]),
    )(*args)


def grads_kernel(at, *refs):
    ins, outs = refs[:7], refs[7:13]
    two_a, two_b, d_gate, d_up, act, cot, wide, tall, sems = refs[13:]
    moves = Moves(sems)
    order = (3, 0)
    for i, s in enumerate(order):
        moves.start("a", ins[0].at[pl.ds(288 * s, 288), :], two_a.at[i])
    moves.start("a", ins[2], d_gate)
    for i, s in enumerate(order):
        moves.start("b", ins[1].at[pl.ds(288 * s, 288), :], two_b.at[i])
    moves.start("b", ins[3], d_up)
    moves.start("c", ins[4], act)
    moves.start("c", ins[5], cot.at[pl.ds(0, TOK), :])
    moves.start("c", ins[6], cot.at[pl.ds(TOK, TOK), :])
    for k, (name, left, right) in enumerate((("a", two_a, d_gate), ("b", two_b, d_up))):
        moves.wait(name)
        for i in range(2):
            wide[k, i] = dot(left[i], right[...]).astype(BF)
            moves.start("out", wide.at[k, i], outs[3 * i + k])
    moves.wait("c")
    for i, s in enumerate(order):
        tall[i] = t_dot(act[:, down_lanes(at, s)], cot[...]).astype(BF)
        moves.start("out", tall.at[i], outs[3 * i + 2])
    moves.wait()


def last_grads(*args):
    outs = [shaped(288, 1536, BF), shaped(288, 1536, BF), shaped(384, D, BF)] * 2
    return pl.pallas_call(
        grads_kernel,
        out_shape=outs,
        in_specs=[SMEM] + [ANY] * 7,
        out_specs=[ANY] * 6,
        scratch_shapes=[
            *[pltpu.VMEM((2, 288, 512), BF)] * 2, *[pltpu.VMEM((512, 1536), BF)] * 3,
            pltpu.VMEM((512, D), BF), pltpu.VMEM((2, 2, 288, 1536), BF),
            pltpu.VMEM((2, 384, D), BF), pltpu.SemaphoreType.DMA((20,)),
        ],
        compiler_params=params(24),
        cost_estimate=cost(27 * 10**8, [*args, *outs]),
    )(*args)


def add_kernel(*refs):
    n = len(refs) // 3
    for a, b, out in zip(refs[:n], refs[n : 2 * n], refs[2 * n :]):
        out[...] = (a[...].astype(F32) + b[...].astype(F32)).astype(BF)


def added(parts, arrived):
    blocks = [pl.BlockSpec((p.shape[0], p.shape[1] // 3), lambda i: (0, i)) for p in parts]
    return pl.pallas_call(
        add_kernel,
        grid=(3,),
        out_shape=[shaped(*p.shape, BF) for p in parts],
        in_specs=blocks * 2,
        out_specs=blocks,
        compiler_params=params(12),
        cost_estimate=cost(10**6, [*parts, *arrived, *parts]),
    )(*parts, *arrived)


def scores_back_kernel(
    gains, middle_in, d_two_in, other_in, cot_own, cot_other, w_o_in, probs_in, *refs
):
    turned_in, kv_in, cos_in, sin_in = refs[0], refs[1:5], refs[5], refs[6]
    d_middle_out, d_branch_out, d_qkv_out = refs[7:10]
    (
        middle, d_two, other, cot, w_o, probs, turned, k_lo, k_hi, v_lo, v_hi, cos, sin,
        d_middle, d_branch, d_mixed, d_pre, d_qkv, sems,
    ) = refs[10:]
    moves = Moves(sems)
    moves.start("rows", middle_in, middle)
    moves.start("rows", d_two_in, d_two)
    moves.start("rows", other_in, other)
    moves.start("rows", cot_own, cot.at[pl.ds(0, TOK), :])
    moves.start("rows", cot_other, cot.at[pl.ds(TOK, TOK), :])
    moves.start("w_o", w_o_in, w_o)
    for source, to in zip((turned_in, *kv_in, cos_in, sin_in, probs_in),
                          (turned, k_lo, k_hi, v_lo, v_hi, cos, sin, probs)):
        moves.start("heads", source, to)
    moves.wait("rows")
    for b in range(2):
        rows, swapped = slice(b * TOK, b * TOK + TOK), slice((1 - b) * TOK, (2 - b) * TOK)
        value = middle[rows, :]
        r2 = lax.rsqrt(jnp.mean(value * value, axis=1, keepdims=True) + EPS)
        e2 = gains[1:2, :] * (d_two[rows, :].astype(F32) + other[swapped, :].astype(F32))
        got = cot[rows, :].astype(F32) + r2 * (
            e2 - value * (r2 * r2 * jnp.mean(value * e2, axis=1, keepdims=True))
        )
        if b == 0:
            d_middle[...] = got
            moves.start("out", d_middle, d_middle_out)
        d_branch[rows, :] = got.astype(BF)
    moves.start("out", d_branch, d_branch_out)
    moves.wait("w_o")
    d_mixed[...] = dot_t(d_branch[...], w_o[...]).astype(BF)
    moves.wait("heads")

    def one_row(b, carry):
        rows = pl.ds(pl.multiple_of(b * TOK, TOK), TOK)
        d_k = {}
        d_v = {}
        for j in range(5):
            lanes = slice(128 * j, 128 * j + 128)
            q_pair, d_pair = turned[rows, lanes], d_mixed[rows, lanes]
            total = None
            for h in (2 * j, 2 * j + 1):
                if h == 9:
                    continue
                kv, half = h // 3, h % 2
                at_kv = slice(128 * kv, 128 * kv + 128)
                k_ref, v_ref = (k_lo, v_lo) if half == 0 else (k_hi, v_hi)
                p = probs[h, rows, :]
                p32 = p.astype(F32)
                d_probs = dot_t(d_pair, v_ref[rows, at_kv])
                row_dot = jnp.sum(p32 * d_probs, axis=1, keepdims=True)
                d_raw = (p32 * (d_probs - row_dot) * HEAD ** (-0.5)).astype(BF)
                got = dot(d_raw, k_ref[rows, at_kv])
                total = got if total is None else total + got
                for sums, value in ((d_k, t_dot(d_raw, q_pair)), (d_v, t_dot(p, d_pair))):
                    sums[kv, half] = value if (kv, half) not in sums else sums[kv, half] + value
            d_pre[:, lanes] = total
        low = low_lanes((TOK, 128))

        def collected(sums, kv, half):
            return sums[kv, half] + pltpu.roll(sums[kv, 1 - half], 64, 1)

        d_pre[:, 512:640] = jnp.where(low, d_pre[:, 512:640], collected(d_k, 0, 1))
        d_pre[:, 640:768] = jnp.where(low, collected(d_k, 1, 0), collected(d_k, 2, 1))
        for j in range(6):
            lanes = slice(128 * j, 128 * j + 128)
            d_qkv[rows, lanes] = turn(d_pre[:, lanes], cos[rows, :], -sin[rows, :]).astype(BF)
        d_qkv[rows, 768:896] = jnp.where(low, collected(d_v, 0, 0), collected(d_v, 1, 1)).astype(BF)
        d_qkv[rows, 896:1024] = jnp.where(low, collected(d_v, 2, 0), 0.0).astype(BF)
        return carry

    lax.fori_loop(0, 2, one_row, 0)
    moves.start("out", d_qkv, d_qkv_out)
    moves.wait()


def scores_back(*args):
    outs = [shaped(TOK, D, F32), shaped(512, D, BF), shaped(512, 1024, BF)]
    return pl.pallas_call(
        scores_back_kernel,
        out_shape=outs,
        in_specs=[VMEM] + [ANY] * (len(args) - 1),
        out_specs=[ANY] * 3,
        scratch_shapes=[
            pltpu.VMEM((512, D), F32), *[pltpu.VMEM((512, D), BF)] * 3, pltpu.VMEM((640, D), BF),
            pltpu.VMEM((9, 512, 256), BF), pltpu.VMEM((512, 768), BF),
            *[pltpu.VMEM((512, 384), BF)] * 4, *[pltpu.VMEM((512, 128), F32)] * 2,
            pltpu.VMEM((TOK, D), F32), pltpu.VMEM((512, D), BF), pltpu.VMEM((512, 640), BF),
            pltpu.VMEM((TOK, 768), F32), pltpu.VMEM((512, 1024), BF),
            pltpu.SemaphoreType.DMA((20,)),
        ],
        compiler_params=params(28),
        cost_estimate=cost(4 * 10**9, [*args, *outs]),
    )(*args)


def attention_grads_kernel(
    at, mlp_row, tok_own, tok_other, w_in, perm_in, left_in, right_in, normed_in, mixed_in,
    d_branch_in, d_qkv_in, part_own_out, part_send_out, sent_grads,
    tok, w, perm, left_t, right_t, normed_p, mixed, d_branch, d_qkv,
    grads, part_own, part_send, d_p, g_out, rows_of_gains, sems,
):
    moves = Moves(sems)
    moves.start("qkv", d_qkv_in, d_qkv)
    moves.start("qkv", normed_in, normed_p)
    moves.start("out", mixed_in, mixed)
    moves.start("out", d_branch_in, d_branch)
    moves.start("out", left_in, left_t)
    moves.start("out", right_in, right_t)
    moves.start("back", w_in.at[:, pl.ds(0, 1024)], w)
    moves.start("back", perm_in, perm)
    moves.start("back", tok_own, tok.at[pl.ds(0, TOK), :])
    moves.start("back", tok_other, tok.at[pl.ds(TOK, TOK), :])
    moves.wait("qkv")

    def qkv_grads(i, carry):
        lanes = pl.ds(pl.multiple_of(i * 256, 256), 256)
        grads[:, lanes] = t_dot(normed_p[...], d_qkv[:, lanes]).astype(BF)
        return carry

    lax.fori_loop(0, 4, qkv_grads, 0)
    moves.wait("out")
    g_out[...] = t_dot(mixed[...], d_branch[...]).astype(BF)
    grads[:, 1024:1536] = (
        dot(left_t[...], g_out[:, :512]) + dot(right_t[...], g_out[:, 640:])
    ).astype(BF)
    grads[:, 1536:] = dot(left_t[...], g_out[:, 512:640]).astype(BF)
    moves.wait("back")
    total = jnp.zeros((1, D), F32)
    for b in range(2):
        rows = slice(b * TOK, b * TOK + TOK)
        d_p[...] = dot_t(d_qkv[rows, :], w[...]).astype(BF)
        x = tok[rows, :].astype(F32)
        r1 = lax.rsqrt(jnp.mean(x * x, axis=1, keepdims=True) + EPS)
        got = dot_t(d_p[...], perm[...])
        total = total + jnp.sum(got * x * r1, axis=0, keepdims=True)
        if b == 0:
            part_own[...] = got
            moves.start("part", part_own, part_own_out)
        else:
            part_send[...] = got.astype(BF)
            moves.start("part", part_send, part_send_out)
    which = lax.broadcasted_iota(jnp.int32, (128, D), 0)
    rows_of_gains[...] = jnp.where(
        which == 64, total, jnp.where(which == 65, mlp_row[0:1, :], 0.0)
    ).astype(BF)
    gain_columns = dot(rows_of_gains[...], perm[...]).T
    grads[:, 896:1024] = (grads[:, 896:1024].astype(F32) + gain_columns).astype(BF)
    for i in range(16):
        block = jnp.where(at[1] > 0, i, (i % 4) * 4 + i // 4)
        to = sent_grads.at[pl.ds(pl.multiple_of(block * 80, 80), 80), :]
        moves.start("grads", grads.at[pl.ds(80 * i, 80), :], to)
    moves.wait()


def attention_grads(*args):
    outs = [shaped(TOK, D, F32), shaped(TOK, D, BF), shaped(DP, 1664, BF)]
    return pl.pallas_call(
        attention_grads_kernel,
        out_shape=outs,
        in_specs=[SMEM, VMEM] + [ANY] * (len(args) - 2),
        out_specs=[ANY] * 3,
        scratch_shapes=[
            pltpu.VMEM((512, D), BF), pltpu.VMEM((DP, 1024), BF), pltpu.VMEM((D, DP), BF),
            *[pltpu.VMEM((DP, 640), BF)] * 2, pltpu.VMEM((512, DP), BF), pltpu.VMEM((512, 640), BF),
            pltpu.VMEM((512, D), BF), pltpu.VMEM((512, 1024), BF), pltpu.VMEM((DP, 1664), BF),
            pltpu.VMEM((TOK, D), F32), pltpu.VMEM((TOK, D), BF), pltpu.VMEM((TOK, DP), BF),
            pltpu.VMEM((640, D), BF), pltpu.VMEM((128, D), BF), pltpu.SemaphoreType.DMA((32,)),
        ],
        compiler_params=params(36),
        cost_estimate=cost(6 * 10**9, [*args, *outs]),
    )(*args)


class Lockstep:
    def __init__(self):
        self.last = ()

    def tie(self, *values):
        tied = lax.optimization_barrier((*values, *self.last))
        self.last = tied
        return tied[: len(values)]

    def after(self, *values):
        self.last = (*self.last, *values)

    def __call__(self, values, pairs, late=(), late_pairs=(), beside=tuple):
        tied = lax.optimization_barrier((*values, *self.last))
        sent = [send(v, p) for v, p in zip(tied, pairs)]
        sent += [send(v, p) for v, p in zip(late, late_pairs)]
        sent += beside()
        self.last = lax.optimization_barrier(tuple(sent))
        return list(self.last)

    def gather(self, blocks, axes, more=(), more_pairs=()):
        values = [b for b in blocks for _ in range(3)]
        pairs = [STRAIGHT[a][n] for a in axes for n in (1, 2, 3)]
        got = self([*values, *more], [*pairs, *more_pairs])
        rings = [[b, *got[3 * i : 3 * i + 3]] for i, b in enumerate(blocks)]
        return rings, got[3 * len(blocks) :]

    def scatter(self, makers, axes, table, more=(), more_pairs=()):
        values = [make(s).astype(BF) for make in makers for s in (1, 2, 3)]
        pairs = [table[a][4 - s] for a in axes for s in (1, 2, 3)]
        got = self([*values, *more], [*pairs, *more_pairs])
        sums = [
            sum([g.astype(F32) for g in got[3 * i : 3 * i + 3]], make(0).astype(F32))
            for i, make in enumerate(makers)
        ]
        return sums, got[3 * len(makers) :]


def place(blocks, at, sign):
    out = jnp.zeros((4, *blocks[0].shape), blocks[0].dtype)
    for step, block in enumerate(blocks):
        out = lax.dynamic_update_index_in_dim(out, block, (at - sign * step) % 4, 0)
    return out


def row_tables(segment_row):
    places = jnp.arange(TOK, dtype=jnp.int32)
    same_doc = segment_row[:, None] == segment_row[None, :]
    starts = jnp.min(jnp.where(same_doc, places[None, :], TOK), axis=1)
    offsets = (places - starts).astype(F32)
    lane = jnp.arange(128, dtype=jnp.int32)
    frequency = jnp.exp((lane % 32).astype(F32) * (-2.0 * math.log(THETA) / HEAD))
    angles = offsets[:, None] * frequency[None, :]
    side = jnp.where(lane % 64 < 32, -1.0, 1.0)
    allowed = same_doc & (places[:, None] >= places[None, :])
    return jnp.cos(angles), jnp.sin(angles) * side, jnp.where(allowed, 0.0, -1e30).astype(F32)


def body(
    tokens, segments, attn_gain, w_query, w_key, w_value, w_out, mlp_gain, w_gate, w_up, w_down,
    cotangent,
):
    core = lax.axis_index("core")
    at = {
        "x": lax.axis_index("x"),
        "y": lax.axis_index("y"),
        "z": lax.axis_index("z_hi") * 2 + lax.axis_index("z_lo"),
    }
    sign = 1 - 2 * core
    first = core == 0

    def halves(w):
        n = w.shape[1] // 2
        low, high = w[:, :n], w[:, n:]
        return jnp.where(first, low, high), jnp.where(first, high, low)

    pairs = [halves(w) for w in (w_gate, w_query, w_up, w_key, w_value)]
    gain_pair = jnp.stack([attn_gain, mlp_gain], axis=1)

    def columns(parts):
        gate, query, up, key, value = parts
        return jnp.concatenate([gate, up, query, key, value, gain_pair], axis=1)

    kept, given = columns([p[0] for p in pairs]), columns([p[1] for p in pairs])
    step = Lockstep()
    given, traded = step(
        [given, jnp.concatenate([w_out, w_down], axis=0)], [CORES, TRADE]
    )
    rows = jnp.concatenate([jnp.where(first, kept, given), jnp.where(first, given, kept)], axis=0)


    order_a, order_b, order_c = ("x", "z", "y"), ("y", "x", "z"), ("z", "y", "x")

    def natural(order):
        k = jnp.arange(D, dtype=jnp.int32)
        r, t = k % 18, k // 18
        c = {}
        for level, axis in enumerate(order):
            c[axis] = (at[axis] - (sign if level > 0 else 1) * ((t // 4**level) % 4)) % 4
        chip = (((c["z"] // 2) * 4 + c["x"]) * 2 + c["z"] % 2) * 4 + c["y"]
        return chip * 18 + r

    one, two, three = zip(order_a, order_b, order_c)
    out_rows = traded[:9]
    attn_rows = jnp.concatenate(
        [rows[:, 3072:], jnp.zeros((18, 62), BF),
         jnp.concatenate([out_rows[:, :640], jnp.pad(out_rows[:, 640:], ((0, 0), (0, 128)))], axis=0)],
        axis=1,
    )
    got = step([attn_rows] * 3, [STRAIGHT["z"][n] for n in (1, 2, 3)])
    w_attn = stack_rows([attn_rows, *got], 80)
    w_attn = lax.all_gather(w_attn, ("x", "y"), axis=0, tiled=True)
    (ha, hb, hc), _ = step.gather([rows[:, :1536], rows[:, 1536:3072], traded[9:]], one)
    down = place(hc, at["z"], 1).reshape(2, 2, 24, D)
    down = jnp.transpose(down, (1, 0, 2, 3)).reshape(96, D)
    ring = [RINGS[a] for a in two]
    held = [[stack_rows(ha), stack_rows(hb), down]]
    *arrived, tok_other, seg_other = step(
        [*held[-1], tokens, segments.astype(F32)], [*ring, CORES, CORES]
    )
    held.append(arrived)
    *arrived, cot_other = step([*held[-1], cotangent], [*ring, CORES])
    held.append(arrived)
    seg_other = seg_other.astype(jnp.int32)
    tables = [row_tables(segments[0]), row_tables(seg_other[0])]
    cos, sin, bias = (jnp.concatenate(t, axis=0) for t in zip(*tables))

    rows_a, rows_b = natural(order_a), natural(order_b)

    k = jnp.arange(DP, dtype=jnp.int32)
    x_at, y_at, r, s = k // 320, (k // 80) % 4, (k % 80) % 18, (k % 80) // 18
    z = (at["z"] - s) % 4
    source = (((z // 2 * 4 + x_at) * 2 + z % 2) * 4 + y_at) * 18 + r
    source = jnp.where(s < 4, source, -1)
    e = ((x_at * 2 + z % 2) * 4 + y_at) * 2 + z // 2
    to_left = jnp.where((r < 9) & (s < 4), e * 9 + r, -1)
    to_right = jnp.where((r >= 9) & (s < 4), e * 9 + r - 9, -1)
    rows_a, rows_b, source, to_left, to_right, *_ = lax.optimization_barrier(
        (rows_a, rows_b, source, to_left, to_right, *step.last)
    )
    d_at = jnp.arange(D, dtype=jnp.int32)[:, None]
    perm_a, perm_b, perm = ((d_at == i[None, :]).astype(BF) for i in (rows_a, rows_b, source))
    e_at = jnp.arange(640, dtype=jnp.int32)
    left, right = ((e_at[:, None] == i[None, :]).astype(BF) for i in (to_left, to_right))
    left_t, right_t = ((i[:, None] == e_at[None, :]).astype(BF) for i in (to_left, to_right))
    one_hots = (perm, left, right, perm_a, perm_b, left_t, right_t)
    held.append(step(held[-1], ring))
    ha, hb, hc = zip(*held)
    ring = [RINGS[a] for a in three]
    down = place([h.reshape(2, 48, D) for h in hc], at["y"], sign)
    down = jnp.transpose(down, (1, 0, 2, 3)).reshape(384, D)
    held = [[jnp.concatenate(ha, axis=0), jnp.concatenate(hb, axis=0), down]]
    (w_attn,) = step.tie(w_attn)
    normed_p, turned, k_lo, k_hi, v_lo, v_hi, w_o, gains = attention_heads(
        tokens, tok_other, w_attn, perm, left, right, cos, sin
    )
    *arrived, turned = step(held[-1], ring, beside=lambda: (turned,))
    held.append(arrived)
    probs, mixed, part, part_low = attention_forward(turned, k_lo, k_hi, v_lo, v_hi, w_o, bias)
    *arrived, part_low = step(held[-1], ring, beside=lambda: (part_low,))
    held.append(arrived)
    *arrived, part_other = step([*held[-1], part_low], [*ring, CORES])
    held.append(arrived)
    ha, hb, hc = zip(*held)

    where = jnp.stack([at["x"], sign]).astype(jnp.int32)
    mlp_row, middle, out_own, out_send, d_two, *kept = feed_forward_and_back(
        where, gains, tokens, tok_other, part, part_other, cotangent, cot_other, perm_a, perm_b,
        *ha, *hb, *hc,
    )
    kept, grads = kept[:5], kept[5:]

    d_middle, d_branch, d_qkv = scores_back(
        gains, middle, d_two, swap(d_two), cotangent, cot_other, w_o, probs, turned, k_lo, k_hi,
        v_lo, v_hi, cos, sin,
    )
    *arrived, d_qkv = step(grads[0::2], ring, beside=lambda: (d_qkv,))
    sums = added(grads[1::2], arrived)
    part_own, part_send, g_attn = attention_grads(
        where, mlp_row, tokens, tok_other, w_attn, perm, left_t, right_t, normed_p, mixed,
        d_branch, d_qkv,
    )
    rest = last_grads(where, *kept, cotangent, cot_other)
    *arrived, part_send, g_attn = step(sums, ring, beside=lambda: (part_send, g_attn))
    *arrived, part_other = step([*added(rest[:3], arrived), part_send], [*ring, CORES])
    g_gate, g_up, g_down = added(rest[3:], arrived)
    g_attn_x = lax.psum_scatter(
        g_attn, AXES, scatter_dimension=0, tiled=True, axis_index_groups=LINES["x", "y"]
    )
    g_attn = lax.psum_scatter(
        g_attn_x, AXES, scatter_dimension=0, tiled=True, axis_index_groups=LINES["y", "x"]
    )

    output = (out_own + swap(out_send).astype(F32)).astype(BF)
    d_normed = part_own + part_other.astype(F32)
    x_own = tokens.astype(F32)
    r_own = lax.rsqrt(jnp.mean(x_own * x_own, axis=-1, keepdims=True) + EPS)
    e1 = d_normed * gains[0]
    grad_input = d_middle + r_own * (
        e1 - x_own * r_own * r_own * jnp.mean(x_own * e1, axis=-1, keepdims=True)
    )

    def rows_of(held, n):
        return lambda s: held[n * s : n * s + n]

    def y_block(s):
        down = g_down.reshape(2, 4, 48, D)
        return lax.dynamic_index_in_dim(down, (at["y"] - sign * s) % 4, 1, False).reshape(96, D)

    (g_gate, g_up, g_down), _ = step.scatter([rows_of(g_gate, 72), rows_of(g_up, 72), y_block], two, SIGNED)

    def z_block(s):
        z = (at["z"] - s) % 4
        down = g_down.reshape(4, 24, D)
        return lax.dynamic_index_in_dim(down, (z % 2) * 2 + z // 2, 0, False)

    def attn_rows_of(s):
        return g_attn[18 * s : 18 * s + 18]

    step.after(g_attn_x)
    (g_gate, g_up, g_down), _ = step.scatter(
        [rows_of(g_gate, 18), rows_of(g_up, 18), z_block], one, STRAIGHT
    )
    (g_attn,), _ = step.scatter([attn_rows_of], ["z"], STRAIGHT)

    g_out = jnp.concatenate([g_attn[:9, 1024:], g_attn[9:, 1024:1536]], axis=1)
    g_rows = jnp.concatenate([g_gate, g_up, g_attn[:, :962]], axis=1)
    mine = jnp.where(first, g_rows[:9], g_rows[9:])
    theirs = jnp.where(first, g_rows[9:], g_rows[:9]).astype(BF)
    theirs, g_od = step(
        [theirs, jnp.concatenate([g_out, g_down], axis=0).astype(BF)], [CORES, TRADE]
    )
    g_od, theirs = g_od.astype(F32), theirs.astype(F32)
    low, high = jnp.where(first, mine, theirs), jnp.where(first, theirs, mine)
    g_gains = (low[:, 4032:] + high[:, 4032:]).T

    def joined(*cuts):
        return jnp.concatenate([h[:, a:b] for h in (low, high) for a, b in cuts], axis=1)

    g_g, g_u = joined((0, 1536)), joined((1536, 3072))
    g_q, g_k, g_v = joined((3072, 3648)), joined((3648, 3840)), joined((3840, 4032))
    return (
        output, grad_input, g_gains[0], g_q, g_k, g_v, g_od[:9], g_gains[1], g_g, g_u, g_od[9:],
    )


def solution(mesh):
    fine = Mesh(mesh.devices.reshape(SHAPE), AXES)
    rows, vector = P(AXES, None), P(AXES)
    return jax.shard_map(
        body,
        mesh=fine,
        in_specs=(rows, rows, vector, rows, rows, rows, rows, vector, rows, rows, rows, rows),
        out_specs=(rows, rows, vector, rows, rows, rows, rows, vector, rows, rows, rows),
        check_vma=False,
    )
```

```python
import functools
import math

import jax
import jax.numpy as jnp
import numpy as np
from jax import lax
from jax.experimental import pallas as pl
from jax.experimental.pallas import tpu as pltpu
from jax.sharding import Mesh
from jax.sharding import PartitionSpec as P

D = 1152
HEADS = 18
KV_HEADS = 6
HEAD = 64
FF = 3072
DP = 1280
TOK = 256
EPS = 1e-05
THETA = 10000.0

SHAPE = (2, 4, 2, 4, 2)
AXES = ("z_hi", "x", "z_lo", "y", "core")
BF = jnp.bfloat16
F32 = jnp.float32


def device_pairs(move):
    pairs = []
    for i in range(128):
        zh, x, zl, y, c = (int(v) for v in np.unravel_index(i, SHAPE))
        x, y, z, c = move(x, y, zh * 2 + zl, c)
        x, y, z = x % 4, y % 4, z % 4
        pairs.append((i, int(np.ravel_multi_index((z // 2, x, z % 2, y, c), SHAPE))))
    return pairs


RINGS = {
    "x": device_pairs(lambda x, y, z, c: (x + 1 - 2 * c, y, z, c)),
    "y": device_pairs(lambda x, y, z, c: (x, y + 1 - 2 * c, z, c)),
    "z": device_pairs(lambda x, y, z, c: (x, y, z + 1 - 2 * c, c)),
}
CORES = device_pairs(lambda x, y, z, c: (x, y, z, 1 - c))
TRADE = device_pairs(lambda x, y, z, c: (x, y, c * 2 + z % 2, z // 2))


def lines(*axes):
    index = np.arange(128).reshape(SHAPE)
    groups = []
    for core, axis in enumerate(axes):
        along = np.moveaxis(index[..., core], AXES.index(axis), -1)
        groups += along.reshape(-1, 4).tolist()
    return groups


LINES = {("x", "y"): lines("x", "y"), ("y", "x"): lines("y", "x")}


def send(value, pairs):
    return lax.ppermute(value, AXES, pairs)


def swap(value):
    return send(value, CORES)


def dot(a, b):
    return jnp.dot(a, b, preferred_element_type=F32)


def dot_t(a, b):
    return lax.dot_general(a, b, (((1,), (1,)), ((), ())), preferred_element_type=F32)


def t_dot(a, b):
    return lax.dot_general(a, b, (((0,), (0,)), ((), ())), preferred_element_type=F32)


def shift(axis, n):
    return device_pairs(lambda x, y, z, c: (
        x + n * (axis == "x"), y + n * (axis == "y"), z + n * (axis == "z"), c))


def signed(axis, n):
    return device_pairs(lambda x, y, z, c: (
        x + n * (1 - 2 * c) * (axis == "x"), y + n * (1 - 2 * c) * (axis == "y"),
        z + n * (1 - 2 * c) * (axis == "z"), c))


SIGNED = {axis: {n: signed(axis, n) for n in (1, 2, 3)} for axis in ("x", "y", "z")}
STRAIGHT = {axis: {n: shift(axis, n) for n in (1, 2, 3)} for axis in ("x", "y", "z")}


def params(mib):
    return pltpu.CompilerParams(vmem_limit_bytes=mib * 2**20)


FAR = pl.BlockSpec(memory_space=pltpu.HBM)
SMEM = pl.BlockSpec(memory_space=pltpu.SMEM)
VMEM = pl.BlockSpec(memory_space=pltpu.VMEM)


def shaped(rows, columns, dtype):
    return jax.ShapeDtypeStruct((rows, columns), dtype)


def cost(flops, arrays):
    return pl.CostEstimate(
        flops=flops,
        bytes_accessed=sum(math.prod(a.shape) * a.dtype.itemsize for a in arrays),
        transcendentals=0,
    )


def low_lanes(shape):
    return lax.broadcasted_iota(jnp.int32, shape, 1) % 128 < 64


def turn(v, cos, sin):
    ahead = lax.broadcasted_iota(jnp.int32, v.shape, 1) % 64 < 32
    return v * cos + jnp.where(ahead, pltpu.roll(v, 96, 1), pltpu.roll(v, 32, 1)) * sin


def fill(to, index):
    def rows_of(i, carry):
        rows = pl.ds(pl.multiple_of(i * 128, 128), 128)
        at = lax.broadcasted_iota(jnp.int32, (128, to.shape[1]), 0) + i * 128
        to[rows, :] = jnp.where(at == index[...], 1.0, 0.0).astype(BF)
        return carry

    lax.fori_loop(0, to.shape[0] // 128, rows_of, 0)


def stack_kernel(*refs):
    *blocks, out = refs
    blocks = [b[...].astype(F32) for b in blocks]
    spare = out.shape[0] - sum(b.shape[0] for b in blocks)
    if spare:
        blocks.append(jnp.zeros((spare, out.shape[1]), F32))
    out[...] = jnp.concatenate(blocks, axis=0).astype(out.dtype)


def stack_rows(blocks, rows=72):
    return pl.pallas_call(
        stack_kernel,
        out_shape=shaped(rows, blocks[0].shape[1], blocks[0].dtype),
        compiler_params=params(8),
    )(*blocks)


CUTS = ((0, 1536), (1536, 1536), (3072, 576), (3648, 192), (3840, 192))


def halves_kernel(core, gate, up, query, key, value, gain_one, gain_two, out, down, kept, given, traded):
    first = core[0] == 0
    for (at, n), w in zip(CUTS, (gate, up, query, key, value)):
        low, high = w[:, :n].astype(F32), w[:, n:].astype(F32)
        kept[:, at : at + n] = jnp.where(first, low, high).astype(BF)
        given[:, at : at + n] = jnp.where(first, high, low).astype(BF)
    row = lax.broadcasted_iota(jnp.int32, (9, 9), 0)
    same = row == lax.broadcasted_iota(jnp.int32, (9, 9), 1)
    for i, gain in enumerate((gain_one, gain_two)):
        spread = jnp.where(same, jnp.broadcast_to(gain[...].astype(F32), (9, 9)), 0.0)
        column = jnp.sum(spread, axis=1, keepdims=True).astype(BF)
        kept[:, 4032 + i : 4033 + i] = column
        given[:, 4032 + i : 4033 + i] = column
    traded[...] = jnp.concatenate([out[...].astype(F32), down[...].astype(F32)], axis=0).astype(BF)


def halves(*args):
    return pl.pallas_call(
        halves_kernel,
        out_shape=[shaped(9, 4034, BF), shaped(9, 4034, BF), shaped(33, D, BF)],
        in_specs=[SMEM] + [VMEM] * 9,
        compiler_params=params(8),
    )(*args)


def whole_kernel(core, mine, theirs, traded, gate, up, query, key, value, out, down, gains):
    first = core[0] == 0
    own, other = mine[...], theirs[...].astype(F32)
    low, high = jnp.where(first, own, other), jnp.where(first, other, own)
    for (at, n), to in zip(CUTS, (gate, up, query, key, value)):
        to[:, :n] = low[:, at : at + n]
        to[:, n:] = high[:, at : at + n]
    rows = traded[...].astype(F32)
    out[...] = rows[:9]
    down[...] = rows[9:]
    same = lax.broadcasted_iota(jnp.int32, (9, 9), 0) == lax.broadcasted_iota(jnp.int32, (9, 9), 1)
    for i in range(2):
        column = low[:, 4032 + i : 4033 + i] + high[:, 4032 + i : 4033 + i]
        spread = jnp.where(same, jnp.broadcast_to(column, (9, 9)), 0.0)
        gains[i : i + 1, :] = jnp.sum(spread, axis=0, keepdims=True)


def whole(*args):
    outs = [shaped(9, 2 * n, F32) for _, n in CUTS]
    return pl.pallas_call(
        whole_kernel,
        out_shape=[*outs, shaped(9, D, F32), shaped(24, D, F32), shaped(2, 9, F32)],
        in_specs=[SMEM] + [VMEM] * 3,
        compiler_params=params(8),
    )(*args)


def heads_kernel(
    tok_own, tok_other, w, source, to_left, to_right, cos, sin,
    normed_p, turned, k_lo, k_hi, v_lo, v_hi, w_o, gains, gathered, pre, perm, left, right,
):
    fill(perm, source)
    fill(left, to_left)
    fill(right, to_right)
    gathered[...] = dot(perm[...], w[:, 896:1024]).T
    gains[...] = gathered[64:72, :]
    for b, tok in enumerate((tok_own, tok_other)):
        rows = slice(b * TOK, b * TOK + TOK)
        x = tok[...].astype(F32)
        r1 = lax.rsqrt(jnp.mean(x * x, axis=1, keepdims=True) + EPS)
        normed = (x * r1 * gains[0:1, :]).astype(BF)
        normed_p[rows, :] = dot(normed, perm[...]).astype(BF)
    w_o[:, :640] = dot(left[...], w[:, 1024:1664]).astype(BF)
    w_o[:, 640:] = dot(right[...], w[:, 1024:1536]).astype(BF)

    def one_row(b, carry):
        rows = pl.ds(pl.multiple_of(b * TOK, TOK), TOK)
        pre[...] = dot(normed_p[rows, :], w[:, :1024])
        for j in range(6):
            lanes = slice(128 * j, 128 * j + 128)
            turned[rows, lanes] = turn(pre[:, lanes], cos[rows, :], sin[rows, :]).astype(BF)
        low = low_lanes((TOK, 128))
        zero = jnp.zeros((TOK, 128), F32)

        def both(value, half, to_low, to_high, kv):
            value = jnp.where(low if half == 0 else ~low, value, zero)
            moved = pltpu.roll(value, 64, 1)
            pair = (value, moved) if half == 0 else (moved, value)
            lanes = slice(128 * kv, 128 * kv + 128)
            to_low[rows, lanes], to_high[rows, lanes] = pair[0].astype(BF), pair[1].astype(BF)

        for kv, (j, half) in enumerate(((4, 1), (5, 0), (5, 1))):
            lanes = slice(128 * j, 128 * j + 128)
            both(turned[rows, lanes].astype(F32), half, k_lo, k_hi, kv)
        for kv, (j, half) in enumerate(((6, 0), (6, 1), (7, 0))):
            both(pre[:, 128 * j : 128 * j + 128], half, v_lo, v_hi, kv)
        return carry

    lax.fori_loop(0, 2, one_row, 0)


def attention_heads(*args):
    outs = [
        shaped(512, DP, BF), shaped(512, 768, BF), *[shaped(512, 384, BF)] * 4, shaped(640, D, BF),
        shaped(8, D, F32),
    ]
    return pl.pallas_call(
        heads_kernel,
        out_shape=outs,
        scratch_shapes=[
            pltpu.VMEM((128, D), F32), pltpu.VMEM((TOK, 1024), F32), pltpu.VMEM((D, DP), BF),
            *[pltpu.VMEM((640, DP), BF)] * 2,
        ],
        compiler_params=params(32),
        cost_estimate=cost(5 * 10**9, [*args, *outs]),
    )(*args)


def attention_kernel(
    turned, k_lo, k_hi, v_lo, v_hi, w_o, bias, probs, mixed, part, part_low
):
    def one_row(b, carry):
        rows = pl.ds(pl.multiple_of(b * TOK, TOK), TOK)
        for j in range(5):
            lanes = slice(128 * j, 128 * j + 128)
            total = None
            for h in (2 * j, 2 * j + 1):
                if h == 9:
                    continue
                kv = slice(128 * (h // 3), 128 * (h // 3) + 128)
                k_ref, v_ref = (k_lo, v_lo) if h % 2 == 0 else (k_hi, v_hi)
                s = dot_t(turned[rows, lanes], k_ref[rows, kv]) * HEAD ** (-0.5) + bias[rows, :]
                e = jnp.exp(s - jnp.max(s, axis=1, keepdims=True))
                p = (e * (1.0 / jnp.sum(e, axis=1, keepdims=True))).astype(BF)
                probs[h, rows, :] = p
                got = dot(p, v_ref[rows, kv])
                total = got if total is None else total + got
            mixed[rows, lanes] = total.astype(BF)
        for n in range(3):
            lanes = slice(384 * n, 384 * n + 384)
            got = dot(mixed[rows, :], w_o[:, lanes])
            part[rows, lanes] = got
            part_low[rows, lanes] = got.astype(BF)
        return carry

    lax.fori_loop(0, 2, one_row, 0)


def attention_forward(*args):
    outs = [
        jax.ShapeDtypeStruct((9, 512, 256), BF), shaped(512, 640, BF), shaped(512, D, F32),
        shaped(512, D, BF),
    ]
    return pl.pallas_call(
        attention_kernel,
        out_shape=outs,
        compiler_params=params(20),
        cost_estimate=cost(3 * 10**9, [*args, *outs]),
    )(*args)


class Moves:
    def __init__(self, sems):
        self.sems, self.count, self.open = sems, 0, {}

    def start(self, name, source, to):
        copy = pltpu.make_async_copy(source, to, self.sems.at[self.count])
        copy.start()
        self.count += 1
        self.open.setdefault(name, []).append(copy)

    def wait(self, *names):
        for name in names or tuple(self.open):
            for copy in self.open.pop(name):
                copy.wait()


def middle_kernel(
    gains, rows_a, rows_b, tok_own, tok_other, part, other,
    middle_out, n2_a_out, n2_b_out, two_at_out, two_bt_out,
    tok, middle, near, perm_a, perm_b, n2, n2_a, n2_b, two_at, two_bt, sems,
):
    moves = Moves(sems)
    moves.start("rows", tok_own, tok.at[pl.ds(0, TOK), :])
    moves.start("rows", tok_other, tok.at[pl.ds(TOK, TOK), :])
    moves.start("rows", part, middle)
    moves.start("rows", other, near)
    fill(perm_a, rows_a)
    fill(perm_b, rows_b)
    moves.wait("rows")
    for b in range(2):
        rows, swapped = slice(b * TOK, b * TOK + TOK), slice((1 - b) * TOK, (2 - b) * TOK)
        value = tok[rows, :].astype(F32) + middle[rows, :] + near[swapped, :].astype(F32)
        middle[rows, :] = value
        r2 = lax.rsqrt(jnp.mean(value * value, axis=1, keepdims=True) + EPS)
        n2[rows, :] = (value * r2 * gains[1:2, :]).astype(BF)
    moves.start("out", middle, middle_out)
    for perm, to, across, to_out, across_out in (
        (perm_a, n2_a, two_at, n2_a_out, two_at_out),
        (perm_b, n2_b, two_bt, n2_b_out, two_bt_out),
    ):
        for n in range(3):
            lanes = slice(384 * n, 384 * n + 384)
            to[:, lanes] = dot(n2[...], perm[:, lanes]).astype(BF)
        moves.start("out", to, to_out)
        across[...] = to[...].T
        moves.start("out", across, across_out)
    moves.wait()


def middle_rows(*args):
    outs = [shaped(512, D, F32), *[shaped(512, D, BF)] * 2, *[shaped(D, 512, BF)] * 2]
    return pl.pallas_call(
        middle_kernel,
        out_shape=outs,
        in_specs=[VMEM] * 3 + [FAR] * 4,
        out_specs=[FAR] * 5,
        scratch_shapes=[
            pltpu.VMEM((512, D), BF), pltpu.VMEM((512, D), F32), pltpu.VMEM((512, D), BF),
            *[pltpu.VMEM((D, D), BF)] * 2, *[pltpu.VMEM((512, D), BF)] * 3,
            *[pltpu.VMEM((D, 512), BF)] * 2, pltpu.SemaphoreType.DMA((12,)),
        ],
        compiler_params=params(60),
        cost_estimate=cost(3 * 10**9, [*args, *outs]),
    )(*args)


def feed_kernel(n2_a_in, n2_b_in, two_at_in, two_bt_in, cot_own, cot_other, *refs):
    blocks, wd_in, kept, grads = refs[:8], refs[8], refs[9:12], refs[12:19]
    (
        n2_a, n2_b, two_at, two_bt, cot, wg, wu, wd, act, d_gate, d_up, wide, tall, sems,
        chunk_sems, grad_sems,
    ) = refs[19:]
    moves = Moves(sems)
    moves.start("rows", n2_a_in, n2_a)
    moves.start("rows", n2_b_in, n2_b)
    moves.start("rows", cot_own, cot.at[pl.ds(0, TOK), :])
    moves.start("rows", cot_other, cot.at[pl.ds(TOK, TOK), :])

    def weight_copies(i):
        lanes = pl.ds(pl.multiple_of(i * 256, 256), 256)
        pairs = [
            (blocks[4 * k + s].at[:, lanes], to.at[pl.ds(288 * s, 288), lanes])
            for s in range(4)
            for k, to in enumerate((wg, wu))
        ]
        pairs.append((wd_in.at[lanes, :], wd.at[lanes, :]))
        return [pltpu.make_async_copy(a, b, chunk_sems.at[i, j]) for j, (a, b) in enumerate(pairs)]

    for i in range(3):
        for c in weight_copies(i):
            c.start()
    moves.wait("rows")

    def grad_copies(k, i):
        lanes = pl.ds(pl.multiple_of(i * 256, 256), 256)
        slot = lax.rem(i, 2)
        return [
            pltpu.make_async_copy(
                wide.at[k, slot, pl.ds(288 * s, 288), :], grads[3 * k + s].at[:, lanes],
                grad_sems.at[k, slot, s],
            )
            for s in range(3)
        ]

    def columns(i, carry):
        lanes = pl.ds(pl.multiple_of(i * 256, 256), 256)
        for c in weight_copies(i):
            c.wait()

        @pl.when(i < 3)
        def _():
            for c in weight_copies(i + 3):
                c.start()

        gate, up = dot(n2_a[...], wg[:, lanes]), dot(n2_b[...], wu[:, lanes])
        d_act = dot_t(cot[...], wd[lanes, :])
        sig = 1.0 / (1.0 + jnp.exp(-gate))
        swish = gate * sig
        act[:, lanes] = (swish * up).astype(BF)
        d_up[:, lanes] = (d_act * swish).astype(BF)
        d_gate[:, lanes] = (d_act * up * sig * (1.0 + gate * (1.0 - sig))).astype(BF)
        return carry

    def grad_columns(i, carry):
        lanes = pl.ds(pl.multiple_of(i * 256, 256), 256)

        @pl.when(i >= 2)
        def _():
            for k in range(2):
                for c in grad_copies(k, i - 2):
                    c.wait()

        slot = lax.rem(i, 2)
        wide[0, slot] = dot(two_at[...], d_gate[:, lanes]).astype(BF)
        wide[1, slot] = dot(two_bt[...], d_up[:, lanes]).astype(BF)
        for k in range(2):
            for c in grad_copies(k, i):
                c.start()
        return carry

    lax.fori_loop(0, 4, columns, 0)
    moves.start("across", two_at_in.at[pl.ds(288, 864), :], two_at)
    moves.start("across", two_bt_in.at[pl.ds(288, 864), :], two_bt)
    lax.fori_loop(4, 6, columns, 0)
    for to, value in zip(kept, (act, d_gate, d_up)):
        moves.start("kept", value, to)
    moves.wait("across")
    lax.fori_loop(0, 6, grad_columns, 0)
    for n in range(4):
        rows = slice(384 * n, 384 * n + 384)
        tall[rows, :] = t_dot(act[:, rows], cot[...]).astype(BF)
        moves.start("down", tall.at[pl.ds(384 * n, 384), :], grads[6].at[pl.ds(384 * n, 384), :])
    for i in (4, 5):
        for k in range(2):
            for c in grad_copies(k, i):
                c.wait()
    moves.wait()


def feed_forward(*args):
    outs = [*[shaped(512, 1536, BF)] * 3, *[shaped(288, 1536, BF)] * 6, shaped(1536, D, BF)]
    return pl.pallas_call(
        feed_kernel,
        out_shape=outs,
        in_specs=[FAR] * 15,
        out_specs=[FAR] * 10,
        scratch_shapes=[
            *[pltpu.VMEM((512, D), BF)] * 2, *[pltpu.VMEM((864, 512), BF)] * 2,
            pltpu.VMEM((512, D), BF), pltpu.VMEM((D, 1536), BF), pltpu.VMEM((D, 1536), BF),
            pltpu.VMEM((1536, D), BF), *[pltpu.VMEM((512, 1536), BF)] * 3,
            pltpu.VMEM((2, 2, 864, 256), BF), pltpu.VMEM((1536, D), BF),
            pltpu.SemaphoreType.DMA((20,)), pltpu.SemaphoreType.DMA((6, 9)),
            pltpu.SemaphoreType.DMA((2, 2, 3)),
        ],
        compiler_params=params(60),
        cost_estimate=cost(10 * 10**9, [*args, *outs]),
    )(*args)


def feed_back_kernel(rows_a, rows_b, middle_in, d_gate_in, d_up_in, act_in, *refs):
    blocks, wd_in = refs[:8], refs[8]
    mlp_row, out_own, out_send, d_two_out = refs[9:13]
    (
        middle, act, d_gate, d_up, wg, wu, wd, perm_a, perm_b, d_a, d_b, own, low, d_two, sems,
    ) = refs[13:]
    moves = Moves(sems)
    moves.start("gate", d_gate_in, d_gate)
    for s in range(4):
        moves.start("gate", blocks[s], wg.at[pl.ds(288 * s, 288), :])
    moves.start("up", d_up_in, d_up)
    for s in range(4):
        moves.start("up", blocks[4 + s], wu.at[pl.ds(288 * s, 288), :])
    fill(perm_a, rows_a)
    fill(perm_b, rows_b)

    def times(left, right, to):
        def columns(i, carry):
            lanes = pl.ds(pl.multiple_of(i * 384, 384), 384)
            to[:, lanes] = dot_t(left[...], right[lanes, :]).astype(BF)
            return carry

        lax.fori_loop(0, 3, columns, 0)

    moves.wait("gate")
    moves.start("middle", middle_in, middle)
    moves.start("down", act_in, act)
    moves.start("down", wd_in, wd)
    times(d_gate, wg, d_a)
    moves.wait("up")
    times(d_up, wu, d_b)
    moves.wait("middle")
    value = middle[...]
    r2 = lax.rsqrt(jnp.mean(value * value, axis=1, keepdims=True) + EPS)

    def unmix(i, carry):
        lanes = pl.ds(pl.multiple_of(i * 384, 384), 384)
        got = dot_t(d_a[...], perm_a[lanes, :]) + dot_t(d_b[...], perm_b[lanes, :])
        d_two[:, lanes] = got.astype(BF)
        total = jnp.sum(got * middle[:, lanes] * r2, axis=0, keepdims=True)
        mlp_row[:, lanes] = jnp.broadcast_to(total, (8, 384))
        return carry

    lax.fori_loop(0, 3, unmix, 0)
    moves.start("two", d_two, d_two_out)
    moves.wait("down")

    def out(i, carry):
        lanes = pl.ds(pl.multiple_of(i * 384, 384), 384)
        got = dot(act[...], wd[:, lanes])
        own[:, lanes] = middle[:TOK, lanes] + got[:TOK]
        low[:, lanes] = got[TOK:].astype(BF)
        return carry

    lax.fori_loop(0, 3, out, 0)
    moves.start("out", own, out_own)
    moves.start("out", low, out_send)
    moves.wait()


def feed_back(*args):
    outs = [shaped(8, D, F32), shaped(TOK, D, F32), shaped(TOK, D, BF), shaped(512, D, BF)]
    return pl.pallas_call(
        feed_back_kernel,
        out_shape=outs,
        in_specs=[VMEM] * 2 + [FAR] * 13,
        out_specs=[VMEM] + [FAR] * 3,
        scratch_shapes=[
            pltpu.VMEM((512, D), F32), *[pltpu.VMEM((512, 1536), BF)] * 3,
            pltpu.VMEM((D, 1536), BF), pltpu.VMEM((D, 1536), BF), pltpu.VMEM((1536, D), BF),
            *[pltpu.VMEM((D, D), BF)] * 2, *[pltpu.VMEM((512, D), BF)] * 2,
            pltpu.VMEM((TOK, D), F32), pltpu.VMEM((TOK, D), BF), pltpu.VMEM((512, D), BF),
            pltpu.SemaphoreType.DMA((24,)),
        ],
        compiler_params=params(60),
        cost_estimate=cost(8 * 10**9, [*args, *outs]),
    )(*args)


def grads_kernel(s, *refs):
    ins, outs = refs[:4], refs[4:6]
    two_a, two_b, d_gate, d_up, wide, sems = refs[6:]
    moves = Moves(sems)
    moves.start("a", ins[0].at[pl.ds(288 * s, 288), :], two_a)
    moves.start("a", ins[2], d_gate)
    moves.start("b", ins[1].at[pl.ds(288 * s, 288), :], two_b)
    moves.start("b", ins[3], d_up)
    for k, (name, left, right) in enumerate((("a", two_a, d_gate), ("b", two_b, d_up))):
        moves.wait(name)
        wide[k] = dot(left[...], right[...]).astype(BF)
        moves.start("out", wide.at[k], outs[k])
    moves.wait()


def feed_grads(s, *args):
    outs = [shaped(288, 1536, BF)] * 2
    return pl.pallas_call(
        functools.partial(grads_kernel, s),
        out_shape=outs,
        in_specs=[FAR] * 4,
        out_specs=[FAR] * 2,
        scratch_shapes=[
            *[pltpu.VMEM((288, 512), BF)] * 2, *[pltpu.VMEM((512, 1536), BF)] * 2,
            pltpu.VMEM((2, 288, 1536), BF), pltpu.SemaphoreType.DMA((12,)),
        ],
        compiler_params=params(60),
        cost_estimate=cost(9 * 10**8, [*args, *outs]),
    )(*args)


def add_kernel(*refs):
    n = len(refs) // 3
    for a, b, out in zip(refs[:n], refs[n : 2 * n], refs[2 * n :]):
        out[...] = (a[...].astype(F32) + b[...].astype(F32)).astype(BF)


def added(parts, arrived):
    blocks = [pl.BlockSpec((p.shape[0], p.shape[1] // 3), lambda i: (0, i)) for p in parts]
    return pl.pallas_call(
        add_kernel,
        grid=(3,),
        out_shape=[shaped(*p.shape, BF) for p in parts],
        in_specs=blocks * 2,
        out_specs=blocks,
        compiler_params=params(12),
        cost_estimate=cost(10**6, [*parts, *arrived, *parts]),
    )(*parts, *arrived)


def attention_back_kernel(
    gains, mlp_row, source, to_left, to_right, middle_in, d_two_in, other_in, cot_own, cot_other,
    w_o_in, probs_in, *refs
):
    turned_in, kv_in, cos_in, sin_in = refs[0], refs[1:5], refs[5], refs[6]
    tok_own, tok_other, w_in, normed_in, mixed_in = refs[7:12]
    d_middle_out, part_own_out, part_send_out, sent_grads = refs[12:16]
    (
        middle, d_two, other, cot, w_o, probs, turned, k_lo, k_hi, v_lo, v_hi, cos, sin,
        d_middle, d_branch, d_mixed, d_pre, d_qkv,
        tok, w, perm, left, right, normed_p, mixed, grads, part_own, part_send, d_p, g_out,
        rows_of_gains, sems,
    ) = refs[16:]
    moves = Moves(sems)
    moves.start("rows", middle_in, middle)
    moves.start("rows", d_two_in, d_two)
    moves.start("rows", other_in, other)
    moves.start("rows", cot_own, cot.at[pl.ds(0, TOK), :])
    moves.start("rows", cot_other, cot.at[pl.ds(TOK, TOK), :])
    moves.start("w_o", w_o_in, w_o)
    fill(perm, source)
    fill(left, to_left)
    fill(right, to_right)
    moves.wait("rows")
    for far, to in zip((turned_in, *kv_in, cos_in, sin_in, probs_in),
                       (turned, k_lo, k_hi, v_lo, v_hi, cos, sin, probs)):
        moves.start("heads", far, to)
    for b in range(2):
        rows, swapped = slice(b * TOK, b * TOK + TOK), slice((1 - b) * TOK, (2 - b) * TOK)
        value = middle[rows, :]
        r2 = lax.rsqrt(jnp.mean(value * value, axis=1, keepdims=True) + EPS)
        e2 = gains[1:2, :] * (d_two[rows, :].astype(F32) + other[swapped, :].astype(F32))
        got = cot[rows, :].astype(F32) + r2 * (
            e2 - value * (r2 * r2 * jnp.mean(value * e2, axis=1, keepdims=True))
        )
        if b == 0:
            d_middle[...] = got
            moves.start("out", d_middle, d_middle_out)
        d_branch[rows, :] = got.astype(BF)
    moves.wait("w_o")
    d_mixed[...] = dot_t(d_branch[...], w_o[...]).astype(BF)
    moves.wait("heads")
    moves.start("normed", normed_in, normed_p)
    moves.start("mixed", mixed_in, mixed)
    moves.start("back", w_in.at[:, pl.ds(0, 1024)], w)
    moves.start("back", tok_own, tok.at[pl.ds(0, TOK), :])
    moves.start("back", tok_other, tok.at[pl.ds(TOK, TOK), :])

    def one_row(b, carry):
        rows = pl.ds(pl.multiple_of(b * TOK, TOK), TOK)
        d_k = {}
        d_v = {}
        for j in range(5):
            lanes = slice(128 * j, 128 * j + 128)
            q_pair, d_pair = turned[rows, lanes], d_mixed[rows, lanes]
            total = None
            for h in (2 * j, 2 * j + 1):
                if h == 9:
                    continue
                kv, half = h // 3, h % 2
                at_kv = slice(128 * kv, 128 * kv + 128)
                k_ref, v_ref = (k_lo, v_lo) if half == 0 else (k_hi, v_hi)
                p = probs[h, rows, :]
                p32 = p.astype(F32)
                d_probs = dot_t(d_pair, v_ref[rows, at_kv])
                row_dot = jnp.sum(p32 * d_probs, axis=1, keepdims=True)
                d_raw = (p32 * (d_probs - row_dot) * HEAD ** (-0.5)).astype(BF)
                got = dot(d_raw, k_ref[rows, at_kv])
                total = got if total is None else total + got
                for sums, value in ((d_k, t_dot(d_raw, q_pair)), (d_v, t_dot(p, d_pair))):
                    sums[kv, half] = value if (kv, half) not in sums else sums[kv, half] + value
            d_pre[:, lanes] = total
        low = low_lanes((TOK, 128))

        def collected(sums, kv, half):
            return sums[kv, half] + pltpu.roll(sums[kv, 1 - half], 64, 1)

        d_pre[:, 512:640] = jnp.where(low, d_pre[:, 512:640], collected(d_k, 0, 1))
        d_pre[:, 640:768] = jnp.where(low, collected(d_k, 1, 0), collected(d_k, 2, 1))
        for j in range(6):
            lanes = slice(128 * j, 128 * j + 128)
            d_qkv[rows, lanes] = turn(d_pre[:, lanes], cos[rows, :], -sin[rows, :]).astype(BF)
        d_qkv[rows, 768:896] = jnp.where(low, collected(d_v, 0, 0), collected(d_v, 1, 1)).astype(BF)
        d_qkv[rows, 896:1024] = jnp.where(low, collected(d_v, 2, 0), 0.0).astype(BF)
        return carry

    lax.fori_loop(0, 2, one_row, 0)
    moves.wait("normed")

    def qkv_grads(i, carry):
        lanes = pl.ds(pl.multiple_of(i * 256, 256), 256)
        grads[:, lanes] = t_dot(normed_p[...], d_qkv[:, lanes]).astype(BF)
        return carry

    lax.fori_loop(0, 4, qkv_grads, 0)
    moves.wait("mixed")
    g_out[...] = t_dot(mixed[...], d_branch[...]).astype(BF)
    grads[:, 1024:1536] = (
        t_dot(left[...], g_out[:, :512]) + t_dot(right[...], g_out[:, 640:])
    ).astype(BF)
    grads[:, 1536:] = t_dot(left[...], g_out[:, 512:640]).astype(BF)
    moves.wait("back")
    total = jnp.zeros((1, D), F32)
    for b in range(2):
        rows = slice(b * TOK, b * TOK + TOK)
        d_p[...] = dot_t(d_qkv[rows, :], w[...]).astype(BF)
        x = tok[rows, :].astype(F32)
        r1 = lax.rsqrt(jnp.mean(x * x, axis=1, keepdims=True) + EPS)
        got = dot_t(d_p[...], perm[...])
        total = total + jnp.sum(got * x * r1, axis=0, keepdims=True)
        if b == 0:
            part_own[...] = got
            moves.start("part", part_own, part_own_out)
        else:
            part_send[...] = got.astype(BF)
            moves.start("part", part_send, part_send_out)
    which = lax.broadcasted_iota(jnp.int32, (128, D), 0)
    rows_of_gains[...] = jnp.where(
        which == 64, total, jnp.where(which == 65, mlp_row[0:1, :], 0.0)
    ).astype(BF)
    gain_columns = dot(rows_of_gains[...], perm[...]).T
    grads[:, 896:1024] = (grads[:, 896:1024].astype(F32) + gain_columns).astype(BF)
    moves.start("grads", grads, sent_grads)
    moves.wait()


def attention_back(*args):
    outs = [shaped(TOK, D, F32), shaped(TOK, D, F32), shaped(TOK, D, BF), shaped(DP, 1664, BF)]
    return pl.pallas_call(
        attention_back_kernel,
        out_shape=outs,
        in_specs=[VMEM] * 5 + [FAR] * (len(args) - 5),
        out_specs=[FAR] * 4,
        scratch_shapes=[
            pltpu.VMEM((512, D), F32), *[pltpu.VMEM((512, D), BF)] * 3, pltpu.VMEM((640, D), BF),
            pltpu.VMEM((9, 512, 256), BF), pltpu.VMEM((512, 768), BF),
            *[pltpu.VMEM((512, 384), BF)] * 4, *[pltpu.VMEM((512, 128), F32)] * 2,
            pltpu.VMEM((TOK, D), F32), pltpu.VMEM((512, D), BF), pltpu.VMEM((512, 640), BF),
            pltpu.VMEM((TOK, 768), F32), pltpu.VMEM((512, 1024), BF),
            pltpu.VMEM((512, D), BF), pltpu.VMEM((DP, 1024), BF), pltpu.VMEM((D, DP), BF),
            *[pltpu.VMEM((640, DP), BF)] * 2, pltpu.VMEM((512, DP), BF), pltpu.VMEM((512, 640), BF),
            pltpu.VMEM((DP, 1664), BF), pltpu.VMEM((TOK, D), F32), pltpu.VMEM((TOK, D), BF),
            pltpu.VMEM((TOK, DP), BF), pltpu.VMEM((640, D), BF), pltpu.VMEM((128, D), BF),
            pltpu.SemaphoreType.DMA((40,)),
        ],
        compiler_params=params(60),
        cost_estimate=cost(10 * 10**9, [*args, *outs]),
    )(*args)


class Lockstep:
    def __init__(self):
        self.last = ()

    def tie(self, *values):
        tied = lax.optimization_barrier((*values, *self.last))
        self.last = tied
        return tied[: len(values)]

    def after(self, *values):
        self.last = (*self.last, *values)

    def __call__(self, values, pairs, late=(), late_pairs=(), beside=tuple):
        tied = lax.optimization_barrier((*values, *self.last))
        sent = [send(v, p) for v, p in zip(tied, pairs)]
        sent += [send(v, p) for v, p in zip(late, late_pairs)]
        sent += beside()
        self.last = lax.optimization_barrier(tuple(sent))
        return list(self.last)

    def gather(self, blocks, axes, more=(), more_pairs=()):
        values = [b for b in blocks for _ in range(3)]
        pairs = [STRAIGHT[a][n] for a in axes for n in (1, 2, 3)]
        got = self([*values, *more], [*pairs, *more_pairs])
        rings = [[b, *got[3 * i : 3 * i + 3]] for i, b in enumerate(blocks)]
        return rings, got[3 * len(blocks) :]

    def scatter(self, makers, axes, table, more=(), more_pairs=()):
        values = [make(s).astype(BF) for make in makers for s in (1, 2, 3)]
        pairs = [table[a][4 - s] for a in axes for s in (1, 2, 3)]
        got = self([*values, *more], [*pairs, *more_pairs])
        sums = [
            sum([g.astype(F32) for g in got[3 * i : 3 * i + 3]], make(0).astype(F32))
            for i, make in enumerate(makers)
        ]
        return sums, got[3 * len(makers) :]


def place(blocks, at, sign):
    out = jnp.zeros((4, *blocks[0].shape), blocks[0].dtype)
    for step, block in enumerate(blocks):
        out = lax.dynamic_update_index_in_dim(out, block, (at - sign * step) % 4, 0)
    return out


def row_tables(segment_row):
    places = jnp.arange(TOK, dtype=jnp.int32)
    same_doc = segment_row[:, None] == segment_row[None, :]
    starts = jnp.min(jnp.where(same_doc, places[None, :], TOK), axis=1)
    offsets = (places - starts).astype(F32)
    lane = jnp.arange(128, dtype=jnp.int32)
    frequency = jnp.exp((lane % 32).astype(F32) * (-2.0 * math.log(THETA) / HEAD))
    angles = offsets[:, None] * frequency[None, :]
    side = jnp.where(lane % 64 < 32, -1.0, 1.0)
    allowed = same_doc & (places[:, None] >= places[None, :])
    return jnp.cos(angles), jnp.sin(angles) * side, jnp.where(allowed, 0.0, -1e30).astype(F32)


def body(
    tokens, segments, attn_gain, w_query, w_key, w_value, w_out, mlp_gain, w_gate, w_up, w_down,
    cotangent,
):
    core = lax.axis_index("core")
    at = {
        "x": lax.axis_index("x"),
        "y": lax.axis_index("y"),
        "z": lax.axis_index("z_hi") * 2 + lax.axis_index("z_lo"),
    }
    sign = 1 - 2 * core
    first = core == 0

    which = jnp.reshape(core, (1,)).astype(jnp.int32)
    kept, given, traded = halves(
        which, w_gate, w_up, w_query, w_key, w_value, attn_gain.reshape(1, 9),
        mlp_gain.reshape(1, 9), w_out, w_down,
    )
    step = Lockstep()
    given, traded = step([given, traded], [CORES, TRADE])
    rows = jnp.concatenate([jnp.where(first, kept, given), jnp.where(first, given, kept)], axis=0)


    order_a, order_b, order_c = ("x", "z", "y"), ("y", "x", "z"), ("z", "y", "x")

    def natural(order):
        k = jnp.arange(D, dtype=jnp.int32)
        r, t = k % 18, k // 18
        c = {}
        for level, axis in enumerate(order):
            c[axis] = (at[axis] - (sign if level > 0 else 1) * ((t // 4**level) % 4)) % 4
        chip = (((c["z"] // 2) * 4 + c["x"]) * 2 + c["z"] % 2) * 4 + c["y"]
        return chip * 18 + r

    one, two, three = zip(order_a, order_b, order_c)
    out_rows = traded[:9]
    attn_rows = jnp.concatenate(
        [rows[:, 3072:], jnp.zeros((18, 62), BF),
         jnp.concatenate([out_rows[:, :640], jnp.pad(out_rows[:, 640:], ((0, 0), (0, 128)))], axis=0)],
        axis=1,
    )
    got = step([attn_rows] * 3, [STRAIGHT["z"][n] for n in (1, 2, 3)])
    w_attn = stack_rows([attn_rows, *got], 80)
    w_attn = lax.all_gather(
        w_attn, AXES, axis=0, tiled=True, axis_index_groups=LINES["y", "x"]
    )
    (ha, hb, hc), _ = step.gather([rows[:, :1536], rows[:, 1536:3072], traded[9:]], one)
    down = place(hc, at["z"], 1).reshape(2, 2, 24, D)
    down = jnp.transpose(down, (1, 0, 2, 3)).reshape(96, D)
    rows_a, rows_b = natural(order_a), natural(order_b)

    k = jnp.arange(DP, dtype=jnp.int32)
    outer, inner, r, s = k // 320, (k // 80) % 4, (k % 80) % 18, (k % 80) // 18
    x_at, y_at = jnp.where(first, outer, inner), jnp.where(first, inner, outer)
    z = (at["z"] - s) % 4
    source = (((z // 2 * 4 + x_at) * 2 + z % 2) * 4 + y_at) * 18 + r
    source = jnp.where(s < 4, source, -1)
    e = ((x_at * 2 + z % 2) * 4 + y_at) * 2 + z // 2
    to_left = jnp.where((r < 9) & (s < 4), e * 9 + r, -1)
    to_right = jnp.where((r >= 9) & (s < 4), e * 9 + r - 9, -1)
    rows_a, rows_b, source = (i[None, :] for i in (rows_a, rows_b, source))
    (w_attn,) = step.tie(w_attn)
    w_attn = lax.all_gather(
        w_attn, AXES, axis=0, tiled=True, axis_index_groups=LINES["x", "y"]
    )
    ring = [RINGS[a] for a in two]
    held = [[stack_rows(ha), stack_rows(hb), down]]
    *arrived, tok_other, seg_other = step(
        [*held[-1], tokens, segments.astype(F32)], [*ring, CORES, CORES]
    )
    held.append(arrived)
    *arrived, cot_other = step([*held[-1], cotangent], [*ring, CORES])
    held.append(arrived)
    seg_other = seg_other.astype(jnp.int32)
    tables = [row_tables(segments[0]), row_tables(seg_other[0])]
    cos, sin, bias = (jnp.concatenate(t, axis=0) for t in zip(*tables))

    held.append(step(held[-1], ring))
    ha, hb, hc = zip(*held)
    ring = [RINGS[a] for a in three[:2]]
    down = place([h.reshape(2, 48, D) for h in hc], at["y"], sign)
    down = jnp.transpose(down, (1, 0, 2, 3)).reshape(384, D)
    held = [[jnp.concatenate(ha, axis=0), jnp.concatenate(hb, axis=0)]]
    w_attn, down = step.tie(w_attn, down)
    wd = lax.all_gather(down, "x", axis=0, tiled=True)
    normed_p, turned, k_lo, k_hi, v_lo, v_hi, w_o, gains = attention_heads(
        tokens, tok_other, w_attn, source, to_left[None, :], to_right[None, :], cos, sin
    )
    *arrived, turned = step(held[-1], ring, beside=lambda: (turned,))
    held.append(arrived)
    probs, mixed, part, part_low = attention_forward(turned, k_lo, k_hi, v_lo, v_hi, w_o, bias)
    *arrived, part_low = step(held[-1], ring, beside=lambda: (part_low,))
    held.append(arrived)
    rows = middle_rows(gains, rows_a, rows_b, tokens, tok_other, part, swap(part_low))
    *arrived, middle, n2_a, n2_b, two_at, two_bt = step(held[-1], ring, beside=lambda: rows)
    held.append(arrived)
    ha, hb = zip(*held)

    act, d_gate, d_up, *grads = feed_forward(
        n2_a, n2_b, two_at, two_bt, cotangent, cot_other, *ha, *hb, wd
    )
    kept = (two_at, two_bt, d_gate, d_up)
    g_down = lax.psum_scatter(grads[6], "x", scatter_dimension=0, tiled=True)

    mlp_row, out_own, out_send, d_two = feed_back(
        rows_a, rows_b, middle, d_gate, d_up, act, *ha, *hb, wd
    )
    *arrived, d_two = step([grads[0], grads[3]], ring, beside=lambda: (d_two,))
    sums = added([grads[1], grads[4]], arrived)
    d_middle, part_own, part_send, g_attn = attention_back(
        gains, mlp_row, source, to_left[None, :], to_right[None, :], middle, d_two, swap(d_two),
        cotangent, cot_other, w_o, probs, turned, k_lo, k_hi, v_lo, v_hi, cos, sin, tokens,
        tok_other, w_attn, normed_p, mixed,
    )
    *kept, part_send = lax.optimization_barrier((*kept, part_send))
    *arrived, part_send, g_attn = step(sums, ring, beside=lambda: (part_send, g_attn))
    sums = added([grads[2], grads[5]], arrived)
    *arrived, part_other, out_other = step([*sums, part_send, out_send], [*ring, CORES, CORES])
    g_gate, g_up = added(feed_grads(0, *kept), arrived)
    g_attn_x = lax.psum_scatter(
        g_attn, AXES, scatter_dimension=0, tiled=True, axis_index_groups=LINES["x", "y"]
    )
    g_attn = lax.psum_scatter(
        g_attn_x, AXES, scatter_dimension=0, tiled=True, axis_index_groups=LINES["y", "x"]
    )

    output = (out_own + out_other.astype(F32)).astype(BF)
    d_normed = part_own + part_other.astype(F32)
    x_own = tokens.astype(F32)
    r_own = lax.rsqrt(jnp.mean(x_own * x_own, axis=-1, keepdims=True) + EPS)
    e1 = d_normed * gains[0]
    grad_input = d_middle + r_own * (
        e1 - x_own * r_own * r_own * jnp.mean(x_own * e1, axis=-1, keepdims=True)
    )

    def rows_of(held, n):
        return lambda s: held[n * s : n * s + n]

    def y_block(s):
        down = g_down.reshape(2, 4, 48, D)
        return lax.dynamic_index_in_dim(down, (at["y"] - sign * s) % 4, 1, False).reshape(96, D)

    (g_gate, g_down), _ = step.scatter([rows_of(g_gate, 72), y_block], (two[0], two[2]), SIGNED)
    step.after(g_attn_x)
    (g_up,), _ = step.scatter([rows_of(g_up, 72)], two[1:2], SIGNED)

    def z_block(s):
        z = (at["z"] - s) % 4
        down = g_down.reshape(4, 24, D)
        return lax.dynamic_index_in_dim(down, (z % 2) * 2 + z // 2, 0, False)

    def attn_rows_of(s):
        return g_attn[18 * s : 18 * s + 18]

    (g_gate, g_up, g_down), _ = step.scatter(
        [rows_of(g_gate, 18), rows_of(g_up, 18), z_block], one, STRAIGHT
    )
    got = [send(attn_rows_of(s), STRAIGHT["z"][4 - s]) for s in (1, 2, 3)]
    g_attn = sum([g.astype(F32) for g in got], attn_rows_of(0).astype(F32))

    g_out = jnp.concatenate([g_attn[:9, 1024:], g_attn[9:, 1024:1536]], axis=1)
    g_rows = jnp.concatenate([g_gate, g_up, g_attn[:, :962]], axis=1)
    mine = jnp.where(first, g_rows[:9], g_rows[9:])
    theirs = jnp.where(first, g_rows[9:], g_rows[:9]).astype(BF)
    theirs, g_od = step(
        [theirs, jnp.concatenate([g_out, g_down], axis=0).astype(BF)], [CORES, TRADE]
    )
    g_g, g_u, g_q, g_k, g_v, g_o, g_d, g_gains = whole(which, mine, theirs, g_od)
    return (
        output, grad_input, g_gains[0], g_q, g_k, g_v, g_o, g_gains[1], g_g, g_u, g_d,
    )


def solution(mesh):
    fine = Mesh(mesh.devices.reshape(SHAPE), AXES)
    rows, vector = P(AXES, None), P(AXES)
    return jax.shard_map(
        body,
        mesh=fine,
        in_specs=(rows, rows, vector, rows, rows, rows, rows, vector, rows, rows, rows, rows),
        out_specs=(rows, rows, vector, rows, rows, rows, rows, vector, rows, rows, rows),
        check_vma=False,
    )
```

```python
import functools
import math

import jax
import jax.numpy as jnp
import numpy as np
from jax import lax
from jax.experimental import pallas as pl
from jax.experimental.pallas import tpu as pltpu
from jax.sharding import Mesh
from jax.sharding import PartitionSpec as P

D = 1152
HEADS = 18
KV_HEADS = 6
HEAD = 64
FF = 3072
DP = 1280
TOK = 256
EPS = 1e-05
THETA = 10000.0

SHAPE = (2, 4, 2, 4, 2)
AXES = ("z_hi", "x", "z_lo", "y", "core")
BF = jnp.bfloat16
F32 = jnp.float32


def device_pairs(move):
    pairs = []
    for i in range(128):
        zh, x, zl, y, c = (int(v) for v in np.unravel_index(i, SHAPE))
        x, y, z, c = move(x, y, zh * 2 + zl, c)
        x, y, z = x % 4, y % 4, z % 4
        pairs.append((i, int(np.ravel_multi_index((z // 2, x, z % 2, y, c), SHAPE))))
    return pairs


RINGS = {
    "x": device_pairs(lambda x, y, z, c: (x + 1 - 2 * c, y, z, c)),
    "y": device_pairs(lambda x, y, z, c: (x, y + 1 - 2 * c, z, c)),
    "z": device_pairs(lambda x, y, z, c: (x, y, z + 1 - 2 * c, c)),
}
CORES = device_pairs(lambda x, y, z, c: (x, y, z, 1 - c))
TRADE = device_pairs(lambda x, y, z, c: (x, y, c * 2 + z % 2, z // 2))


def lines(*axes):
    index = np.arange(128).reshape(SHAPE)
    groups = []
    for core, axis in enumerate(axes):
        along = np.moveaxis(index[..., core], AXES.index(axis), -1)
        groups += along.reshape(-1, 4).tolist()
    return groups


LINES = {("x", "y"): lines("x", "y"), ("y", "x"): lines("y", "x")}


def send(value, pairs):
    return lax.ppermute(value, AXES, pairs)


def swap(value):
    return send(value, CORES)


def dot(a, b):
    return jnp.dot(a, b, preferred_element_type=F32)


def dot_t(a, b):
    return lax.dot_general(a, b, (((1,), (1,)), ((), ())), preferred_element_type=F32)


def t_dot(a, b):
    return lax.dot_general(a, b, (((0,), (0,)), ((), ())), preferred_element_type=F32)


def shift(axis, n):
    return device_pairs(lambda x, y, z, c: (
        x + n * (axis == "x"), y + n * (axis == "y"), z + n * (axis == "z"), c))


def signed(axis, n):
    return device_pairs(lambda x, y, z, c: (
        x + n * (1 - 2 * c) * (axis == "x"), y + n * (1 - 2 * c) * (axis == "y"),
        z + n * (1 - 2 * c) * (axis == "z"), c))


SIGNED = {axis: {n: signed(axis, n) for n in (1, 2, 3)} for axis in ("x", "y", "z")}
STRAIGHT = {axis: {n: shift(axis, n) for n in (1, 2, 3)} for axis in ("x", "y", "z")}


def params(mib):
    return pltpu.CompilerParams(vmem_limit_bytes=mib * 2**20)


FAR = pl.BlockSpec(memory_space=pltpu.HBM)
SMEM = pl.BlockSpec(memory_space=pltpu.SMEM)
VMEM = pl.BlockSpec(memory_space=pltpu.VMEM)


def shaped(rows, columns, dtype):
    return jax.ShapeDtypeStruct((rows, columns), dtype)


def cost(flops, arrays):
    return pl.CostEstimate(
        flops=flops,
        bytes_accessed=sum(math.prod(a.shape) * a.dtype.itemsize for a in arrays),
        transcendentals=0,
    )


def low_lanes(shape):
    return lax.broadcasted_iota(jnp.int32, shape, 1) % 128 < 64


def turn(v, cos, sin):
    ahead = lax.broadcasted_iota(jnp.int32, v.shape, 1) % 64 < 32
    return v * cos + jnp.where(ahead, pltpu.roll(v, 96, 1), pltpu.roll(v, 32, 1)) * sin


def fill(to, index):
    def rows_of(i, carry):
        rows = pl.ds(pl.multiple_of(i * 128, 128), 128)
        at = lax.broadcasted_iota(jnp.int32, (128, to.shape[1]), 0) + i * 128
        to[rows, :] = jnp.where(at == index[...], 1.0, 0.0).astype(BF)
        return carry

    lax.fori_loop(0, to.shape[0] // 128, rows_of, 0)


def stack_kernel(*refs):
    *blocks, out = refs
    out[...] = jnp.concatenate([b[...].astype(F32) for b in blocks], axis=0).astype(out.dtype)


def stack_rows(blocks):
    rows = sum(b.shape[0] for b in blocks)
    return pl.pallas_call(
        stack_kernel,
        out_shape=shaped(rows, blocks[0].shape[1], blocks[0].dtype),
        compiler_params=params(8),
    )(*blocks)


CUTS = ((0, 1536), (1536, 1536), (3072, 576), (3648, 192), (3840, 192))


def folded(rows):
    last = jnp.concatenate([rows[18:, 384 * j : 384 * j + 384] for j in range(3)], axis=0)
    return jnp.concatenate([rows[:18], last], axis=1)


def unfolded(rows):
    last = [rows[6 * j : 6 * j + 6, D:] for j in range(3)]
    return jnp.concatenate([rows[:, :D], jnp.concatenate(last, axis=1)], axis=0)


def z_place(at, s):
    z = lax.rem(at[0] - s + 4, 4)
    return lax.rem(z, 2) * 2 + z // 2


def spread_kernel(at, *refs):
    *blocks, attn, down = refs
    rows = [b[...].astype(F32) for b in blocks]
    spare = jnp.zeros((8, 1664), F32)
    attn[...] = jnp.concatenate([*(r[:, :1664] for r in rows), spare], axis=0).astype(BF)
    for s, r in enumerate(rows):
        down[z_place(at, s)] = unfolded(r[:, 1664:]).astype(BF)


def spread(at, *blocks):
    return pl.pallas_call(
        spread_kernel,
        out_shape=[shaped(80, 1664, BF), jax.ShapeDtypeStruct((4, 24, D), BF)],
        in_specs=[SMEM] + [VMEM] * 4,
        compiler_params=params(8),
    )(at, *blocks)


def pack_kernel(at, attn, down, *outs):
    rows = attn[...].astype(F32)
    for s, out in enumerate(outs):
        out[:, :1664] = rows[18 * s : 18 * s + 18].astype(BF)
        out[:, 1664:] = folded(down[z_place(at, s)].astype(F32)).astype(BF)


def pack(*args):
    return pl.pallas_call(
        pack_kernel,
        out_shape=[shaped(18, 3200, BF)] * 4,
        in_specs=[SMEM] + [VMEM] * 2,
        compiler_params=params(8),
    )(*args)


def halves_kernel(core, gate, up, query, key, value, gain_one, gain_two, out, down, kept, given, traded):
    first = core[0] == 0
    for (at, n), w in zip(CUTS, (gate, up, query, key, value)):
        low, high = w[:, :n].astype(F32), w[:, n:].astype(F32)
        kept[:, at : at + n] = jnp.where(first, low, high).astype(BF)
        given[:, at : at + n] = jnp.where(first, high, low).astype(BF)
    row = lax.broadcasted_iota(jnp.int32, (9, 9), 0)
    same = row == lax.broadcasted_iota(jnp.int32, (9, 9), 1)
    for i, gain in enumerate((gain_one, gain_two)):
        spread = jnp.where(same, jnp.broadcast_to(gain[...].astype(F32), (9, 9)), 0.0)
        column = jnp.sum(spread, axis=1, keepdims=True).astype(BF)
        kept[:, 4032 + i : 4033 + i] = column
        given[:, 4032 + i : 4033 + i] = column
    rows = out[...].astype(F32)
    spare = jnp.zeros((9, 128), F32)
    rows = jnp.concatenate(
        [rows[:, :640], jnp.concatenate([rows[:, 640:], spare], axis=1)], axis=0
    )
    traded[:, :640] = rows.astype(BF)
    traded[:, 640:] = folded(down[...].astype(F32)).astype(BF)


def halves(*args):
    return pl.pallas_call(
        halves_kernel,
        out_shape=[shaped(9, 4034, BF), shaped(9, 4034, BF), shaped(18, 2176, BF)],
        in_specs=[SMEM] + [VMEM] * 9,
        compiler_params=params(8),
    )(*args)


def whole_kernel(core, mine, theirs, traded, gate, up, query, key, value, out, down, gains):
    first = core[0] == 0
    own, other = mine[...], theirs[...].astype(F32)
    low, high = jnp.where(first, own, other), jnp.where(first, other, own)
    for (at, n), to in zip(CUTS, (gate, up, query, key, value)):
        to[:, :n] = low[:, at : at + n]
        to[:, n:] = high[:, at : at + n]
    rows = traded[...].astype(F32)
    out[:, :640] = rows[:9, :640]
    out[:, 640:] = rows[9:, :512]
    down[...] = unfolded(rows[:, 640:])
    same = lax.broadcasted_iota(jnp.int32, (9, 9), 0) == lax.broadcasted_iota(jnp.int32, (9, 9), 1)
    for i in range(2):
        column = low[:, 4032 + i : 4033 + i] + high[:, 4032 + i : 4033 + i]
        spread = jnp.where(same, jnp.broadcast_to(column, (9, 9)), 0.0)
        gains[i : i + 1, :] = jnp.sum(spread, axis=0, keepdims=True)


def whole(*args):
    outs = [shaped(9, 2 * n, F32) for _, n in CUTS]
    return pl.pallas_call(
        whole_kernel,
        out_shape=[*outs, shaped(9, D, F32), shaped(24, D, F32), shaped(2, 9, F32)],
        in_specs=[SMEM] + [VMEM] * 3,
        compiler_params=params(8),
    )(*args)


def heads_kernel(
    tok_own, tok_other, w, source, to_left, to_right, cos, sin,
    normed_p, turned, k_lo, k_hi, v_lo, v_hi, w_o, gains, gathered, pre, perm, left, right,
):
    fill(perm, source)
    fill(left, to_left)
    fill(right, to_right)
    gathered[...] = dot(perm[...], w[:, 896:1024]).T
    gains[...] = gathered[64:72, :]
    for b, tok in enumerate((tok_own, tok_other)):
        rows = slice(b * TOK, b * TOK + TOK)
        x = tok[...].astype(F32)
        r1 = lax.rsqrt(jnp.mean(x * x, axis=1, keepdims=True) + EPS)
        normed = (x * r1 * gains[0:1, :]).astype(BF)
        normed_p[rows, :] = dot(normed, perm[...]).astype(BF)
    w_o[:, :640] = dot(left[...], w[:, 1024:1664]).astype(BF)
    w_o[:, 640:] = dot(right[...], w[:, 1024:1536]).astype(BF)

    def one_row(b, carry):
        rows = pl.ds(pl.multiple_of(b * TOK, TOK), TOK)
        pre[...] = dot(normed_p[rows, :], w[:, :1024])
        for j in range(6):
            lanes = slice(128 * j, 128 * j + 128)
            turned[rows, lanes] = turn(pre[:, lanes], cos[rows, :], sin[rows, :]).astype(BF)
        low = low_lanes((TOK, 128))
        zero = jnp.zeros((TOK, 128), F32)

        def both(value, half, to_low, to_high, kv):
            value = jnp.where(low if half == 0 else ~low, value, zero)
            moved = pltpu.roll(value, 64, 1)
            pair = (value, moved) if half == 0 else (moved, value)
            lanes = slice(128 * kv, 128 * kv + 128)
            to_low[rows, lanes], to_high[rows, lanes] = pair[0].astype(BF), pair[1].astype(BF)

        for kv, (j, half) in enumerate(((4, 1), (5, 0), (5, 1))):
            lanes = slice(128 * j, 128 * j + 128)
            both(turned[rows, lanes].astype(F32), half, k_lo, k_hi, kv)
        for kv, (j, half) in enumerate(((6, 0), (6, 1), (7, 0))):
            both(pre[:, 128 * j : 128 * j + 128], half, v_lo, v_hi, kv)
        return carry

    lax.fori_loop(0, 2, one_row, 0)


def attention_heads(*args):
    outs = [
        shaped(512, DP, BF), shaped(512, 768, BF), *[shaped(512, 384, BF)] * 4, shaped(640, D, BF),
        shaped(8, D, F32),
    ]
    return pl.pallas_call(
        heads_kernel,
        out_shape=outs,
        scratch_shapes=[
            pltpu.VMEM((128, D), F32), pltpu.VMEM((TOK, 1024), F32), pltpu.VMEM((D, DP), BF),
            *[pltpu.VMEM((640, DP), BF)] * 2,
        ],
        compiler_params=params(32),
        cost_estimate=cost(5 * 10**9, [*args, *outs]),
    )(*args)


def attention_kernel(
    turned, k_lo, k_hi, v_lo, v_hi, w_o, bias, probs, mixed, part, part_low
):
    def one_row(b, carry):
        rows = pl.ds(pl.multiple_of(b * TOK, TOK), TOK)
        for j in range(5):
            lanes = slice(128 * j, 128 * j + 128)
            total = None
            for h in (2 * j, 2 * j + 1):
                if h == 9:
                    continue
                kv = slice(128 * (h // 3), 128 * (h // 3) + 128)
                k_ref, v_ref = (k_lo, v_lo) if h % 2 == 0 else (k_hi, v_hi)
                s = dot_t(turned[rows, lanes], k_ref[rows, kv]) * HEAD ** (-0.5) + bias[rows, :]
                e = jnp.exp(s - jnp.max(s, axis=1, keepdims=True))
                p = (e * (1.0 / jnp.sum(e, axis=1, keepdims=True))).astype(BF)
                probs[h, rows, :] = p
                got = dot(p, v_ref[rows, kv])
                total = got if total is None else total + got
            mixed[rows, lanes] = total.astype(BF)
        for n in range(3):
            lanes = slice(384 * n, 384 * n + 384)
            got = dot(mixed[rows, :], w_o[:, lanes])
            part[rows, lanes] = got
            part_low[rows, lanes] = got.astype(BF)
        return carry

    lax.fori_loop(0, 2, one_row, 0)


def attention_forward(*args):
    outs = [
        jax.ShapeDtypeStruct((9, 512, 256), BF), shaped(512, 640, BF), shaped(512, D, F32),
        shaped(512, D, BF),
    ]
    return pl.pallas_call(
        attention_kernel,
        out_shape=outs,
        compiler_params=params(20),
        cost_estimate=cost(3 * 10**9, [*args, *outs]),
    )(*args)


class Moves:
    def __init__(self, sems):
        self.sems, self.count, self.open = sems, 0, {}

    def start(self, name, source, to):
        copy = pltpu.make_async_copy(source, to, self.sems.at[self.count])
        copy.start()
        self.count += 1
        self.open.setdefault(name, []).append(copy)

    def wait(self, *names):
        for name in names or tuple(self.open):
            for copy in self.open.pop(name):
                copy.wait()


def middle_kernel(
    gains, rows_a, rows_b, tok_own, tok_other, part, other,
    middle_out, n2_a_out, n2_b_out, two_at_out, two_bt_out,
    tok, middle, near, perm_a, perm_b, n2, n2_a, n2_b, two_at, two_bt, sems,
):
    moves = Moves(sems)
    moves.start("rows", tok_own, tok.at[pl.ds(0, TOK), :])
    moves.start("rows", tok_other, tok.at[pl.ds(TOK, TOK), :])
    moves.start("rows", part, middle)
    moves.start("rows", other, near)
    fill(perm_a, rows_a)
    fill(perm_b, rows_b)
    moves.wait("rows")
    for b in range(2):
        rows, swapped = slice(b * TOK, b * TOK + TOK), slice((1 - b) * TOK, (2 - b) * TOK)
        value = tok[rows, :].astype(F32) + middle[rows, :] + near[swapped, :].astype(F32)
        middle[rows, :] = value
        r2 = lax.rsqrt(jnp.mean(value * value, axis=1, keepdims=True) + EPS)
        n2[rows, :] = (value * r2 * gains[1:2, :]).astype(BF)
    moves.start("out", middle, middle_out)
    for perm, to, across, to_out, across_out in (
        (perm_a, n2_a, two_at, n2_a_out, two_at_out),
        (perm_b, n2_b, two_bt, n2_b_out, two_bt_out),
    ):
        for n in range(3):
            lanes = slice(384 * n, 384 * n + 384)
            to[:, lanes] = dot(n2[...], perm[:, lanes]).astype(BF)
        moves.start("out", to, to_out)
        across[...] = to[...].T
        moves.start("out", across, across_out)
    moves.wait()


def middle_rows(*args):
    outs = [shaped(512, D, F32), *[shaped(512, D, BF)] * 2, *[shaped(D, 512, BF)] * 2]
    return pl.pallas_call(
        middle_kernel,
        out_shape=outs,
        in_specs=[VMEM] * 3 + [FAR] * 4,
        out_specs=[FAR] * 5,
        scratch_shapes=[
            pltpu.VMEM((512, D), BF), pltpu.VMEM((512, D), F32), pltpu.VMEM((512, D), BF),
            *[pltpu.VMEM((D, D), BF)] * 2, *[pltpu.VMEM((512, D), BF)] * 3,
            *[pltpu.VMEM((D, 512), BF)] * 2, pltpu.SemaphoreType.DMA((12,)),
        ],
        compiler_params=params(60),
        cost_estimate=cost(3 * 10**9, [*args, *outs]),
    )(*args)


def feed_kernel(n2_a_in, n2_b_in, two_at_in, two_bt_in, cot_own, cot_other, *refs):
    blocks, wd_in, kept, grads = refs[:8], refs[8], refs[9:12], refs[12:19]
    (
        n2_a, n2_b, two_at, two_bt, cot, wg, wu, wd, act, d_gate, d_up, wide, tall, sems,
        chunk_sems, grad_sems,
    ) = refs[19:]
    moves = Moves(sems)
    moves.start("rows", n2_a_in, n2_a)
    moves.start("rows", n2_b_in, n2_b)
    moves.start("rows", cot_own, cot.at[pl.ds(0, TOK), :])
    moves.start("rows", cot_other, cot.at[pl.ds(TOK, TOK), :])

    def weight_copies(i):
        lanes = pl.ds(pl.multiple_of(i * 256, 256), 256)
        pairs = [
            (blocks[4 * k + s].at[:, lanes], to.at[pl.ds(288 * s, 288), lanes])
            for s in range(4)
            for k, to in enumerate((wg, wu))
        ]
        pairs.append((wd_in.at[lanes, :], wd.at[lanes, :]))
        return [pltpu.make_async_copy(a, b, chunk_sems.at[i, j]) for j, (a, b) in enumerate(pairs)]

    for i in range(3):
        for c in weight_copies(i):
            c.start()
    moves.wait("rows")

    def grad_copies(k, i):
        lanes = pl.ds(pl.multiple_of(i * 256, 256), 256)
        slot = lax.rem(i, 2)
        return [
            pltpu.make_async_copy(
                wide.at[k, slot, pl.ds(288 * s, 288), :], grads[3 * k + s].at[:, lanes],
                grad_sems.at[k, slot, s],
            )
            for s in range(3)
        ]

    def columns(i, carry):
        lanes = pl.ds(pl.multiple_of(i * 256, 256), 256)
        for c in weight_copies(i):
            c.wait()

        @pl.when(i < 3)
        def _():
            for c in weight_copies(i + 3):
                c.start()

        gate, up = dot(n2_a[...], wg[:, lanes]), dot(n2_b[...], wu[:, lanes])
        d_act = dot_t(cot[...], wd[lanes, :])
        sig = 1.0 / (1.0 + jnp.exp(-gate))
        swish = gate * sig
        act[:, lanes] = (swish * up).astype(BF)
        d_up[:, lanes] = (d_act * swish).astype(BF)
        d_gate[:, lanes] = (d_act * up * sig * (1.0 + gate * (1.0 - sig))).astype(BF)
        return carry

    def grad_columns(i, carry):
        lanes = pl.ds(pl.multiple_of(i * 256, 256), 256)

        @pl.when(i >= 2)
        def _():
            for k in range(2):
                for c in grad_copies(k, i - 2):
                    c.wait()

        slot = lax.rem(i, 2)
        wide[0, slot] = dot(two_at[...], d_gate[:, lanes]).astype(BF)
        wide[1, slot] = dot(two_bt[...], d_up[:, lanes]).astype(BF)
        for k in range(2):
            for c in grad_copies(k, i):
                c.start()
        return carry

    lax.fori_loop(0, 4, columns, 0)
    moves.start("across", two_at_in.at[pl.ds(288, 864), :], two_at)
    moves.start("across", two_bt_in.at[pl.ds(288, 864), :], two_bt)
    lax.fori_loop(4, 6, columns, 0)
    for to, value in zip(kept, (act, d_gate, d_up)):
        moves.start("kept", value, to)
    moves.wait("across")
    lax.fori_loop(0, 6, grad_columns, 0)
    for n in range(4):
        rows = slice(384 * n, 384 * n + 384)
        tall[rows, :] = t_dot(act[:, rows], cot[...]).astype(BF)
        moves.start("down", tall.at[pl.ds(384 * n, 384), :], grads[6].at[pl.ds(384 * n, 384), :])
    for i in (4, 5):
        for k in range(2):
            for c in grad_copies(k, i):
                c.wait()
    moves.wait()


def feed_forward(*args):
    outs = [*[shaped(512, 1536, BF)] * 3, *[shaped(288, 1536, BF)] * 6, shaped(1536, D, BF)]
    return pl.pallas_call(
        feed_kernel,
        out_shape=outs,
        in_specs=[FAR] * 15,
        out_specs=[FAR] * 10,
        scratch_shapes=[
            *[pltpu.VMEM((512, D), BF)] * 2, *[pltpu.VMEM((864, 512), BF)] * 2,
            pltpu.VMEM((512, D), BF), pltpu.VMEM((D, 1536), BF), pltpu.VMEM((D, 1536), BF),
            pltpu.VMEM((1536, D), BF), *[pltpu.VMEM((512, 1536), BF)] * 3,
            pltpu.VMEM((2, 2, 864, 256), BF), pltpu.VMEM((1536, D), BF),
            pltpu.SemaphoreType.DMA((20,)), pltpu.SemaphoreType.DMA((6, 9)),
            pltpu.SemaphoreType.DMA((2, 2, 3)),
        ],
        compiler_params=params(60),
        cost_estimate=cost(10 * 10**9, [*args, *outs]),
    )(*args)


def feed_back_kernel(rows_a, rows_b, middle_in, d_gate_in, d_up_in, *refs):
    blocks, mlp_row, d_two_out = refs[:8], refs[8], refs[9]
    middle, d_gate, d_up, wg, wu, perm_a, perm_b, d_a, d_b, d_two, sems = refs[10:]
    moves = Moves(sems)
    moves.start("gate", d_gate_in, d_gate)
    for s in range(4):
        moves.start("gate", blocks[s], wg.at[pl.ds(288 * s, 288), :])
    moves.start("up", d_up_in, d_up)
    for s in range(4):
        moves.start("up", blocks[4 + s], wu.at[pl.ds(288 * s, 288), :])
    fill(perm_a, rows_a)
    fill(perm_b, rows_b)

    def times(left, right, to):
        def columns(i, carry):
            lanes = pl.ds(pl.multiple_of(i * 384, 384), 384)
            to[:, lanes] = dot_t(left[...], right[lanes, :]).astype(BF)
            return carry

        lax.fori_loop(0, 3, columns, 0)

    moves.wait("gate")
    moves.start("middle", middle_in, middle)
    times(d_gate, wg, d_a)
    moves.wait("up")
    times(d_up, wu, d_b)
    moves.wait("middle")
    value = middle[...]
    r2 = lax.rsqrt(jnp.mean(value * value, axis=1, keepdims=True) + EPS)

    def unmix(i, carry):
        lanes = pl.ds(pl.multiple_of(i * 384, 384), 384)
        got = dot_t(d_a[...], perm_a[lanes, :]) + dot_t(d_b[...], perm_b[lanes, :])
        d_two[:, lanes] = got.astype(BF)
        total = jnp.sum(got * middle[:, lanes] * r2, axis=0, keepdims=True)
        mlp_row[:, lanes] = jnp.broadcast_to(total, (8, 384))
        return carry

    lax.fori_loop(0, 3, unmix, 0)
    moves.start("two", d_two, d_two_out)
    moves.wait()


def feed_back(*args):
    outs = [shaped(8, D, F32), shaped(512, D, BF)]
    return pl.pallas_call(
        feed_back_kernel,
        out_shape=outs,
        in_specs=[VMEM] * 2 + [FAR] * 11,
        out_specs=[VMEM, FAR],
        scratch_shapes=[
            pltpu.VMEM((512, D), F32), *[pltpu.VMEM((512, 1536), BF)] * 2,
            pltpu.VMEM((D, 1536), BF), pltpu.VMEM((D, 1536), BF),
            *[pltpu.VMEM((D, D), BF)] * 2, *[pltpu.VMEM((512, D), BF)] * 3,
            pltpu.SemaphoreType.DMA((16,)),
        ],
        compiler_params=params(60),
        cost_estimate=cost(7 * 10**9, [*args, *outs]),
    )(*args)


def feed_out_kernel(middle_in, act_in, wd_in, out_own, out_send, middle, act, wd, own, low, sems):
    moves = Moves(sems)
    moves.start("in", act_in, act)
    moves.start("in", wd_in, wd)
    moves.start("in", middle_in.at[pl.ds(0, TOK), :], middle)
    moves.wait("in")

    def columns(i, carry):
        lanes = pl.ds(pl.multiple_of(i * 384, 384), 384)
        got = dot(act[...], wd[:, lanes])
        own[:, lanes] = middle[:, lanes] + got[:TOK]
        low[:, lanes] = got[TOK:].astype(BF)
        return carry

    lax.fori_loop(0, 3, columns, 0)
    moves.start("out", own, out_own)
    moves.start("out", low, out_send)
    moves.wait()


def feed_out(*args):
    outs = [shaped(TOK, D, F32), shaped(TOK, D, BF)]
    return pl.pallas_call(
        feed_out_kernel,
        out_shape=outs,
        in_specs=[FAR] * 3,
        out_specs=[FAR] * 2,
        scratch_shapes=[
            pltpu.VMEM((TOK, D), F32), pltpu.VMEM((512, 1536), BF), pltpu.VMEM((1536, D), BF),
            pltpu.VMEM((TOK, D), F32), pltpu.VMEM((TOK, D), BF), pltpu.SemaphoreType.DMA((8,)),
        ],
        compiler_params=params(60),
        cost_estimate=cost(2 * 10**9, [*args, *outs]),
    )(*args)


def grads_kernel(s, *refs):
    ins, outs = refs[:4], refs[4:6]
    two_a, two_b, d_gate, d_up, wide, sems = refs[6:]
    moves = Moves(sems)
    moves.start("a", ins[0].at[pl.ds(288 * s, 288), :], two_a)
    moves.start("a", ins[2], d_gate)
    moves.start("b", ins[1].at[pl.ds(288 * s, 288), :], two_b)
    moves.start("b", ins[3], d_up)
    for k, (name, left, right) in enumerate((("a", two_a, d_gate), ("b", two_b, d_up))):
        moves.wait(name)
        wide[k] = dot(left[...], right[...]).astype(BF)
        moves.start("out", wide.at[k], outs[k])
    moves.wait()


def feed_grads(s, *args):
    outs = [shaped(288, 1536, BF)] * 2
    return pl.pallas_call(
        functools.partial(grads_kernel, s),
        out_shape=outs,
        in_specs=[FAR] * 4,
        out_specs=[FAR] * 2,
        scratch_shapes=[
            *[pltpu.VMEM((288, 512), BF)] * 2, *[pltpu.VMEM((512, 1536), BF)] * 2,
            pltpu.VMEM((2, 288, 1536), BF), pltpu.SemaphoreType.DMA((12,)),
        ],
        compiler_params=params(60),
        cost_estimate=cost(9 * 10**8, [*args, *outs]),
    )(*args)


def add_kernel(*refs):
    n = len(refs) // 3
    for a, b, out in zip(refs[:n], refs[n : 2 * n], refs[2 * n :]):
        out[...] = (a[...].astype(F32) + b[...].astype(F32)).astype(BF)


def added(parts, arrived):
    blocks = [pl.BlockSpec((p.shape[0], p.shape[1] // 3), lambda i: (0, i)) for p in parts]
    return pl.pallas_call(
        add_kernel,
        grid=(3,),
        out_shape=[shaped(*p.shape, BF) for p in parts],
        in_specs=blocks * 2,
        out_specs=blocks,
        compiler_params=params(12),
        cost_estimate=cost(10**6, [*parts, *arrived, *parts]),
    )(*parts, *arrived)


def attention_back_kernel(
    gains, mlp_row, source, to_left, to_right, middle_in, d_two_in, other_in, cot_own, cot_other,
    w_o_in, probs_in, *refs
):
    turned_in, kv_in, cos_in, sin_in = refs[0], refs[1:5], refs[5], refs[6]
    tok_own, tok_other, w_in, normed_in, mixed_in = refs[7:12]
    d_middle_out, part_own_out, part_send_out, sent_grads = refs[12:16]
    (
        middle, d_two, other, cot, w_o, probs, turned, k_lo, k_hi, v_lo, v_hi, cos, sin,
        d_middle, d_branch, d_mixed, d_pre, d_qkv,
        tok, w, perm, left, right, normed_p, mixed, grads, part_own, part_send, d_p, g_out,
        rows_of_gains, sems,
    ) = refs[16:]
    moves = Moves(sems)
    moves.start("rows", middle_in, middle)
    moves.start("rows", d_two_in, d_two)
    moves.start("rows", other_in, other)
    moves.start("rows", cot_own, cot.at[pl.ds(0, TOK), :])
    moves.start("rows", cot_other, cot.at[pl.ds(TOK, TOK), :])
    moves.start("w_o", w_o_in, w_o)
    fill(perm, source)
    fill(left, to_left)
    fill(right, to_right)
    moves.wait("rows")
    for far, to in zip((turned_in, *kv_in, cos_in, sin_in, probs_in),
                       (turned, k_lo, k_hi, v_lo, v_hi, cos, sin, probs)):
        moves.start("heads", far, to)
    for b in range(2):
        rows, swapped = slice(b * TOK, b * TOK + TOK), slice((1 - b) * TOK, (2 - b) * TOK)
        value = middle[rows, :]
        r2 = lax.rsqrt(jnp.mean(value * value, axis=1, keepdims=True) + EPS)
        e2 = gains[1:2, :] * (d_two[rows, :].astype(F32) + other[swapped, :].astype(F32))
        got = cot[rows, :].astype(F32) + r2 * (
            e2 - value * (r2 * r2 * jnp.mean(value * e2, axis=1, keepdims=True))
        )
        if b == 0:
            d_middle[...] = got
            moves.start("out", d_middle, d_middle_out)
        d_branch[rows, :] = got.astype(BF)
    moves.wait("w_o")
    d_mixed[...] = dot_t(d_branch[...], w_o[...]).astype(BF)
    moves.wait("heads")
    moves.start("normed", normed_in, normed_p)
    moves.start("mixed", mixed_in, mixed)
    moves.start("back", w_in.at[:, pl.ds(0, 1024)], w)
    moves.start("back", tok_own, tok.at[pl.ds(0, TOK), :])
    moves.start("back", tok_other, tok.at[pl.ds(TOK, TOK), :])

    def one_row(b, carry):
        rows = pl.ds(pl.multiple_of(b * TOK, TOK), TOK)
        d_k = {}
        d_v = {}
        for j in range(5):
            lanes = slice(128 * j, 128 * j + 128)
            q_pair, d_pair = turned[rows, lanes], d_mixed[rows, lanes]
            total = None
            for h in (2 * j, 2 * j + 1):
                if h == 9:
                    continue
                kv, half = h // 3, h % 2
                at_kv = slice(128 * kv, 128 * kv + 128)
                k_ref, v_ref = (k_lo, v_lo) if half == 0 else (k_hi, v_hi)
                p = probs[h, rows, :]
                p32 = p.astype(F32)
                d_probs = dot_t(d_pair, v_ref[rows, at_kv])
                row_dot = jnp.sum(p32 * d_probs, axis=1, keepdims=True)
                d_raw = (p32 * (d_probs - row_dot) * HEAD ** (-0.5)).astype(BF)
                got = dot(d_raw, k_ref[rows, at_kv])
                total = got if total is None else total + got
                for sums, value in ((d_k, t_dot(d_raw, q_pair)), (d_v, t_dot(p, d_pair))):
                    sums[kv, half] = value if (kv, half) not in sums else sums[kv, half] + value
            d_pre[:, lanes] = total
        low = low_lanes((TOK, 128))

        def collected(sums, kv, half):
            return sums[kv, half] + pltpu.roll(sums[kv, 1 - half], 64, 1)

        d_pre[:, 512:640] = jnp.where(low, d_pre[:, 512:640], collected(d_k, 0, 1))
        d_pre[:, 640:768] = jnp.where(low, collected(d_k, 1, 0), collected(d_k, 2, 1))
        for j in range(6):
            lanes = slice(128 * j, 128 * j + 128)
            d_qkv[rows, lanes] = turn(d_pre[:, lanes], cos[rows, :], -sin[rows, :]).astype(BF)
        d_qkv[rows, 768:896] = jnp.where(low, collected(d_v, 0, 0), collected(d_v, 1, 1)).astype(BF)
        d_qkv[rows, 896:1024] = jnp.where(low, collected(d_v, 2, 0), 0.0).astype(BF)
        return carry

    lax.fori_loop(0, 2, one_row, 0)
    moves.wait("normed")

    def qkv_grads(i, carry):
        lanes = pl.ds(pl.multiple_of(i * 256, 256), 256)
        grads[:, lanes] = t_dot(normed_p[...], d_qkv[:, lanes]).astype(BF)
        return carry

    lax.fori_loop(0, 4, qkv_grads, 0)
    moves.wait("mixed")
    g_out[...] = t_dot(mixed[...], d_branch[...]).astype(BF)
    grads[:, 1024:1536] = (
        t_dot(left[...], g_out[:, :512]) + t_dot(right[...], g_out[:, 640:])
    ).astype(BF)
    grads[:, 1536:] = t_dot(left[...], g_out[:, 512:640]).astype(BF)
    moves.wait("back")
    total = jnp.zeros((1, D), F32)
    for b in range(2):
        rows = slice(b * TOK, b * TOK + TOK)
        d_p[...] = dot_t(d_qkv[rows, :], w[...]).astype(BF)
        x = tok[rows, :].astype(F32)
        r1 = lax.rsqrt(jnp.mean(x * x, axis=1, keepdims=True) + EPS)
        got = dot_t(d_p[...], perm[...])
        total = total + jnp.sum(got * x * r1, axis=0, keepdims=True)
        if b == 0:
            part_own[...] = got
            moves.start("part", part_own, part_own_out)
        else:
            part_send[...] = got.astype(BF)
            moves.start("part", part_send, part_send_out)
    which = lax.broadcasted_iota(jnp.int32, (128, D), 0)
    rows_of_gains[...] = jnp.where(
        which == 64, total, jnp.where(which == 65, mlp_row[0:1, :], 0.0)
    ).astype(BF)
    gain_columns = dot(rows_of_gains[...], perm[...]).T
    grads[:, 896:1024] = (grads[:, 896:1024].astype(F32) + gain_columns).astype(BF)
    moves.start("grads", grads, sent_grads)
    moves.wait()


def attention_back(*args):
    outs = [shaped(TOK, D, F32), shaped(TOK, D, F32), shaped(TOK, D, BF), shaped(DP, 1664, BF)]
    return pl.pallas_call(
        attention_back_kernel,
        out_shape=outs,
        in_specs=[VMEM] * 5 + [FAR] * (len(args) - 5),
        out_specs=[FAR] * 4,
        scratch_shapes=[
            pltpu.VMEM((512, D), F32), *[pltpu.VMEM((512, D), BF)] * 3, pltpu.VMEM((640, D), BF),
            pltpu.VMEM((9, 512, 256), BF), pltpu.VMEM((512, 768), BF),
            *[pltpu.VMEM((512, 384), BF)] * 4, *[pltpu.VMEM((512, 128), F32)] * 2,
            pltpu.VMEM((TOK, D), F32), pltpu.VMEM((512, D), BF), pltpu.VMEM((512, 640), BF),
            pltpu.VMEM((TOK, 768), F32), pltpu.VMEM((512, 1024), BF),
            pltpu.VMEM((512, D), BF), pltpu.VMEM((DP, 1024), BF), pltpu.VMEM((D, DP), BF),
            *[pltpu.VMEM((640, DP), BF)] * 2, pltpu.VMEM((512, DP), BF), pltpu.VMEM((512, 640), BF),
            pltpu.VMEM((DP, 1664), BF), pltpu.VMEM((TOK, D), F32), pltpu.VMEM((TOK, D), BF),
            pltpu.VMEM((TOK, DP), BF), pltpu.VMEM((640, D), BF), pltpu.VMEM((128, D), BF),
            pltpu.SemaphoreType.DMA((40,)),
        ],
        compiler_params=params(60),
        cost_estimate=cost(10 * 10**9, [*args, *outs]),
    )(*args)


class Lockstep:
    def __init__(self):
        self.last = ()

    def tie(self, *values):
        tied = lax.optimization_barrier((*values, *self.last))
        self.last = tied
        return tied[: len(values)]

    def after(self, *values):
        self.last = (*self.last, *values)

    def __call__(self, values, pairs, late=(), late_pairs=(), beside=tuple):
        tied = lax.optimization_barrier((*values, *self.last))
        sent = [send(v, p) for v, p in zip(tied, pairs)]
        sent += [send(v, p) for v, p in zip(late, late_pairs)]
        sent += beside()
        self.last = lax.optimization_barrier(tuple(sent))
        return list(self.last)

    def gather(self, blocks, axes, more=(), more_pairs=()):
        values = [b for b in blocks for _ in range(3)]
        pairs = [STRAIGHT[a][n] for a in axes for n in (1, 2, 3)]
        got = self([*values, *more], [*pairs, *more_pairs])
        rings = [[b, *got[3 * i : 3 * i + 3]] for i, b in enumerate(blocks)]
        return rings, got[3 * len(blocks) :]

    def scatter(self, makers, axes, table, late=(), late_pairs=()):
        values = [make(s).astype(BF) for make in makers for s in (1, 2, 3)]
        pairs = [table[a][4 - s] for a in axes for s in (1, 2, 3)]
        got = self(values, pairs, late, late_pairs)
        sums = [
            sum([g.astype(F32) for g in got[3 * i : 3 * i + 3]], make(0).astype(F32))
            for i, make in enumerate(makers)
        ]
        return sums, got[3 * len(makers) :]


def place(blocks, at, sign):
    out = jnp.zeros((4, *blocks[0].shape), blocks[0].dtype)
    for step, block in enumerate(blocks):
        out = lax.dynamic_update_index_in_dim(out, block, (at - sign * step) % 4, 0)
    return out


def row_tables(segment_row):
    places = jnp.arange(TOK, dtype=jnp.int32)
    same_doc = segment_row[:, None] == segment_row[None, :]
    starts = jnp.min(jnp.where(same_doc, places[None, :], TOK), axis=1)
    offsets = (places - starts).astype(F32)
    lane = jnp.arange(128, dtype=jnp.int32)
    frequency = jnp.exp((lane % 32).astype(F32) * (-2.0 * math.log(THETA) / HEAD))
    angles = offsets[:, None] * frequency[None, :]
    side = jnp.where(lane % 64 < 32, -1.0, 1.0)
    allowed = same_doc & (places[:, None] >= places[None, :])
    return jnp.cos(angles), jnp.sin(angles) * side, jnp.where(allowed, 0.0, -1e30).astype(F32)


def body(
    tokens, segments, attn_gain, w_query, w_key, w_value, w_out, mlp_gain, w_gate, w_up, w_down,
    cotangent,
):
    core = lax.axis_index("core")
    at = {
        "x": lax.axis_index("x"),
        "y": lax.axis_index("y"),
        "z": lax.axis_index("z_hi") * 2 + lax.axis_index("z_lo"),
    }
    sign = 1 - 2 * core
    first = core == 0

    which = jnp.reshape(core, (1,)).astype(jnp.int32)
    kept, given, traded = halves(
        which, w_gate, w_up, w_query, w_key, w_value, attn_gain.reshape(1, 9),
        mlp_gain.reshape(1, 9), w_out, w_down,
    )
    step = Lockstep()
    given, traded = step([given, traded], [CORES, TRADE])
    rows = jnp.concatenate([jnp.where(first, kept, given), jnp.where(first, given, kept)], axis=0)


    order_a, order_b, order_c = ("x", "z", "y"), ("y", "x", "z"), ("z", "y", "x")

    def natural(order):
        k = jnp.arange(D, dtype=jnp.int32)
        r, t = k % 18, k // 18
        c = {}
        for level, axis in enumerate(order):
            c[axis] = (at[axis] - (sign if level > 0 else 1) * ((t // 4**level) % 4)) % 4
        chip = (((c["z"] // 2) * 4 + c["x"]) * 2 + c["z"] % 2) * 4 + c["y"]
        return chip * 18 + r

    one, two, three = zip(order_a, order_b, order_c)
    z_rows = jnp.concatenate([rows[:, 3072:], jnp.zeros((18, 62), BF), traded], axis=1)
    got = step([z_rows] * 3, [STRAIGHT["z"][n] for n in (1, 2, 3)])
    z_at = jnp.reshape(at["z"], (1,)).astype(jnp.int32)
    w_attn, down = spread(z_at, z_rows, *got)
    w_attn = lax.all_gather(
        w_attn, AXES, axis=0, tiled=True, axis_index_groups=LINES["y", "x"]
    )
    (ha, hb), _ = step.gather([rows[:, :1536], rows[:, 1536:3072]], one[:2])
    rows_a, rows_b = natural(order_a), natural(order_b)

    k = jnp.arange(DP, dtype=jnp.int32)
    outer, inner, r, s = k // 320, (k // 80) % 4, (k % 80) % 18, (k % 80) // 18
    x_at, y_at = jnp.where(first, outer, inner), jnp.where(first, inner, outer)
    z = (at["z"] - s) % 4
    source = (((z // 2 * 4 + x_at) * 2 + z % 2) * 4 + y_at) * 18 + r
    source = jnp.where(s < 4, source, -1)
    e = ((x_at * 2 + z % 2) * 4 + y_at) * 2 + z // 2
    to_left = jnp.where((r < 9) & (s < 4), e * 9 + r, -1)
    to_right = jnp.where((r >= 9) & (s < 4), e * 9 + r - 9, -1)
    rows_a, rows_b, source = (i[None, :] for i in (rows_a, rows_b, source))
    ring = [RINGS[a] for a in two]
    held = [[stack_rows(ha), stack_rows(hb), down.reshape(96, D)]]
    *arrived, tok_other, seg_other = step(
        [*held[-1], tokens, segments.astype(F32)], [*ring, CORES, CORES]
    )
    held.append(arrived)
    (w_attn,) = step.tie(w_attn)
    w_attn = lax.all_gather(
        w_attn, AXES, axis=0, tiled=True, axis_index_groups=LINES["x", "y"]
    )
    *arrived, cot_other = step([*held[-1], cotangent], [*ring, CORES])
    held.append(arrived)
    seg_other = seg_other.astype(jnp.int32)
    tables = [row_tables(segments[0]), row_tables(seg_other[0])]
    cos, sin, bias = (jnp.concatenate(t, axis=0) for t in zip(*tables))

    held.append(step(held[-1], ring))
    ha, hb, hc = zip(*held)
    ring = [RINGS[a] for a in three[:2]]
    down = place([h.reshape(2, 48, D) for h in hc], at["y"], sign)
    down = jnp.transpose(down, (1, 0, 2, 3)).reshape(384, D)
    held = [[jnp.concatenate(ha, axis=0), jnp.concatenate(hb, axis=0)]]
    wd = lax.all_gather(down, "x", axis=0, tiled=True)
    held.append(step(held[-1], ring))
    (w_attn,) = step.tie(w_attn)
    normed_p, turned, k_lo, k_hi, v_lo, v_hi, w_o, gains = attention_heads(
        tokens, tok_other, w_attn, source, to_left[None, :], to_right[None, :], cos, sin
    )
    probs, mixed, part, part_low = attention_forward(turned, k_lo, k_hi, v_lo, v_hi, w_o, bias)
    *arrived, part_low = step(held[-1], ring, beside=lambda: (part_low,))
    held.append(arrived)
    rows = middle_rows(gains, rows_a, rows_b, tokens, tok_other, part, swap(part_low))
    *arrived, middle, n2_a, n2_b, two_at, two_bt = step(held[-1], ring, beside=lambda: rows)
    held.append(arrived)
    ha, hb = zip(*held)

    act, d_gate, d_up, *grads = feed_forward(
        n2_a, n2_b, two_at, two_bt, cotangent, cot_other, *ha, *hb, wd
    )
    kept = (two_at, two_bt, d_gate, d_up)
    g_down = lax.psum_scatter(grads[6], "x", scatter_dimension=0, tiled=True)

    mlp_row, d_two = feed_back(rows_a, rows_b, middle, d_gate, d_up, *ha, *hb)
    *arrived, d_two = step([grads[0], grads[3]], ring, beside=lambda: (d_two,))
    sums = added([grads[1], grads[4]], arrived)
    d_middle, part_own, part_send, g_attn = attention_back(
        gains, mlp_row, source, to_left[None, :], to_right[None, :], middle, d_two, swap(d_two),
        cotangent, cot_other, w_o, probs, turned, k_lo, k_hi, v_lo, v_hi, cos, sin, tokens,
        tok_other, w_attn, normed_p, mixed,
    )
    *kept, act, part_send = lax.optimization_barrier((*kept, act, part_send))
    *arrived, part_send, g_attn = step(sums, ring, beside=lambda: (part_send, g_attn))
    sums = added([grads[2], grads[5]], arrived)
    out_own, out_send = feed_out(middle, act, wd)
    *arrived, part_other, out_send = step(
        [*sums, part_send], [*ring, CORES], beside=lambda: (out_send,)
    )
    g_gate, g_up = added(feed_grads(0, *kept), arrived)
    g_attn_x = lax.psum_scatter(
        g_attn, AXES, scatter_dimension=0, tiled=True, axis_index_groups=LINES["x", "y"]
    )
    g_attn = lax.psum_scatter(
        g_attn_x, AXES, scatter_dimension=0, tiled=True, axis_index_groups=LINES["y", "x"]
    )

    d_normed = part_own + part_other.astype(F32)
    x_own = tokens.astype(F32)
    r_own = lax.rsqrt(jnp.mean(x_own * x_own, axis=-1, keepdims=True) + EPS)
    e1 = d_normed * gains[0]
    grad_input = d_middle + r_own * (
        e1 - x_own * r_own * r_own * jnp.mean(x_own * e1, axis=-1, keepdims=True)
    )

    def rows_of(held, n):
        return lambda s: held[n * s : n * s + n]

    def y_block(s):
        down = g_down.reshape(2, 4, 48, D)
        return lax.dynamic_index_in_dim(down, (at["y"] - sign * s) % 4, 1, False).reshape(96, D)

    (g_up,), (out_other,) = step.scatter(
        [rows_of(g_up, 72)], two[1:2], SIGNED, [out_send], [CORES]
    )
    output = (out_own + out_other.astype(F32)).astype(BF)
    step.after(g_attn_x)
    (g_gate, g_down), _ = step.scatter(
        [rows_of(g_gate, 72), y_block], (two[0], two[2]), SIGNED
    )
    own, *packed = pack(z_at, g_attn, g_down.astype(BF).reshape(4, 24, D))
    (g_gate, g_up), got = step.scatter(
        [rows_of(g_gate, 18), rows_of(g_up, 18)], one[:2], STRAIGHT,
        packed, [STRAIGHT["z"][4 - s] for s in (1, 2, 3)],
    )
    g_z = sum([g.astype(F32) for g in got], own.astype(F32))

    g_rows = jnp.concatenate([g_gate, g_up, g_z[:, :962]], axis=1)
    mine = jnp.where(first, g_rows[:9], g_rows[9:])
    theirs = jnp.where(first, g_rows[9:], g_rows[:9]).astype(BF)
    theirs, g_od = step([theirs, g_z[:, 1024:].astype(BF)], [CORES, TRADE])
    g_g, g_u, g_q, g_k, g_v, g_o, g_d, g_gains = whole(which, mine, theirs, g_od)
    return (
        output, grad_input, g_gains[0], g_q, g_k, g_v, g_o, g_gains[1], g_g, g_u, g_d,
    )


def solution(mesh):
    fine = Mesh(mesh.devices.reshape(SHAPE), AXES)
    rows, vector = P(AXES, None), P(AXES)
    return jax.shard_map(
        body,
        mesh=fine,
        in_specs=(rows, rows, vector, rows, rows, rows, rows, vector, rows, rows, rows, rows),
        out_specs=(rows, rows, vector, rows, rows, rows, rows, vector, rows, rows, rows),
        check_vma=False,
    )
```

```python
import functools
import math

import jax
import jax.numpy as jnp
import numpy as np
from jax import lax
from jax.experimental import pallas as pl
from jax.experimental.pallas import tpu as pltpu
from jax.sharding import Mesh
from jax.sharding import PartitionSpec as P

D = 1152
HEADS = 18
KV_HEADS = 6
HEAD = 64
FF = 3072
DP = 1280
TOK = 256
EPS = 1e-05
THETA = 10000.0

SHAPE = (2, 4, 2, 4, 2)
AXES = ("z_hi", "x", "z_lo", "y", "core")
BF = jnp.bfloat16
F32 = jnp.float32


def device_pairs(move):
    pairs = []
    for i in range(128):
        zh, x, zl, y, c = (int(v) for v in np.unravel_index(i, SHAPE))
        x, y, z, c = move(x, y, zh * 2 + zl, c)
        x, y, z = x % 4, y % 4, z % 4
        pairs.append((i, int(np.ravel_multi_index((z // 2, x, z % 2, y, c), SHAPE))))
    return pairs


RINGS = {
    "x": device_pairs(lambda x, y, z, c: (x + 1 - 2 * c, y, z, c)),
    "y": device_pairs(lambda x, y, z, c: (x, y + 1 - 2 * c, z, c)),
    "z": device_pairs(lambda x, y, z, c: (x, y, z + 1 - 2 * c, c)),
}
CORES = device_pairs(lambda x, y, z, c: (x, y, z, 1 - c))
TRADE = device_pairs(lambda x, y, z, c: (x, y, c * 2 + z % 2, z // 2))


def lines(*axes):
    index = np.arange(128).reshape(SHAPE)
    groups = []
    for core, axis in enumerate(axes):
        along = np.moveaxis(index[..., core], AXES.index(axis), -1)
        groups += along.reshape(-1, 4).tolist()
    return groups


LINES = {("x", "y"): lines("x", "y"), ("y", "x"): lines("y", "x")}


def send(value, pairs):
    return lax.ppermute(value, AXES, pairs)


def swap(value):
    return send(value, CORES)


def dot(a, b):
    return jnp.dot(a, b, preferred_element_type=F32)


def dot_t(a, b):
    return lax.dot_general(a, b, (((1,), (1,)), ((), ())), preferred_element_type=F32)


def t_dot(a, b):
    return lax.dot_general(a, b, (((0,), (0,)), ((), ())), preferred_element_type=F32)


def shift(axis, n):
    return device_pairs(lambda x, y, z, c: (
        x + n * (axis == "x"), y + n * (axis == "y"), z + n * (axis == "z"), c))


def signed(axis, n):
    return device_pairs(lambda x, y, z, c: (
        x + n * (1 - 2 * c) * (axis == "x"), y + n * (1 - 2 * c) * (axis == "y"),
        z + n * (1 - 2 * c) * (axis == "z"), c))


SIGNED = {axis: {n: signed(axis, n) for n in (1, 2, 3)} for axis in ("x", "y", "z")}
STRAIGHT = {axis: {n: shift(axis, n) for n in (1, 2, 3)} for axis in ("x", "y", "z")}


def params(mib):
    return pltpu.CompilerParams(vmem_limit_bytes=mib * 2**20)


FAR = pl.BlockSpec(memory_space=pltpu.HBM)
SMEM = pl.BlockSpec(memory_space=pltpu.SMEM)
VMEM = pl.BlockSpec(memory_space=pltpu.VMEM)


def shaped(rows, columns, dtype):
    return jax.ShapeDtypeStruct((rows, columns), dtype)


def cost(flops, arrays):
    return pl.CostEstimate(
        flops=flops,
        bytes_accessed=sum(math.prod(a.shape) * a.dtype.itemsize for a in arrays),
        transcendentals=0,
    )


def low_lanes(shape):
    return lax.broadcasted_iota(jnp.int32, shape, 1) % 128 < 64


def turn(v, cos, sin):
    ahead = lax.broadcasted_iota(jnp.int32, v.shape, 1) % 64 < 32
    return v * cos + jnp.where(ahead, pltpu.roll(v, 96, 1), pltpu.roll(v, 32, 1)) * sin


def fill(to, index):
    def rows_of(i, carry):
        rows = pl.ds(pl.multiple_of(i * 128, 128), 128)
        at = lax.broadcasted_iota(jnp.int32, (128, to.shape[1]), 0) + i * 128
        to[rows, :] = jnp.where(at == index[...], 1.0, 0.0).astype(BF)
        return carry

    lax.fori_loop(0, to.shape[0] // 128, rows_of, 0)


def stack_kernel(*refs):
    *blocks, out = refs
    out[...] = jnp.concatenate([b[...].astype(F32) for b in blocks], axis=0).astype(out.dtype)


def stack_rows(blocks):
    rows = sum(b.shape[0] for b in blocks)
    return pl.pallas_call(
        stack_kernel,
        out_shape=shaped(rows, blocks[0].shape[1], blocks[0].dtype),
        compiler_params=params(8),
    )(*blocks)


CUTS = ((0, 1536), (1536, 1536), (3072, 576), (3648, 192), (3840, 192))


def folded(rows):
    last = jnp.concatenate([rows[18:, 384 * j : 384 * j + 384] for j in range(3)], axis=0)
    return jnp.concatenate([rows[:18], last], axis=1)


def unfolded(rows):
    last = [rows[6 * j : 6 * j + 6, D:] for j in range(3)]
    return jnp.concatenate([rows[:, :D], jnp.concatenate(last, axis=1)], axis=0)


def z_place(at, s):
    z = lax.rem(at[0] - s + 4, 4)
    return lax.rem(z, 2) * 2 + z // 2


def spread_kernel(at, *refs):
    *blocks, attn, down = refs
    rows = [b[...].astype(F32) for b in blocks]
    spare = jnp.zeros((8, 1664), F32)
    attn[...] = jnp.concatenate([*(r[:, :1664] for r in rows), spare], axis=0).astype(BF)
    for s, r in enumerate(rows):
        down[z_place(at, s)] = unfolded(r[:, 1664:]).astype(BF)


def spread(at, *blocks):
    return pl.pallas_call(
        spread_kernel,
        out_shape=[shaped(80, 1664, BF), jax.ShapeDtypeStruct((4, 24, D), BF)],
        in_specs=[SMEM] + [VMEM] * 4,
        compiler_params=params(8),
    )(at, *blocks)


def pack_kernel(at, attn, down, *outs):
    rows = attn[...].astype(F32)
    for s, out in enumerate(outs):
        out[:, :1664] = rows[18 * s : 18 * s + 18].astype(BF)
        out[:, 1664:] = folded(down[z_place(at, s)].astype(F32)).astype(BF)


def pack(*args):
    return pl.pallas_call(
        pack_kernel,
        out_shape=[shaped(18, 3200, BF)] * 4,
        in_specs=[SMEM] + [VMEM] * 2,
        compiler_params=params(8),
    )(*args)


def halves_kernel(core, gate, up, query, key, value, gain_one, gain_two, out, down, kept, given, traded):
    first = core[0] == 0
    for (at, n), w in zip(CUTS, (gate, up, query, key, value)):
        low, high = w[:, :n].astype(F32), w[:, n:].astype(F32)
        kept[:, at : at + n] = jnp.where(first, low, high).astype(BF)
        given[:, at : at + n] = jnp.where(first, high, low).astype(BF)
    row = lax.broadcasted_iota(jnp.int32, (9, 9), 0)
    same = row == lax.broadcasted_iota(jnp.int32, (9, 9), 1)
    for i, gain in enumerate((gain_one, gain_two)):
        spread = jnp.where(same, jnp.broadcast_to(gain[...].astype(F32), (9, 9)), 0.0)
        column = jnp.sum(spread, axis=1, keepdims=True).astype(BF)
        kept[:, 4032 + i : 4033 + i] = column
        given[:, 4032 + i : 4033 + i] = column
    rows = out[...].astype(F32)
    spare = jnp.zeros((9, 128), F32)
    rows = jnp.concatenate(
        [rows[:, :640], jnp.concatenate([rows[:, 640:], spare], axis=1)], axis=0
    )
    traded[:, :640] = rows.astype(BF)
    traded[:, 640:] = folded(down[...].astype(F32)).astype(BF)


def halves(*args):
    return pl.pallas_call(
        halves_kernel,
        out_shape=[shaped(9, 4034, BF), shaped(9, 4034, BF), shaped(18, 2176, BF)],
        in_specs=[SMEM] + [VMEM] * 9,
        compiler_params=params(60),
    )(*args)


def whole_kernel(core, mine, theirs, traded, gate, up, query, key, value, out, down, gains):
    first = core[0] == 0
    own, other = mine[...], theirs[...].astype(F32)
    low, high = jnp.where(first, own, other), jnp.where(first, other, own)
    for (at, n), to in zip(CUTS, (gate, up, query, key, value)):
        to[:, :n] = low[:, at : at + n]
        to[:, n:] = high[:, at : at + n]
    rows = traded[...].astype(F32)
    out[:, :640] = rows[:9, :640]
    out[:, 640:] = rows[9:, :512]
    down[...] = unfolded(rows[:, 640:])
    same = lax.broadcasted_iota(jnp.int32, (9, 9), 0) == lax.broadcasted_iota(jnp.int32, (9, 9), 1)
    for i in range(2):
        column = low[:, 4032 + i : 4033 + i] + high[:, 4032 + i : 4033 + i]
        spread = jnp.where(same, jnp.broadcast_to(column, (9, 9)), 0.0)
        gains[i : i + 1, :] = jnp.sum(spread, axis=0, keepdims=True)


def whole(*args):
    outs = [shaped(9, 2 * n, F32) for _, n in CUTS]
    return pl.pallas_call(
        whole_kernel,
        out_shape=[*outs, shaped(9, D, F32), shaped(24, D, F32), shaped(2, 9, F32)],
        in_specs=[SMEM] + [VMEM] * 3,
        compiler_params=params(8),
    )(*args)


def heads_kernel(
    tok_own, tok_other, w, source, to_left, to_right, cos, sin,
    normed_p, turned, k_lo, k_hi, v_lo, v_hi, w_o, gains, gathered, pre, perm, left, right,
):
    fill(perm, source)
    fill(left, to_left)
    fill(right, to_right)
    gathered[...] = dot(perm[...], w[:, 896:1024]).T
    gains[...] = gathered[64:72, :]
    for b, tok in enumerate((tok_own, tok_other)):
        rows = slice(b * TOK, b * TOK + TOK)
        x = tok[...].astype(F32)
        r1 = lax.rsqrt(jnp.mean(x * x, axis=1, keepdims=True) + EPS)
        normed = (x * r1 * gains[0:1, :]).astype(BF)
        normed_p[rows, :] = dot(normed, perm[...]).astype(BF)
    w_o[:, :640] = dot(left[...], w[:, 1024:1664]).astype(BF)
    w_o[:, 640:] = dot(right[...], w[:, 1024:1536]).astype(BF)

    def one_row(b, carry):
        rows = pl.ds(pl.multiple_of(b * TOK, TOK), TOK)
        pre[...] = dot(normed_p[rows, :], w[:, :1024])
        for j in range(6):
            lanes = slice(128 * j, 128 * j + 128)
            turned[rows, lanes] = turn(pre[:, lanes], cos[rows, :], sin[rows, :]).astype(BF)
        low = low_lanes((TOK, 128))
        zero = jnp.zeros((TOK, 128), F32)

        def both(value, half, to_low, to_high, kv):
            value = jnp.where(low if half == 0 else ~low, value, zero)
            moved = pltpu.roll(value, 64, 1)
            pair = (value, moved) if half == 0 else (moved, value)
            lanes = slice(128 * kv, 128 * kv + 128)
            to_low[rows, lanes], to_high[rows, lanes] = pair[0].astype(BF), pair[1].astype(BF)

        for kv, (j, half) in enumerate(((4, 1), (5, 0), (5, 1))):
            lanes = slice(128 * j, 128 * j + 128)
            both(turned[rows, lanes].astype(F32), half, k_lo, k_hi, kv)
        for kv, (j, half) in enumerate(((6, 0), (6, 1), (7, 0))):
            both(pre[:, 128 * j : 128 * j + 128], half, v_lo, v_hi, kv)
        return carry

    lax.fori_loop(0, 2, one_row, 0)


def attention_heads(*args):
    outs = [
        shaped(512, DP, BF), shaped(512, 768, BF), *[shaped(512, 384, BF)] * 4, shaped(640, D, BF),
        shaped(8, D, F32),
    ]
    return pl.pallas_call(
        heads_kernel,
        out_shape=outs,
        scratch_shapes=[
            pltpu.VMEM((128, D), F32), pltpu.VMEM((TOK, 1024), F32), pltpu.VMEM((D, DP), BF),
            *[pltpu.VMEM((640, DP), BF)] * 2,
        ],
        compiler_params=params(32),
        cost_estimate=cost(5 * 10**9, [*args, *outs]),
    )(*args)


def attention_kernel(
    turned, k_lo, k_hi, v_lo, v_hi, w_o, bias, probs, mixed, part, part_low
):
    def one_row(b, carry):
        rows = pl.ds(pl.multiple_of(b * TOK, TOK), TOK)
        for j in range(5):
            lanes = slice(128 * j, 128 * j + 128)
            total = None
            for h in (2 * j, 2 * j + 1):
                if h == 9:
                    continue
                kv = slice(128 * (h // 3), 128 * (h // 3) + 128)
                k_ref, v_ref = (k_lo, v_lo) if h % 2 == 0 else (k_hi, v_hi)
                s = dot_t(turned[rows, lanes], k_ref[rows, kv]) * HEAD ** (-0.5) + bias[rows, :]
                e = jnp.exp(s - jnp.max(s, axis=1, keepdims=True))
                p = (e * (1.0 / jnp.sum(e, axis=1, keepdims=True))).astype(BF)
                probs[h, rows, :] = p
                got = dot(p, v_ref[rows, kv])
                total = got if total is None else total + got
            mixed[rows, lanes] = total.astype(BF)
        for n in range(3):
            lanes = slice(384 * n, 384 * n + 384)
            got = dot(mixed[rows, :], w_o[:, lanes])
            part[rows, lanes] = got
            part_low[rows, lanes] = got.astype(BF)
        return carry

    lax.fori_loop(0, 2, one_row, 0)


def attention_forward(*args):
    outs = [
        jax.ShapeDtypeStruct((9, 512, 256), BF), shaped(512, 640, BF), shaped(512, D, F32),
        shaped(512, D, BF),
    ]
    return pl.pallas_call(
        attention_kernel,
        out_shape=outs,
        compiler_params=params(20),
        cost_estimate=cost(3 * 10**9, [*args, *outs]),
    )(*args)


class Moves:
    def __init__(self, sems):
        self.sems, self.count, self.open = sems, 0, {}

    def start(self, name, source, to):
        copy = pltpu.make_async_copy(source, to, self.sems.at[self.count])
        copy.start()
        self.count += 1
        self.open.setdefault(name, []).append(copy)

    def wait(self, *names):
        for name in names or tuple(self.open):
            for copy in self.open.pop(name):
                copy.wait()


def middle_kernel(
    gains, rows_a, rows_b, tok_own, tok_other, part, other,
    middle_out, n2_a_out, n2_b_out, two_at_out, two_bt_out,
    tok, middle, near, perm_a, perm_b, n2, n2_a, n2_b, two_at, two_bt, sems,
):
    moves = Moves(sems)
    moves.start("rows", tok_own, tok.at[pl.ds(0, TOK), :])
    moves.start("rows", tok_other, tok.at[pl.ds(TOK, TOK), :])
    moves.start("rows", part, middle)
    moves.start("rows", other, near)
    fill(perm_a, rows_a)
    fill(perm_b, rows_b)
    moves.wait("rows")
    for b in range(2):
        rows, swapped = slice(b * TOK, b * TOK + TOK), slice((1 - b) * TOK, (2 - b) * TOK)
        value = tok[rows, :].astype(F32) + middle[rows, :] + near[swapped, :].astype(F32)
        middle[rows, :] = value
        r2 = lax.rsqrt(jnp.mean(value * value, axis=1, keepdims=True) + EPS)
        n2[rows, :] = (value * r2 * gains[1:2, :]).astype(BF)
    moves.start("out", middle, middle_out)
    for perm, to, across, to_out, across_out in (
        (perm_a, n2_a, two_at, n2_a_out, two_at_out),
        (perm_b, n2_b, two_bt, n2_b_out, two_bt_out),
    ):
        for n in range(3):
            lanes = slice(384 * n, 384 * n + 384)
            to[:, lanes] = dot(n2[...], perm[:, lanes]).astype(BF)
        moves.start("out", to, to_out)
        across[...] = to[...].T
        moves.start("out", across, across_out)
    moves.wait()


def middle_rows(*args):
    outs = [shaped(512, D, F32), *[shaped(512, D, BF)] * 2, *[shaped(D, 512, BF)] * 2]
    return pl.pallas_call(
        middle_kernel,
        out_shape=outs,
        in_specs=[VMEM] * 3 + [FAR] * 4,
        out_specs=[FAR] * 5,
        scratch_shapes=[
            pltpu.VMEM((512, D), BF), pltpu.VMEM((512, D), F32), pltpu.VMEM((512, D), BF),
            *[pltpu.VMEM((D, D), BF)] * 2, *[pltpu.VMEM((512, D), BF)] * 3,
            *[pltpu.VMEM((D, 512), BF)] * 2, pltpu.SemaphoreType.DMA((12,)),
        ],
        compiler_params=params(60),
        cost_estimate=cost(3 * 10**9, [*args, *outs]),
    )(*args)


def feed_kernel(n2_a_in, n2_b_in, two_at_in, two_bt_in, cot_own, cot_other, *refs):
    blocks, wd_in, kept, grads = refs[:8], refs[8], refs[9:12], refs[12:19]
    (
        n2_a, n2_b, two_at, two_bt, cot, wg, wu, wd, act, d_gate, d_up, wide, tall, sems,
        chunk_sems, grad_sems,
    ) = refs[19:]
    moves = Moves(sems)
    moves.start("rows", n2_a_in, n2_a)
    moves.start("rows", n2_b_in, n2_b)
    moves.start("rows", cot_own, cot.at[pl.ds(0, TOK), :])
    moves.start("rows", cot_other, cot.at[pl.ds(TOK, TOK), :])

    def weight_copies(i):
        lanes = pl.ds(pl.multiple_of(i * 256, 256), 256)
        pairs = [
            (blocks[4 * k + s].at[:, lanes], to.at[pl.ds(288 * s, 288), lanes])
            for s in range(4)
            for k, to in enumerate((wg, wu))
        ]
        pairs.append((wd_in.at[lanes, :], wd.at[lanes, :]))
        return [pltpu.make_async_copy(a, b, chunk_sems.at[i, j]) for j, (a, b) in enumerate(pairs)]

    for i in range(3):
        for c in weight_copies(i):
            c.start()
    moves.wait("rows")

    def grad_copies(k, i):
        lanes = pl.ds(pl.multiple_of(i * 256, 256), 256)
        slot = lax.rem(i, 2)
        return [
            pltpu.make_async_copy(
                wide.at[k, slot, pl.ds(288 * s, 288), :], grads[3 * k + s].at[:, lanes],
                grad_sems.at[k, slot, s],
            )
            for s in range(3)
        ]

    def columns(i, carry):
        lanes = pl.ds(pl.multiple_of(i * 256, 256), 256)
        for c in weight_copies(i):
            c.wait()

        @pl.when(i < 3)
        def _():
            for c in weight_copies(i + 3):
                c.start()

        gate, up = dot(n2_a[...], wg[:, lanes]), dot(n2_b[...], wu[:, lanes])
        d_act = dot_t(cot[...], wd[lanes, :])
        sig = 1.0 / (1.0 + jnp.exp(-gate))
        swish = gate * sig
        act[:, lanes] = (swish * up).astype(BF)
        d_up[:, lanes] = (d_act * swish).astype(BF)
        d_gate[:, lanes] = (d_act * up * sig * (1.0 + gate * (1.0 - sig))).astype(BF)
        return carry

    def grad_columns(i, carry):
        lanes = pl.ds(pl.multiple_of(i * 256, 256), 256)

        @pl.when(i >= 2)
        def _():
            for k in range(2):
                for c in grad_copies(k, i - 2):
                    c.wait()

        slot = lax.rem(i, 2)
        wide[0, slot] = dot(two_at[...], d_gate[:, lanes]).astype(BF)
        wide[1, slot] = dot(two_bt[...], d_up[:, lanes]).astype(BF)
        for k in range(2):
            for c in grad_copies(k, i):
                c.start()
        return carry

    lax.fori_loop(0, 4, columns, 0)
    moves.start("across", two_at_in.at[pl.ds(288, 864), :], two_at)
    moves.start("across", two_bt_in.at[pl.ds(288, 864), :], two_bt)
    lax.fori_loop(4, 6, columns, 0)
    for to, value in zip(kept, (act, d_gate, d_up)):
        moves.start("kept", value, to)
    moves.wait("across")
    lax.fori_loop(0, 6, grad_columns, 0)
    for n in range(4):
        rows = slice(384 * n, 384 * n + 384)
        tall[rows, :] = t_dot(act[:, rows], cot[...]).astype(BF)
        moves.start("down", tall.at[pl.ds(384 * n, 384), :], grads[6].at[pl.ds(384 * n, 384), :])
    for i in (4, 5):
        for k in range(2):
            for c in grad_copies(k, i):
                c.wait()
    moves.wait()


def feed_forward(*args):
    outs = [*[shaped(512, 1536, BF)] * 3, *[shaped(288, 1536, BF)] * 6, shaped(1536, D, BF)]
    return pl.pallas_call(
        feed_kernel,
        out_shape=outs,
        in_specs=[FAR] * 15,
        out_specs=[FAR] * 10,
        scratch_shapes=[
            *[pltpu.VMEM((512, D), BF)] * 2, *[pltpu.VMEM((864, 512), BF)] * 2,
            pltpu.VMEM((512, D), BF), pltpu.VMEM((D, 1536), BF), pltpu.VMEM((D, 1536), BF),
            pltpu.VMEM((1536, D), BF), *[pltpu.VMEM((512, 1536), BF)] * 3,
            pltpu.VMEM((2, 2, 864, 256), BF), pltpu.VMEM((1536, D), BF),
            pltpu.SemaphoreType.DMA((20,)), pltpu.SemaphoreType.DMA((6, 9)),
            pltpu.SemaphoreType.DMA((2, 2, 3)),
        ],
        compiler_params=params(60),
        cost_estimate=cost(10 * 10**9, [*args, *outs]),
    )(*args)


def feed_back_kernel(rows_a, rows_b, middle_in, d_gate_in, d_up_in, *refs):
    blocks, mlp_row, d_two_out = refs[:8], refs[8], refs[9]
    middle, d_gate, d_up, wg, wu, perm_a, perm_b, d_a, d_b, d_two, sems = refs[10:]
    moves = Moves(sems)
    moves.start("gate", d_gate_in, d_gate)
    for s in range(4):
        moves.start("gate", blocks[s], wg.at[pl.ds(288 * s, 288), :])
    moves.start("up", d_up_in, d_up)
    for s in range(4):
        moves.start("up", blocks[4 + s], wu.at[pl.ds(288 * s, 288), :])
    fill(perm_a, rows_a)
    fill(perm_b, rows_b)

    def times(left, right, to):
        def columns(i, carry):
            lanes = pl.ds(pl.multiple_of(i * 384, 384), 384)
            to[:, lanes] = dot_t(left[...], right[lanes, :]).astype(BF)
            return carry

        lax.fori_loop(0, 3, columns, 0)

    moves.wait("gate")
    moves.start("middle", middle_in, middle)
    times(d_gate, wg, d_a)
    moves.wait("up")
    times(d_up, wu, d_b)
    moves.wait("middle")
    value = middle[...]
    r2 = lax.rsqrt(jnp.mean(value * value, axis=1, keepdims=True) + EPS)

    def unmix(i, carry):
        lanes = pl.ds(pl.multiple_of(i * 384, 384), 384)
        got = dot_t(d_a[...], perm_a[lanes, :]) + dot_t(d_b[...], perm_b[lanes, :])
        d_two[:, lanes] = got.astype(BF)
        total = jnp.sum(got * middle[:, lanes] * r2, axis=0, keepdims=True)
        mlp_row[:, lanes] = jnp.broadcast_to(total, (8, 384))
        return carry

    lax.fori_loop(0, 3, unmix, 0)
    moves.start("two", d_two, d_two_out)
    moves.wait()


def feed_back(*args):
    outs = [shaped(8, D, F32), shaped(512, D, BF)]
    return pl.pallas_call(
        feed_back_kernel,
        out_shape=outs,
        in_specs=[VMEM] * 2 + [FAR] * 11,
        out_specs=[VMEM, FAR],
        scratch_shapes=[
            pltpu.VMEM((512, D), F32), *[pltpu.VMEM((512, 1536), BF)] * 2,
            pltpu.VMEM((D, 1536), BF), pltpu.VMEM((D, 1536), BF),
            *[pltpu.VMEM((D, D), BF)] * 2, *[pltpu.VMEM((512, D), BF)] * 3,
            pltpu.SemaphoreType.DMA((16,)),
        ],
        compiler_params=params(60),
        cost_estimate=cost(7 * 10**9, [*args, *outs]),
    )(*args)


def feed_out_kernel(middle_in, act_in, wd_in, out_own, out_send, middle, act, wd, own, low, sems):
    moves = Moves(sems)
    moves.start("in", act_in, act)
    moves.start("in", wd_in, wd)
    moves.start("in", middle_in.at[pl.ds(0, TOK), :], middle)
    moves.wait("in")

    def columns(i, carry):
        lanes = pl.ds(pl.multiple_of(i * 384, 384), 384)
        got = dot(act[...], wd[:, lanes])
        own[:, lanes] = middle[:, lanes] + got[:TOK]
        low[:, lanes] = got[TOK:].astype(BF)
        return carry

    lax.fori_loop(0, 3, columns, 0)
    moves.start("out", own, out_own)
    moves.start("out", low, out_send)
    moves.wait()


def feed_out(*args):
    outs = [shaped(TOK, D, F32), shaped(TOK, D, BF)]
    return pl.pallas_call(
        feed_out_kernel,
        out_shape=outs,
        in_specs=[FAR] * 3,
        out_specs=[FAR] * 2,
        scratch_shapes=[
            pltpu.VMEM((TOK, D), F32), pltpu.VMEM((512, 1536), BF), pltpu.VMEM((1536, D), BF),
            pltpu.VMEM((TOK, D), F32), pltpu.VMEM((TOK, D), BF), pltpu.SemaphoreType.DMA((8,)),
        ],
        compiler_params=params(60),
        cost_estimate=cost(2 * 10**9, [*args, *outs]),
    )(*args)


def grads_kernel(s, *refs):
    ins, outs = refs[:4], refs[4:6]
    two_a, two_b, d_gate, d_up, wide, sems = refs[6:]
    moves = Moves(sems)
    moves.start("a", ins[0].at[pl.ds(288 * s, 288), :], two_a)
    moves.start("a", ins[2], d_gate)
    moves.start("b", ins[1].at[pl.ds(288 * s, 288), :], two_b)
    moves.start("b", ins[3], d_up)
    for k, (name, left, right) in enumerate((("a", two_a, d_gate), ("b", two_b, d_up))):
        moves.wait(name)
        wide[k] = dot(left[...], right[...]).astype(BF)
        moves.start("out", wide.at[k], outs[k])
    moves.wait()


def feed_grads(s, *args):
    outs = [shaped(288, 1536, BF)] * 2
    return pl.pallas_call(
        functools.partial(grads_kernel, s),
        out_shape=outs,
        in_specs=[FAR] * 4,
        out_specs=[FAR] * 2,
        scratch_shapes=[
            *[pltpu.VMEM((288, 512), BF)] * 2, *[pltpu.VMEM((512, 1536), BF)] * 2,
            pltpu.VMEM((2, 288, 1536), BF), pltpu.SemaphoreType.DMA((12,)),
        ],
        compiler_params=params(60),
        cost_estimate=cost(9 * 10**8, [*args, *outs]),
    )(*args)


def add_kernel(*refs):
    n = len(refs) // 3
    for a, b, out in zip(refs[:n], refs[n : 2 * n], refs[2 * n :]):
        out[...] = (a[...].astype(F32) + b[...].astype(F32)).astype(BF)


def added(parts, arrived):
    blocks = [pl.BlockSpec((p.shape[0], p.shape[1] // 3), lambda i: (0, i)) for p in parts]
    return pl.pallas_call(
        add_kernel,
        grid=(3,),
        out_shape=[shaped(*p.shape, BF) for p in parts],
        in_specs=blocks * 2,
        out_specs=blocks,
        compiler_params=params(12),
        cost_estimate=cost(10**6, [*parts, *arrived, *parts]),
    )(*parts, *arrived)


def attention_back_kernel(
    gains, mlp_row, source, to_left, to_right, middle_in, d_two_in, other_in, cot_own, cot_other,
    w_o_in, probs_in, *refs
):
    turned_in, kv_in, cos_in, sin_in = refs[0], refs[1:5], refs[5], refs[6]
    tok_own, tok_other, w_in, normed_in, mixed_in = refs[7:12]
    d_middle_out, part_own_out, part_send_out, sent_grads = refs[12:16]
    (
        middle, d_two, other, cot, w_o, probs, turned, k_lo, k_hi, v_lo, v_hi, cos, sin,
        d_middle, d_branch, d_mixed, d_pre, d_qkv,
        tok, w, perm, left, right, normed_p, mixed, grads, part_own, part_send, d_p, g_out,
        rows_of_gains, sems,
    ) = refs[16:]
    moves = Moves(sems)
    moves.start("rows", middle_in, middle)
    moves.start("rows", d_two_in, d_two)
    moves.start("rows", other_in, other)
    moves.start("rows", cot_own, cot.at[pl.ds(0, TOK), :])
    moves.start("rows", cot_other, cot.at[pl.ds(TOK, TOK), :])
    moves.start("w_o", w_o_in, w_o)
    fill(perm, source)
    fill(left, to_left)
    fill(right, to_right)
    moves.wait("rows")
    for far, to in zip((turned_in, *kv_in, cos_in, sin_in, probs_in),
                       (turned, k_lo, k_hi, v_lo, v_hi, cos, sin, probs)):
        moves.start("heads", far, to)
    for b in range(2):
        rows, swapped = slice(b * TOK, b * TOK + TOK), slice((1 - b) * TOK, (2 - b) * TOK)
        value = middle[rows, :]
        r2 = lax.rsqrt(jnp.mean(value * value, axis=1, keepdims=True) + EPS)
        e2 = gains[1:2, :] * (d_two[rows, :].astype(F32) + other[swapped, :].astype(F32))
        got = cot[rows, :].astype(F32) + r2 * (
            e2 - value * (r2 * r2 * jnp.mean(value * e2, axis=1, keepdims=True))
        )
        if b == 0:
            d_middle[...] = got
            moves.start("out", d_middle, d_middle_out)
        d_branch[rows, :] = got.astype(BF)
    moves.wait("w_o")
    d_mixed[...] = dot_t(d_branch[...], w_o[...]).astype(BF)
    moves.wait("heads")
    moves.start("normed", normed_in, normed_p)
    moves.start("mixed", mixed_in, mixed)
    moves.start("back", w_in.at[:, pl.ds(0, 1024)], w)
    moves.start("back", tok_own, tok.at[pl.ds(0, TOK), :])
    moves.start("back", tok_other, tok.at[pl.ds(TOK, TOK), :])

    def one_row(b, carry):
        rows = pl.ds(pl.multiple_of(b * TOK, TOK), TOK)
        d_k = {}
        d_v = {}
        for j in range(5):
            lanes = slice(128 * j, 128 * j + 128)
            q_pair, d_pair = turned[rows, lanes], d_mixed[rows, lanes]
            total = None
            for h in (2 * j, 2 * j + 1):
                if h == 9:
                    continue
                kv, half = h // 3, h % 2
                at_kv = slice(128 * kv, 128 * kv + 128)
                k_ref, v_ref = (k_lo, v_lo) if half == 0 else (k_hi, v_hi)
                p = probs[h, rows, :]
                p32 = p.astype(F32)
                d_probs = dot_t(d_pair, v_ref[rows, at_kv])
                row_dot = jnp.sum(p32 * d_probs, axis=1, keepdims=True)
                d_raw = (p32 * (d_probs - row_dot) * HEAD ** (-0.5)).astype(BF)
                got = dot(d_raw, k_ref[rows, at_kv])
                total = got if total is None else total + got
                for sums, value in ((d_k, t_dot(d_raw, q_pair)), (d_v, t_dot(p, d_pair))):
                    sums[kv, half] = value if (kv, half) not in sums else sums[kv, half] + value
            d_pre[:, lanes] = total
        low = low_lanes((TOK, 128))

        def collected(sums, kv, half):
            return sums[kv, half] + pltpu.roll(sums[kv, 1 - half], 64, 1)

        d_pre[:, 512:640] = jnp.where(low, d_pre[:, 512:640], collected(d_k, 0, 1))
        d_pre[:, 640:768] = jnp.where(low, collected(d_k, 1, 0), collected(d_k, 2, 1))
        for j in range(6):
            lanes = slice(128 * j, 128 * j + 128)
            d_qkv[rows, lanes] = turn(d_pre[:, lanes], cos[rows, :], -sin[rows, :]).astype(BF)
        d_qkv[rows, 768:896] = jnp.where(low, collected(d_v, 0, 0), collected(d_v, 1, 1)).astype(BF)
        d_qkv[rows, 896:1024] = jnp.where(low, collected(d_v, 2, 0), 0.0).astype(BF)
        return carry

    lax.fori_loop(0, 2, one_row, 0)
    moves.wait("normed")

    def qkv_grads(i, carry):
        lanes = pl.ds(pl.multiple_of(i * 256, 256), 256)
        grads[:, lanes] = t_dot(normed_p[...], d_qkv[:, lanes]).astype(BF)
        return carry

    lax.fori_loop(0, 4, qkv_grads, 0)
    moves.wait("mixed")
    g_out[...] = t_dot(mixed[...], d_branch[...]).astype(BF)
    grads[:, 1024:1536] = (
        t_dot(left[...], g_out[:, :512]) + t_dot(right[...], g_out[:, 640:])
    ).astype(BF)
    grads[:, 1536:] = t_dot(left[...], g_out[:, 512:640]).astype(BF)
    moves.wait("back")
    total = jnp.zeros((1, D), F32)
    for b in range(2):
        rows = slice(b * TOK, b * TOK + TOK)
        d_p[...] = dot_t(d_qkv[rows, :], w[...]).astype(BF)
        x = tok[rows, :].astype(F32)
        r1 = lax.rsqrt(jnp.mean(x * x, axis=1, keepdims=True) + EPS)
        got = dot_t(d_p[...], perm[...])
        total = total + jnp.sum(got * x * r1, axis=0, keepdims=True)
        if b == 0:
            part_own[...] = got
            moves.start("part", part_own, part_own_out)
        else:
            part_send[...] = got.astype(BF)
            moves.start("part", part_send, part_send_out)
    which = lax.broadcasted_iota(jnp.int32, (128, D), 0)
    rows_of_gains[...] = jnp.where(
        which == 64, total, jnp.where(which == 65, mlp_row[0:1, :], 0.0)
    ).astype(BF)
    gain_columns = dot(rows_of_gains[...], perm[...]).T
    grads[:, 896:1024] = (grads[:, 896:1024].astype(F32) + gain_columns).astype(BF)
    moves.start("grads", grads, sent_grads)
    moves.wait()


def attention_back(*args):
    outs = [shaped(TOK, D, F32), shaped(TOK, D, F32), shaped(TOK, D, BF), shaped(DP, 1664, BF)]
    return pl.pallas_call(
        attention_back_kernel,
        out_shape=outs,
        in_specs=[VMEM] * 5 + [FAR] * (len(args) - 5),
        out_specs=[FAR] * 4,
        scratch_shapes=[
            pltpu.VMEM((512, D), F32), *[pltpu.VMEM((512, D), BF)] * 3, pltpu.VMEM((640, D), BF),
            pltpu.VMEM((9, 512, 256), BF), pltpu.VMEM((512, 768), BF),
            *[pltpu.VMEM((512, 384), BF)] * 4, *[pltpu.VMEM((512, 128), F32)] * 2,
            pltpu.VMEM((TOK, D), F32), pltpu.VMEM((512, D), BF), pltpu.VMEM((512, 640), BF),
            pltpu.VMEM((TOK, 768), F32), pltpu.VMEM((512, 1024), BF),
            pltpu.VMEM((512, D), BF), pltpu.VMEM((DP, 1024), BF), pltpu.VMEM((D, DP), BF),
            *[pltpu.VMEM((640, DP), BF)] * 2, pltpu.VMEM((512, DP), BF), pltpu.VMEM((512, 640), BF),
            pltpu.VMEM((DP, 1664), BF), pltpu.VMEM((TOK, D), F32), pltpu.VMEM((TOK, D), BF),
            pltpu.VMEM((TOK, DP), BF), pltpu.VMEM((640, D), BF), pltpu.VMEM((128, D), BF),
            pltpu.SemaphoreType.DMA((40,)),
        ],
        compiler_params=params(60),
        cost_estimate=cost(10 * 10**9, [*args, *outs]),
    )(*args)


class Lockstep:
    def __init__(self):
        self.last = ()

    def tie(self, *values):
        tied = lax.optimization_barrier((*values, *self.last))
        self.last = tied
        return tied[: len(values)]

    def after(self, *values):
        self.last = (*self.last, *values)

    def __call__(self, values, pairs, late=(), late_pairs=(), beside=tuple):
        tied = lax.optimization_barrier((*values, *self.last))
        sent = [send(v, p) for v, p in zip(tied, pairs)]
        sent += [send(v, p) for v, p in zip(late, late_pairs)]
        sent += beside()
        self.last = lax.optimization_barrier(tuple(sent))
        return list(self.last)

    def gather(self, blocks, axes, more=(), more_pairs=()):
        values = [b for b in blocks for _ in range(3)]
        pairs = [STRAIGHT[a][n] for a in axes for n in (1, 2, 3)]
        got = self([*values, *more], [*pairs, *more_pairs])
        rings = [[b, *got[3 * i : 3 * i + 3]] for i, b in enumerate(blocks)]
        return rings, got[3 * len(blocks) :]

    def scatter(self, makers, axes, table, late=(), late_pairs=()):
        values = [make(s).astype(BF) for make in makers for s in (1, 2, 3)]
        pairs = [table[a][4 - s] for a in axes for s in (1, 2, 3)]
        got = self(values, pairs, late, late_pairs)
        sums = [
            sum([g.astype(F32) for g in got[3 * i : 3 * i + 3]], make(0).astype(F32))
            for i, make in enumerate(makers)
        ]
        return sums, got[3 * len(makers) :]


def place(blocks, at, sign):
    out = jnp.zeros((4, *blocks[0].shape), blocks[0].dtype)
    for step, block in enumerate(blocks):
        out = lax.dynamic_update_index_in_dim(out, block, (at - sign * step) % 4, 0)
    return out


def row_tables(segment_row):
    places = jnp.arange(TOK, dtype=jnp.int32)
    same_doc = segment_row[:, None] == segment_row[None, :]
    starts = jnp.min(jnp.where(same_doc, places[None, :], TOK), axis=1)
    offsets = (places - starts).astype(F32)
    lane = jnp.arange(128, dtype=jnp.int32)
    frequency = jnp.exp((lane % 32).astype(F32) * (-2.0 * math.log(THETA) / HEAD))
    angles = offsets[:, None] * frequency[None, :]
    side = jnp.where(lane % 64 < 32, -1.0, 1.0)
    allowed = same_doc & (places[:, None] >= places[None, :])
    return jnp.cos(angles), jnp.sin(angles) * side, jnp.where(allowed, 0.0, -1e30).astype(F32)


def body(
    tokens, segments, attn_gain, w_query, w_key, w_value, w_out, mlp_gain, w_gate, w_up, w_down,
    cotangent,
):
    core = lax.axis_index("core")
    at = {
        "x": lax.axis_index("x"),
        "y": lax.axis_index("y"),
        "z": lax.axis_index("z_hi") * 2 + lax.axis_index("z_lo"),
    }
    sign = 1 - 2 * core
    first = core == 0

    which = jnp.reshape(core, (1,)).astype(jnp.int32)
    kept, given, traded = halves(
        which, w_gate, w_up, w_query, w_key, w_value, attn_gain.reshape(1, 9),
        mlp_gain.reshape(1, 9), w_out, w_down,
    )
    step = Lockstep()
    given, traded, seg_other = step(
        [given, traded, segments.astype(F32)], [CORES, TRADE, CORES]
    )
    rows = jnp.concatenate([jnp.where(first, kept, given), jnp.where(first, given, kept)], axis=0)


    order_a, order_b, order_c = ("x", "z", "y"), ("y", "x", "z"), ("z", "y", "x")

    def natural(order):
        k = jnp.arange(D, dtype=jnp.int32)
        r, t = k % 18, k // 18
        c = {}
        for level, axis in enumerate(order):
            c[axis] = (at[axis] - (sign if level > 0 else 1) * ((t // 4**level) % 4)) % 4
        chip = (((c["z"] // 2) * 4 + c["x"]) * 2 + c["z"] % 2) * 4 + c["y"]
        return chip * 18 + r

    one, two, three = zip(order_a, order_b, order_c)
    z_rows = jnp.concatenate([rows[:, 3072:], jnp.zeros((18, 62), BF), traded], axis=1)
    got = step([z_rows] * 3, [STRAIGHT["z"][n] for n in (1, 2, 3)])
    z_at = jnp.reshape(at["z"], (1,)).astype(jnp.int32)
    w_attn, down = spread(z_at, z_rows, *got)
    w_attn = lax.all_gather(
        w_attn, AXES, axis=0, tiled=True, axis_index_groups=LINES["y", "x"]
    )
    (ha, hb), _ = step.gather([rows[:, :1536], rows[:, 1536:3072]], one[:2])
    rows_a, rows_b = natural(order_a), natural(order_b)

    k = jnp.arange(DP, dtype=jnp.int32)
    outer, inner, r, s = k // 320, (k // 80) % 4, (k % 80) % 18, (k % 80) // 18
    x_at, y_at = jnp.where(first, outer, inner), jnp.where(first, inner, outer)
    z = (at["z"] - s) % 4
    source = (((z // 2 * 4 + x_at) * 2 + z % 2) * 4 + y_at) * 18 + r
    source = jnp.where(s < 4, source, -1)
    e = ((x_at * 2 + z % 2) * 4 + y_at) * 2 + z // 2
    to_left = jnp.where((r < 9) & (s < 4), e * 9 + r, -1)
    to_right = jnp.where((r >= 9) & (s < 4), e * 9 + r - 9, -1)
    rows_a, rows_b, source = (i[None, :] for i in (rows_a, rows_b, source))
    ring = [RINGS[a] for a in two]
    held = [[stack_rows(ha), stack_rows(hb), down.reshape(96, D)]]
    *arrived, tok_other = step([*held[-1], tokens], [*ring, CORES])
    held.append(arrived)
    (w_attn,) = step.tie(w_attn)
    w_attn = lax.all_gather(
        w_attn, AXES, axis=0, tiled=True, axis_index_groups=LINES["x", "y"]
    )
    *arrived, cot_other = step([*held[-1], cotangent], [*ring, CORES])
    held.append(arrived)
    seg_other = seg_other.astype(jnp.int32)
    tables = [row_tables(segments[0]), row_tables(seg_other[0])]
    cos, sin, bias = (jnp.concatenate(t, axis=0) for t in zip(*tables))

    held.append(step(held[-1], ring))
    ha, hb, hc = zip(*held)
    ring = [RINGS[a] for a in three[:2]]
    down = place([h.reshape(2, 48, D) for h in hc], at["y"], sign)
    down = jnp.transpose(down, (1, 0, 2, 3)).reshape(384, D)
    held = [[jnp.concatenate(ha, axis=0), jnp.concatenate(hb, axis=0)]]
    wd = lax.all_gather(down, "x", axis=0, tiled=True)
    held.append(step(held[-1], ring))
    (w_attn,) = step.tie(w_attn)
    normed_p, turned, k_lo, k_hi, v_lo, v_hi, w_o, gains = attention_heads(
        tokens, tok_other, w_attn, source, to_left[None, :], to_right[None, :], cos, sin
    )
    probs, mixed, part, part_low = attention_forward(turned, k_lo, k_hi, v_lo, v_hi, w_o, bias)
    *arrived, part_low = step(held[-1], ring, beside=lambda: (part_low,))
    held.append(arrived)
    rows = middle_rows(gains, rows_a, rows_b, tokens, tok_other, part, swap(part_low))
    *arrived, middle, n2_a, n2_b, two_at, two_bt = step(held[-1], ring, beside=lambda: rows)
    held.append(arrived)
    ha, hb = zip(*held)

    act, d_gate, d_up, *grads = feed_forward(
        n2_a, n2_b, two_at, two_bt, cotangent, cot_other, *ha, *hb, wd
    )
    kept = (two_at, two_bt, d_gate, d_up)
    g_down = lax.psum_scatter(grads[6], "x", scatter_dimension=0, tiled=True)

    mlp_row, d_two = feed_back(rows_a, rows_b, middle, d_gate, d_up, *ha, *hb)
    *arrived, d_two = step([grads[0], grads[3]], ring, beside=lambda: (d_two,))
    sums = added([grads[1], grads[4]], arrived)
    d_middle, part_own, part_send, g_attn = attention_back(
        gains, mlp_row, source, to_left[None, :], to_right[None, :], middle, d_two, swap(d_two),
        cotangent, cot_other, w_o, probs, turned, k_lo, k_hi, v_lo, v_hi, cos, sin, tokens,
        tok_other, w_attn, normed_p, mixed,
    )
    *kept, act, part_send = lax.optimization_barrier((*kept, act, part_send))
    *arrived, part_send, g_attn = step(sums, ring, beside=lambda: (part_send, g_attn))
    sums = added([grads[2], grads[5]], arrived)
    out_own, out_send = feed_out(middle, act, wd)
    *arrived, part_other, out_send = step(
        [*sums, part_send], [*ring, CORES], beside=lambda: (out_send,)
    )
    g_gate, g_up = added(feed_grads(0, *kept), arrived)
    g_attn_x = lax.psum_scatter(
        g_attn, AXES, scatter_dimension=0, tiled=True, axis_index_groups=LINES["x", "y"]
    )
    g_attn = lax.psum_scatter(
        g_attn_x, AXES, scatter_dimension=0, tiled=True, axis_index_groups=LINES["y", "x"]
    )

    d_normed = part_own + part_other.astype(F32)
    x_own = tokens.astype(F32)
    r_own = lax.rsqrt(jnp.mean(x_own * x_own, axis=-1, keepdims=True) + EPS)
    e1 = d_normed * gains[0]
    grad_input = d_middle + r_own * (
        e1 - x_own * r_own * r_own * jnp.mean(x_own * e1, axis=-1, keepdims=True)
    )

    def rows_of(held, n):
        return lambda s: held[n * s : n * s + n]

    def y_block(s):
        down = g_down.reshape(2, 4, 48, D)
        return lax.dynamic_index_in_dim(down, (at["y"] - sign * s) % 4, 1, False).reshape(96, D)

    (g_up,), (out_other,) = step.scatter(
        [rows_of(g_up, 72)], two[1:2], SIGNED, [out_send], [CORES]
    )
    output = (out_own + out_other.astype(F32)).astype(BF)
    step.after(g_attn_x)
    (g_gate, g_down), _ = step.scatter(
        [rows_of(g_gate, 72), y_block], (two[0], two[2]), SIGNED
    )
    own, *packed = pack(z_at, g_attn, g_down.astype(BF).reshape(4, 24, D))
    (g_gate, g_up), got = step.scatter(
        [rows_of(g_gate, 18), rows_of(g_up, 18)], one[:2], STRAIGHT,
        packed, [STRAIGHT["z"][4 - s] for s in (1, 2, 3)],
    )
    g_z = sum([g.astype(F32) for g in got], own.astype(F32))

    g_rows = jnp.concatenate([g_gate, g_up, g_z[:, :962]], axis=1)
    mine = jnp.where(first, g_rows[:9], g_rows[9:])
    theirs = jnp.where(first, g_rows[9:], g_rows[:9]).astype(BF)
    theirs, g_od = step([theirs, g_z[:, 1024:].astype(BF)], [CORES, TRADE])
    g_g, g_u, g_q, g_k, g_v, g_o, g_d, g_gains = whole(which, mine, theirs, g_od)
    return (
        output, grad_input, g_gains[0], g_q, g_k, g_v, g_o, g_gains[1], g_g, g_u, g_d,
    )


def solution(mesh):
    fine = Mesh(mesh.devices.reshape(SHAPE), AXES)
    rows, vector = P(AXES, None), P(AXES)
    return jax.shard_map(
        body,
        mesh=fine,
        in_specs=(rows, rows, vector, rows, rows, rows, rows, vector, rows, rows, rows, rows),
        out_specs=(rows, rows, vector, rows, rows, rows, rows, vector, rows, rows, rows),
        check_vma=False,
    )
```

```python
import functools
import math

import jax
import jax.numpy as jnp
import numpy as np
from jax import lax
from jax.experimental import pallas as pl
from jax.experimental.pallas import tpu as pltpu
from jax.sharding import Mesh
from jax.sharding import PartitionSpec as P

D = 1152
HEADS = 18
KV_HEADS = 6
HEAD = 64
FF = 3072
DP = 1280
TOK = 256
EPS = 1e-05
THETA = 10000.0

SHAPE = (2, 4, 2, 4, 2)
AXES = ("z_hi", "x", "z_lo", "y", "core")
BF = jnp.bfloat16
F32 = jnp.float32


def device_pairs(move):
    pairs = []
    for i in range(128):
        zh, x, zl, y, c = (int(v) for v in np.unravel_index(i, SHAPE))
        x, y, z, c = move(x, y, zh * 2 + zl, c)
        x, y, z = x % 4, y % 4, z % 4
        pairs.append((i, int(np.ravel_multi_index((z // 2, x, z % 2, y, c), SHAPE))))
    return pairs


RINGS = {
    "x": device_pairs(lambda x, y, z, c: (x + 1 - 2 * c, y, z, c)),
    "y": device_pairs(lambda x, y, z, c: (x, y + 1 - 2 * c, z, c)),
    "z": device_pairs(lambda x, y, z, c: (x, y, z + 1 - 2 * c, c)),
}
CORES = device_pairs(lambda x, y, z, c: (x, y, z, 1 - c))
TRADE = device_pairs(lambda x, y, z, c: (x, y, c * 2 + z % 2, z // 2))


def lines(*axes):
    index = np.arange(128).reshape(SHAPE)
    groups = []
    for core, axis in enumerate(axes):
        along = np.moveaxis(index[..., core], AXES.index(axis), -1)
        groups += along.reshape(-1, 4).tolist()
    return groups


LINES = {("x", "y"): lines("x", "y"), ("y", "x"): lines("y", "x")}


def send(value, pairs):
    return lax.ppermute(value, AXES, pairs)


def swap(value):
    return send(value, CORES)


def dot(a, b):
    return jnp.dot(a, b, preferred_element_type=F32)


def dot_t(a, b):
    return lax.dot_general(a, b, (((1,), (1,)), ((), ())), preferred_element_type=F32)


def t_dot(a, b):
    return lax.dot_general(a, b, (((0,), (0,)), ((), ())), preferred_element_type=F32)


def shift(axis, n):
    return device_pairs(lambda x, y, z, c: (
        x + n * (axis == "x"), y + n * (axis == "y"), z + n * (axis == "z"), c))


def signed(axis, n):
    return device_pairs(lambda x, y, z, c: (
        x + n * (1 - 2 * c) * (axis == "x"), y + n * (1 - 2 * c) * (axis == "y"),
        z + n * (1 - 2 * c) * (axis == "z"), c))


SIGNED = {axis: {n: signed(axis, n) for n in (1, 2, 3)} for axis in ("x", "y", "z")}
STRAIGHT = {axis: {n: shift(axis, n) for n in (1, 2, 3)} for axis in ("x", "y", "z")}


def params(mib):
    return pltpu.CompilerParams(vmem_limit_bytes=mib * 2**20)


FAR = pl.BlockSpec(memory_space=pltpu.HBM)
SMEM = pl.BlockSpec(memory_space=pltpu.SMEM)
VMEM = pl.BlockSpec(memory_space=pltpu.VMEM)


def shaped(rows, columns, dtype):
    return jax.ShapeDtypeStruct((rows, columns), dtype)


def cost(flops, arrays):
    return pl.CostEstimate(
        flops=flops,
        bytes_accessed=sum(math.prod(a.shape) * a.dtype.itemsize for a in arrays),
        transcendentals=0,
    )


def low_lanes(shape):
    return lax.broadcasted_iota(jnp.int32, shape, 1) % 128 < 64


def turn(v, cos, sin):
    ahead = lax.broadcasted_iota(jnp.int32, v.shape, 1) % 64 < 32
    return v * cos + jnp.where(ahead, pltpu.roll(v, 96, 1), pltpu.roll(v, 32, 1)) * sin


def fill(to, index):
    def rows_of(i, carry):
        rows = pl.ds(pl.multiple_of(i * 128, 128), 128)
        at = lax.broadcasted_iota(jnp.int32, (128, to.shape[1]), 0) + i * 128
        to[rows, :] = jnp.where(at == index[...], 1.0, 0.0).astype(BF)
        return carry

    lax.fori_loop(0, to.shape[0] // 128, rows_of, 0)


def stack_kernel(*refs):
    *blocks, out = refs
    out[...] = jnp.concatenate([b[...].astype(F32) for b in blocks], axis=0).astype(out.dtype)


def stack_rows(blocks):
    rows = sum(b.shape[0] for b in blocks)
    return pl.pallas_call(
        stack_kernel,
        out_shape=shaped(rows, blocks[0].shape[1], blocks[0].dtype),
        compiler_params=params(8),
    )(*blocks)


CUTS = ((0, 1536), (1536, 1536), (3072, 576), (3648, 192), (3840, 192))


def folded(rows):
    last = jnp.concatenate([rows[18:, 384 * j : 384 * j + 384] for j in range(3)], axis=0)
    return jnp.concatenate([rows[:18], last], axis=1)


def unfolded(rows):
    last = [rows[6 * j : 6 * j + 6, D:] for j in range(3)]
    return jnp.concatenate([rows[:, :D], jnp.concatenate(last, axis=1)], axis=0)


def z_place(at, s):
    z = lax.rem(at[0] - s + 4, 4)
    return lax.rem(z, 2) * 2 + z // 2


def spread_kernel(at, *refs):
    *blocks, attn, down = refs
    rows = [b[...].astype(F32) for b in blocks]
    spare = jnp.zeros((8, 1664), F32)
    attn[...] = jnp.concatenate([*(r[:, :1664] for r in rows), spare], axis=0).astype(BF)
    for s, r in enumerate(rows):
        down[z_place(at, s)] = unfolded(r[:, 1664:]).astype(BF)


def spread(at, *blocks):
    return pl.pallas_call(
        spread_kernel,
        out_shape=[shaped(80, 1664, BF), jax.ShapeDtypeStruct((4, 24, D), BF)],
        in_specs=[SMEM] + [VMEM] * 4,
        compiler_params=params(8),
    )(at, *blocks)


def pack_kernel(at, attn, down, *outs):
    rows = attn[...].astype(F32)
    for s, out in enumerate(outs):
        out[:, :1664] = rows[18 * s : 18 * s + 18].astype(BF)
        out[:, 1664:] = folded(down[z_place(at, s)].astype(F32)).astype(BF)


def pack(*args):
    return pl.pallas_call(
        pack_kernel,
        out_shape=[shaped(18, 3200, BF)] * 4,
        in_specs=[SMEM] + [VMEM] * 2,
        compiler_params=params(8),
    )(*args)


def halves_kernel(core, gate, up, query, key, value, gain_one, gain_two, out, down, kept, given, traded):
    first = core[0] == 0
    for (at, n), w in zip(CUTS, (gate, up, query, key, value)):
        low, high = w[:, :n].astype(F32), w[:, n:].astype(F32)
        kept[:, at : at + n] = jnp.where(first, low, high).astype(BF)
        given[:, at : at + n] = jnp.where(first, high, low).astype(BF)
    row = lax.broadcasted_iota(jnp.int32, (9, 9), 0)
    same = row == lax.broadcasted_iota(jnp.int32, (9, 9), 1)
    for i, gain in enumerate((gain_one, gain_two)):
        spread = jnp.where(same, jnp.broadcast_to(gain[...].astype(F32), (9, 9)), 0.0)
        column = jnp.sum(spread, axis=1, keepdims=True).astype(BF)
        kept[:, 4032 + i : 4033 + i] = column
        given[:, 4032 + i : 4033 + i] = column
    rows = out[...].astype(F32)
    spare = jnp.zeros((9, 128), F32)
    rows = jnp.concatenate(
        [rows[:, :640], jnp.concatenate([rows[:, 640:], spare], axis=1)], axis=0
    )
    traded[:, :640] = rows.astype(BF)
    traded[:, 640:] = folded(down[...].astype(F32)).astype(BF)


def halves(*args):
    return pl.pallas_call(
        halves_kernel,
        out_shape=[shaped(9, 4034, BF), shaped(9, 4034, BF), shaped(18, 2176, BF)],
        in_specs=[SMEM] + [VMEM] * 9,
        compiler_params=params(60),
    )(*args)


def whole_kernel(core, mine, theirs, traded, gate, up, query, key, value, out, down, gains):
    first = core[0] == 0
    own, other = mine[...], theirs[...].astype(F32)
    low, high = jnp.where(first, own, other), jnp.where(first, other, own)
    for (at, n), to in zip(CUTS, (gate, up, query, key, value)):
        to[:, :n] = low[:, at : at + n]
        to[:, n:] = high[:, at : at + n]
    rows = traded[...].astype(F32)
    out[:, :640] = rows[:9, :640]
    out[:, 640:] = rows[9:, :512]
    down[...] = unfolded(rows[:, 640:])
    same = lax.broadcasted_iota(jnp.int32, (9, 9), 0) == lax.broadcasted_iota(jnp.int32, (9, 9), 1)
    for i in range(2):
        column = low[:, 4032 + i : 4033 + i] + high[:, 4032 + i : 4033 + i]
        spread = jnp.where(same, jnp.broadcast_to(column, (9, 9)), 0.0)
        gains[i : i + 1, :] = jnp.sum(spread, axis=0, keepdims=True)


def whole(*args):
    outs = [shaped(9, 2 * n, F32) for _, n in CUTS]
    return pl.pallas_call(
        whole_kernel,
        out_shape=[*outs, shaped(9, D, F32), shaped(24, D, F32), shaped(2, 9, F32)],
        in_specs=[SMEM] + [VMEM] * 3,
        compiler_params=params(8),
    )(*args)


def heads_kernel(
    tok_own, tok_other, w, source, to_left, to_right, cos, sin,
    normed_p, turned, k_lo, k_hi, v_lo, v_hi, w_o, gains, gathered, pre, perm, left, right,
):
    fill(perm, source)
    fill(left, to_left)
    fill(right, to_right)
    gathered[...] = dot(perm[...], w[:, 896:1024]).T
    gains[...] = gathered[64:72, :]
    for b, tok in enumerate((tok_own, tok_other)):
        rows = slice(b * TOK, b * TOK + TOK)
        x = tok[...].astype(F32)
        r1 = lax.rsqrt(jnp.mean(x * x, axis=1, keepdims=True) + EPS)
        normed = (x * r1 * gains[0:1, :]).astype(BF)
        normed_p[rows, :] = dot(normed, perm[...]).astype(BF)
    w_o[:, :640] = dot(left[...], w[:, 1024:1664]).astype(BF)
    w_o[:, 640:] = dot(right[...], w[:, 1024:1536]).astype(BF)

    def one_row(b, carry):
        rows = pl.ds(pl.multiple_of(b * TOK, TOK), TOK)
        pre[...] = dot(normed_p[rows, :], w[:, :1024])
        for j in range(6):
            lanes = slice(128 * j, 128 * j + 128)
            turned[rows, lanes] = turn(pre[:, lanes], cos[rows, :], sin[rows, :]).astype(BF)
        low = low_lanes((TOK, 128))
        zero = jnp.zeros((TOK, 128), F32)

        def both(value, half, to_low, to_high, kv):
            value = jnp.where(low if half == 0 else ~low, value, zero)
            moved = pltpu.roll(value, 64, 1)
            pair = (value, moved) if half == 0 else (moved, value)
            lanes = slice(128 * kv, 128 * kv + 128)
            to_low[rows, lanes], to_high[rows, lanes] = pair[0].astype(BF), pair[1].astype(BF)

        for kv, (j, half) in enumerate(((4, 1), (5, 0), (5, 1))):
            lanes = slice(128 * j, 128 * j + 128)
            both(turned[rows, lanes].astype(F32), half, k_lo, k_hi, kv)
        for kv, (j, half) in enumerate(((6, 0), (6, 1), (7, 0))):
            both(pre[:, 128 * j : 128 * j + 128], half, v_lo, v_hi, kv)
        return carry

    lax.fori_loop(0, 2, one_row, 0)


def attention_heads(*args):
    outs = [
        shaped(512, DP, BF), shaped(512, 768, BF), *[shaped(512, 384, BF)] * 4, shaped(640, D, BF),
        shaped(8, D, F32),
    ]
    return pl.pallas_call(
        heads_kernel,
        out_shape=outs,
        scratch_shapes=[
            pltpu.VMEM((128, D), F32), pltpu.VMEM((TOK, 1024), F32), pltpu.VMEM((D, DP), BF),
            *[pltpu.VMEM((640, DP), BF)] * 2,
        ],
        compiler_params=params(32),
        cost_estimate=cost(5 * 10**9, [*args, *outs]),
    )(*args)


def attention_kernel(
    turned, k_lo, k_hi, v_lo, v_hi, w_o, bias, probs, mixed, part, part_low
):
    def one_row(b, carry):
        rows = pl.ds(pl.multiple_of(b * TOK, TOK), TOK)
        for j in range(5):
            lanes = slice(128 * j, 128 * j + 128)
            total = None
            for h in (2 * j, 2 * j + 1):
                if h == 9:
                    continue
                kv = slice(128 * (h // 3), 128 * (h // 3) + 128)
                k_ref, v_ref = (k_lo, v_lo) if h % 2 == 0 else (k_hi, v_hi)
                s = dot_t(turned[rows, lanes], k_ref[rows, kv]) * HEAD ** (-0.5) + bias[rows, :]
                e = jnp.exp(s - jnp.max(s, axis=1, keepdims=True))
                p = (e * (1.0 / jnp.sum(e, axis=1, keepdims=True))).astype(BF)
                probs[h, rows, :] = p
                got = dot(p, v_ref[rows, kv])
                total = got if total is None else total + got
            mixed[rows, lanes] = total.astype(BF)
        for n in range(3):
            lanes = slice(384 * n, 384 * n + 384)
            got = dot(mixed[rows, :], w_o[:, lanes])
            part[rows, lanes] = got
            part_low[rows, lanes] = got.astype(BF)
        return carry

    lax.fori_loop(0, 2, one_row, 0)


def attention_forward(*args):
    outs = [
        jax.ShapeDtypeStruct((9, 512, 256), BF), shaped(512, 640, BF), shaped(512, D, F32),
        shaped(512, D, BF),
    ]
    return pl.pallas_call(
        attention_kernel,
        out_shape=outs,
        compiler_params=params(20),
        cost_estimate=cost(3 * 10**9, [*args, *outs]),
    )(*args)


class Moves:
    def __init__(self, sems):
        self.sems, self.count, self.open = sems, 0, {}

    def start(self, name, source, to):
        copy = pltpu.make_async_copy(source, to, self.sems.at[self.count])
        copy.start()
        self.count += 1
        self.open.setdefault(name, []).append(copy)

    def wait(self, *names):
        for name in names or tuple(self.open):
            for copy in self.open.pop(name):
                copy.wait()


def middle_kernel(
    gains, rows_a, rows_b, tok_own, tok_other, part, other,
    middle_out, n2_a_out, n2_b_out, two_at_out, two_bt_out,
    tok, middle, near, perm_a, perm_b, n2, n2_a, n2_b, two_at, two_bt, sems,
):
    moves = Moves(sems)
    moves.start("rows", tok_own, tok.at[pl.ds(0, TOK), :])
    moves.start("rows", tok_other, tok.at[pl.ds(TOK, TOK), :])
    moves.start("rows", part, middle)
    moves.start("rows", other, near)
    fill(perm_a, rows_a)
    fill(perm_b, rows_b)
    moves.wait("rows")
    for b in range(2):
        rows, swapped = slice(b * TOK, b * TOK + TOK), slice((1 - b) * TOK, (2 - b) * TOK)
        value = tok[rows, :].astype(F32) + middle[rows, :] + near[swapped, :].astype(F32)
        middle[rows, :] = value
        r2 = lax.rsqrt(jnp.mean(value * value, axis=1, keepdims=True) + EPS)
        n2[rows, :] = (value * r2 * gains[1:2, :]).astype(BF)
    moves.start("out", middle, middle_out)
    for perm, to, across, to_out, across_out in (
        (perm_a, n2_a, two_at, n2_a_out, two_at_out),
        (perm_b, n2_b, two_bt, n2_b_out, two_bt_out),
    ):
        for n in range(3):
            lanes = slice(384 * n, 384 * n + 384)
            to[:, lanes] = dot(n2[...], perm[:, lanes]).astype(BF)
        moves.start("out", to, to_out)
        across[...] = to[...].T
        moves.start("out", across, across_out)
    moves.wait()


def middle_rows(*args):
    outs = [shaped(512, D, F32), *[shaped(512, D, BF)] * 2, *[shaped(D, 512, BF)] * 2]
    return pl.pallas_call(
        middle_kernel,
        out_shape=outs,
        in_specs=[VMEM] * 3 + [FAR] * 4,
        out_specs=[FAR] * 5,
        scratch_shapes=[
            pltpu.VMEM((512, D), BF), pltpu.VMEM((512, D), F32), pltpu.VMEM((512, D), BF),
            *[pltpu.VMEM((D, D), BF)] * 2, *[pltpu.VMEM((512, D), BF)] * 3,
            *[pltpu.VMEM((D, 512), BF)] * 2, pltpu.SemaphoreType.DMA((12,)),
        ],
        compiler_params=params(60),
        cost_estimate=cost(3 * 10**9, [*args, *outs]),
    )(*args)


def feed_kernel(n2_a_in, n2_b_in, two_at_in, two_bt_in, cot_own, cot_other, *refs):
    blocks, wd_in, kept, grads = refs[:8], refs[8], refs[9:12], refs[12:19]
    (
        n2_a, n2_b, two_at, two_bt, cot, wg, wu, wd, act, d_gate, d_up, wide, tall, sems,
        chunk_sems, grad_sems,
    ) = refs[19:]
    moves = Moves(sems)
    moves.start("rows", n2_a_in, n2_a)
    moves.start("rows", n2_b_in, n2_b)
    moves.start("rows", cot_own, cot.at[pl.ds(0, TOK), :])
    moves.start("rows", cot_other, cot.at[pl.ds(TOK, TOK), :])

    def weight_copies(i):
        lanes = pl.ds(pl.multiple_of(i * 256, 256), 256)
        pairs = [
            (blocks[4 * k + s].at[:, lanes], to.at[pl.ds(288 * s, 288), lanes])
            for s in range(4)
            for k, to in enumerate((wg, wu))
        ]
        pairs.append((wd_in.at[lanes, :], wd.at[lanes, :]))
        return [pltpu.make_async_copy(a, b, chunk_sems.at[i, j]) for j, (a, b) in enumerate(pairs)]

    for i in range(3):
        for c in weight_copies(i):
            c.start()
    moves.wait("rows")

    def grad_copies(k, i):
        lanes = pl.ds(pl.multiple_of(i * 256, 256), 256)
        slot = lax.rem(i, 2)
        return [
            pltpu.make_async_copy(
                wide.at[k, slot, pl.ds(288 * s, 288), :], grads[3 * k + s].at[:, lanes],
                grad_sems.at[k, slot, s],
            )
            for s in range(3)
        ]

    def columns(i, carry):
        lanes = pl.ds(pl.multiple_of(i * 256, 256), 256)
        for c in weight_copies(i):
            c.wait()

        @pl.when(i < 3)
        def _():
            for c in weight_copies(i + 3):
                c.start()

        gate, up = dot(n2_a[...], wg[:, lanes]), dot(n2_b[...], wu[:, lanes])
        d_act = dot_t(cot[...], wd[lanes, :])
        sig = 1.0 / (1.0 + jnp.exp(-gate))
        swish = gate * sig
        act[:, lanes] = (swish * up).astype(BF)
        d_up[:, lanes] = (d_act * swish).astype(BF)
        d_gate[:, lanes] = (d_act * up * sig * (1.0 + gate * (1.0 - sig))).astype(BF)
        return carry

    def grad_columns(i, carry):
        lanes = pl.ds(pl.multiple_of(i * 256, 256), 256)

        @pl.when(i >= 2)
        def _():
            for k in range(2):
                for c in grad_copies(k, i - 2):
                    c.wait()

        slot = lax.rem(i, 2)
        wide[0, slot] = dot(two_at[...], d_gate[:, lanes]).astype(BF)
        wide[1, slot] = dot(two_bt[...], d_up[:, lanes]).astype(BF)
        for k in range(2):
            for c in grad_copies(k, i):
                c.start()
        return carry

    lax.fori_loop(0, 4, columns, 0)
    moves.start("across", two_at_in.at[pl.ds(288, 864), :], two_at)
    moves.start("across", two_bt_in.at[pl.ds(288, 864), :], two_bt)
    lax.fori_loop(4, 6, columns, 0)
    for to, value in zip(kept, (act, d_gate, d_up)):
        moves.start("kept", value, to)
    moves.wait("across")
    lax.fori_loop(0, 6, grad_columns, 0)
    for n in range(4):
        rows = slice(384 * n, 384 * n + 384)
        tall[rows, :] = t_dot(act[:, rows], cot[...]).astype(BF)
        moves.start("down", tall.at[pl.ds(384 * n, 384), :], grads[6].at[pl.ds(384 * n, 384), :])
    for i in (4, 5):
        for k in range(2):
            for c in grad_copies(k, i):
                c.wait()
    moves.wait()


def feed_forward(*args):
    outs = [*[shaped(512, 1536, BF)] * 3, *[shaped(288, 1536, BF)] * 6, shaped(1536, D, BF)]
    return pl.pallas_call(
        feed_kernel,
        out_shape=outs,
        in_specs=[FAR] * 15,
        out_specs=[FAR] * 10,
        scratch_shapes=[
            *[pltpu.VMEM((512, D), BF)] * 2, *[pltpu.VMEM((864, 512), BF)] * 2,
            pltpu.VMEM((512, D), BF), pltpu.VMEM((D, 1536), BF), pltpu.VMEM((D, 1536), BF),
            pltpu.VMEM((1536, D), BF), *[pltpu.VMEM((512, 1536), BF)] * 3,
            pltpu.VMEM((2, 2, 864, 256), BF), pltpu.VMEM((1536, D), BF),
            pltpu.SemaphoreType.DMA((20,)), pltpu.SemaphoreType.DMA((6, 9)),
            pltpu.SemaphoreType.DMA((2, 2, 3)),
        ],
        compiler_params=params(60),
        cost_estimate=cost(10 * 10**9, [*args, *outs]),
    )(*args)


def feed_back_kernel(rows_a, rows_b, middle_in, d_gate_in, d_up_in, *refs):
    blocks, mlp_row, d_two_out = refs[:8], refs[8], refs[9]
    middle, d_gate, d_up, wg, wu, perm_a, perm_b, d_a, d_b, d_two, sems = refs[10:]
    moves = Moves(sems)
    moves.start("gate", d_gate_in, d_gate)
    for s in range(4):
        moves.start("gate", blocks[s], wg.at[pl.ds(288 * s, 288), :])
    moves.start("up", d_up_in, d_up)
    for s in range(4):
        moves.start("up", blocks[4 + s], wu.at[pl.ds(288 * s, 288), :])
    fill(perm_a, rows_a)
    fill(perm_b, rows_b)

    def times(left, right, to):
        def columns(i, carry):
            lanes = pl.ds(pl.multiple_of(i * 384, 384), 384)
            to[:, lanes] = dot_t(left[...], right[lanes, :]).astype(BF)
            return carry

        lax.fori_loop(0, 3, columns, 0)

    moves.wait("gate")
    moves.start("middle", middle_in, middle)
    times(d_gate, wg, d_a)
    moves.wait("up")
    times(d_up, wu, d_b)
    moves.wait("middle")
    value = middle[...]
    r2 = lax.rsqrt(jnp.mean(value * value, axis=1, keepdims=True) + EPS)

    def unmix(i, carry):
        lanes = pl.ds(pl.multiple_of(i * 384, 384), 384)
        got = dot_t(d_a[...], perm_a[lanes, :]) + dot_t(d_b[...], perm_b[lanes, :])
        d_two[:, lanes] = got.astype(BF)
        total = jnp.sum(got * middle[:, lanes] * r2, axis=0, keepdims=True)
        mlp_row[:, lanes] = jnp.broadcast_to(total, (8, 384))
        return carry

    lax.fori_loop(0, 3, unmix, 0)
    moves.start("two", d_two, d_two_out)
    moves.wait()


def feed_back(*args):
    outs = [shaped(8, D, F32), shaped(512, D, BF)]
    return pl.pallas_call(
        feed_back_kernel,
        out_shape=outs,
        in_specs=[VMEM] * 2 + [FAR] * 11,
        out_specs=[VMEM, FAR],
        scratch_shapes=[
            pltpu.VMEM((512, D), F32), *[pltpu.VMEM((512, 1536), BF)] * 2,
            pltpu.VMEM((D, 1536), BF), pltpu.VMEM((D, 1536), BF),
            *[pltpu.VMEM((D, D), BF)] * 2, *[pltpu.VMEM((512, D), BF)] * 3,
            pltpu.SemaphoreType.DMA((16,)),
        ],
        compiler_params=params(60),
        cost_estimate=cost(7 * 10**9, [*args, *outs]),
    )(*args)


def feed_out_kernel(middle_in, act_in, wd_in, out_own, out_send, middle, act, wd, own, low, sems):
    moves = Moves(sems)
    moves.start("in", act_in, act)
    moves.start("in", wd_in, wd)
    moves.start("in", middle_in.at[pl.ds(0, TOK), :], middle)
    moves.wait("in")

    def columns(i, carry):
        lanes = pl.ds(pl.multiple_of(i * 384, 384), 384)
        got = dot(act[...], wd[:, lanes])
        own[:, lanes] = middle[:, lanes] + got[:TOK]
        low[:, lanes] = got[TOK:].astype(BF)
        return carry

    lax.fori_loop(0, 3, columns, 0)
    moves.start("out", own, out_own)
    moves.start("out", low, out_send)
    moves.wait()


def feed_out(*args):
    outs = [shaped(TOK, D, F32), shaped(TOK, D, BF)]
    return pl.pallas_call(
        feed_out_kernel,
        out_shape=outs,
        in_specs=[FAR] * 3,
        out_specs=[FAR] * 2,
        scratch_shapes=[
            pltpu.VMEM((TOK, D), F32), pltpu.VMEM((512, 1536), BF), pltpu.VMEM((1536, D), BF),
            pltpu.VMEM((TOK, D), F32), pltpu.VMEM((TOK, D), BF), pltpu.SemaphoreType.DMA((8,)),
        ],
        compiler_params=params(60),
        cost_estimate=cost(2 * 10**9, [*args, *outs]),
    )(*args)


def grads_kernel(s, *refs):
    ins, outs = refs[:4], refs[4:6]
    two_a, two_b, d_gate, d_up, wide, sems = refs[6:]
    moves = Moves(sems)
    moves.start("a", ins[0].at[pl.ds(288 * s, 288), :], two_a)
    moves.start("a", ins[2], d_gate)
    moves.start("b", ins[1].at[pl.ds(288 * s, 288), :], two_b)
    moves.start("b", ins[3], d_up)
    for k, (name, left, right) in enumerate((("a", two_a, d_gate), ("b", two_b, d_up))):
        moves.wait(name)
        wide[k] = dot(left[...], right[...]).astype(BF)
        moves.start("out", wide.at[k], outs[k])
    moves.wait()


def feed_grads(s, *args):
    outs = [shaped(288, 1536, BF)] * 2
    return pl.pallas_call(
        functools.partial(grads_kernel, s),
        out_shape=outs,
        in_specs=[FAR] * 4,
        out_specs=[FAR] * 2,
        scratch_shapes=[
            *[pltpu.VMEM((288, 512), BF)] * 2, *[pltpu.VMEM((512, 1536), BF)] * 2,
            pltpu.VMEM((2, 288, 1536), BF), pltpu.SemaphoreType.DMA((12,)),
        ],
        compiler_params=params(60),
        cost_estimate=cost(9 * 10**8, [*args, *outs]),
    )(*args)


def add_kernel(*refs):
    n = len(refs) // 3
    for a, b, out in zip(refs[:n], refs[n : 2 * n], refs[2 * n :]):
        out[...] = (a[...].astype(F32) + b[...].astype(F32)).astype(BF)


def added(parts, arrived):
    blocks = [pl.BlockSpec((p.shape[0], p.shape[1] // 3), lambda i: (0, i)) for p in parts]
    return pl.pallas_call(
        add_kernel,
        grid=(3,),
        out_shape=[shaped(*p.shape, BF) for p in parts],
        in_specs=blocks * 2,
        out_specs=blocks,
        compiler_params=params(60),
        cost_estimate=cost(10**6, [*parts, *arrived, *parts]),
    )(*parts, *arrived)


def attention_back_kernel(
    gains, mlp_row, source, to_left, to_right, middle_in, d_two_in, other_in, cot_own, cot_other,
    w_o_in, probs_in, *refs
):
    turned_in, kv_in, cos_in, sin_in = refs[0], refs[1:5], refs[5], refs[6]
    tok_own, tok_other, w_in, normed_in, mixed_in = refs[7:12]
    d_middle_out, part_own_out, part_send_out, sent_grads = refs[12:16]
    (
        middle, d_two, other, cot, w_o, probs, turned, k_lo, k_hi, v_lo, v_hi, cos, sin,
        d_middle, d_branch, d_mixed, d_pre, d_qkv,
        tok, w, perm, left, right, normed_p, mixed, grads, part_own, part_send, d_p, g_out,
        rows_of_gains, sems,
    ) = refs[16:]
    moves = Moves(sems)
    moves.start("rows", middle_in, middle)
    moves.start("rows", d_two_in, d_two)
    moves.start("rows", other_in, other)
    moves.start("rows", cot_own, cot.at[pl.ds(0, TOK), :])
    moves.start("rows", cot_other, cot.at[pl.ds(TOK, TOK), :])
    moves.start("w_o", w_o_in, w_o)
    fill(perm, source)
    fill(left, to_left)
    fill(right, to_right)
    moves.wait("rows")
    for far, to in zip((turned_in, *kv_in, cos_in, sin_in, probs_in),
                       (turned, k_lo, k_hi, v_lo, v_hi, cos, sin, probs)):
        moves.start("heads", far, to)
    for b in range(2):
        rows, swapped = slice(b * TOK, b * TOK + TOK), slice((1 - b) * TOK, (2 - b) * TOK)
        value = middle[rows, :]
        r2 = lax.rsqrt(jnp.mean(value * value, axis=1, keepdims=True) + EPS)
        e2 = gains[1:2, :] * (d_two[rows, :].astype(F32) + other[swapped, :].astype(F32))
        got = cot[rows, :].astype(F32) + r2 * (
            e2 - value * (r2 * r2 * jnp.mean(value * e2, axis=1, keepdims=True))
        )
        if b == 0:
            d_middle[...] = got
            moves.start("out", d_middle, d_middle_out)
        d_branch[rows, :] = got.astype(BF)
    moves.wait("w_o")
    d_mixed[...] = dot_t(d_branch[...], w_o[...]).astype(BF)
    moves.wait("heads")
    moves.start("normed", normed_in, normed_p)
    moves.start("mixed", mixed_in, mixed)
    moves.start("back", w_in.at[:, pl.ds(0, 1024)], w)
    moves.start("back", tok_own, tok.at[pl.ds(0, TOK), :])
    moves.start("back", tok_other, tok.at[pl.ds(TOK, TOK), :])

    def one_row(b, carry):
        rows = pl.ds(pl.multiple_of(b * TOK, TOK), TOK)
        d_k = {}
        d_v = {}
        for j in range(5):
            lanes = slice(128 * j, 128 * j + 128)
            q_pair, d_pair = turned[rows, lanes], d_mixed[rows, lanes]
            total = None
            for h in (2 * j, 2 * j + 1):
                if h == 9:
                    continue
                kv, half = h // 3, h % 2
                at_kv = slice(128 * kv, 128 * kv + 128)
                k_ref, v_ref = (k_lo, v_lo) if half == 0 else (k_hi, v_hi)
                p = probs[h, rows, :]
                p32 = p.astype(F32)
                d_probs = dot_t(d_pair, v_ref[rows, at_kv])
                row_dot = jnp.sum(p32 * d_probs, axis=1, keepdims=True)
                d_raw = (p32 * (d_probs - row_dot) * HEAD ** (-0.5)).astype(BF)
                got = dot(d_raw, k_ref[rows, at_kv])
                total = got if total is None else total + got
                for sums, value in ((d_k, t_dot(d_raw, q_pair)), (d_v, t_dot(p, d_pair))):
                    sums[kv, half] = value if (kv, half) not in sums else sums[kv, half] + value
            d_pre[:, lanes] = total
        low = low_lanes((TOK, 128))

        def collected(sums, kv, half):
            return sums[kv, half] + pltpu.roll(sums[kv, 1 - half], 64, 1)

        d_pre[:, 512:640] = jnp.where(low, d_pre[:, 512:640], collected(d_k, 0, 1))
        d_pre[:, 640:768] = jnp.where(low, collected(d_k, 1, 0), collected(d_k, 2, 1))
        for j in range(6):
            lanes = slice(128 * j, 128 * j + 128)
            d_qkv[rows, lanes] = turn(d_pre[:, lanes], cos[rows, :], -sin[rows, :]).astype(BF)
        d_qkv[rows, 768:896] = jnp.where(low, collected(d_v, 0, 0), collected(d_v, 1, 1)).astype(BF)
        d_qkv[rows, 896:1024] = jnp.where(low, collected(d_v, 2, 0), 0.0).astype(BF)
        return carry

    lax.fori_loop(0, 2, one_row, 0)
    moves.wait("normed")

    def qkv_grads(i, carry):
        lanes = pl.ds(pl.multiple_of(i * 256, 256), 256)
        grads[:, lanes] = t_dot(normed_p[...], d_qkv[:, lanes]).astype(BF)
        return carry

    lax.fori_loop(0, 4, qkv_grads, 0)
    moves.wait("mixed")
    g_out[...] = t_dot(mixed[...], d_branch[...]).astype(BF)
    grads[:, 1024:1536] = (
        t_dot(left[...], g_out[:, :512]) + t_dot(right[...], g_out[:, 640:])
    ).astype(BF)
    grads[:, 1536:] = t_dot(left[...], g_out[:, 512:640]).astype(BF)
    moves.wait("back")
    total = jnp.zeros((1, D), F32)
    for b in range(2):
        rows = slice(b * TOK, b * TOK + TOK)
        d_p[...] = dot_t(d_qkv[rows, :], w[...]).astype(BF)
        x = tok[rows, :].astype(F32)
        r1 = lax.rsqrt(jnp.mean(x * x, axis=1, keepdims=True) + EPS)
        got = dot_t(d_p[...], perm[...])
        total = total + jnp.sum(got * x * r1, axis=0, keepdims=True)
        if b == 0:
            part_own[...] = got
            moves.start("part", part_own, part_own_out)
        else:
            part_send[...] = got.astype(BF)
            moves.start("part", part_send, part_send_out)
    which = lax.broadcasted_iota(jnp.int32, (128, D), 0)
    rows_of_gains[...] = jnp.where(
        which == 64, total, jnp.where(which == 65, mlp_row[0:1, :], 0.0)
    ).astype(BF)
    gain_columns = dot(rows_of_gains[...], perm[...]).T
    grads[:, 896:1024] = (grads[:, 896:1024].astype(F32) + gain_columns).astype(BF)
    moves.start("grads", grads, sent_grads)
    moves.wait()


def attention_back(*args):
    outs = [shaped(TOK, D, F32), shaped(TOK, D, F32), shaped(TOK, D, BF), shaped(DP, 1664, BF)]
    return pl.pallas_call(
        attention_back_kernel,
        out_shape=outs,
        in_specs=[VMEM] * 5 + [FAR] * (len(args) - 5),
        out_specs=[FAR] * 4,
        scratch_shapes=[
            pltpu.VMEM((512, D), F32), *[pltpu.VMEM((512, D), BF)] * 3, pltpu.VMEM((640, D), BF),
            pltpu.VMEM((9, 512, 256), BF), pltpu.VMEM((512, 768), BF),
            *[pltpu.VMEM((512, 384), BF)] * 4, *[pltpu.VMEM((512, 128), F32)] * 2,
            pltpu.VMEM((TOK, D), F32), pltpu.VMEM((512, D), BF), pltpu.VMEM((512, 640), BF),
            pltpu.VMEM((TOK, 768), F32), pltpu.VMEM((512, 1024), BF),
            pltpu.VMEM((512, D), BF), pltpu.VMEM((DP, 1024), BF), pltpu.VMEM((D, DP), BF),
            *[pltpu.VMEM((640, DP), BF)] * 2, pltpu.VMEM((512, DP), BF), pltpu.VMEM((512, 640), BF),
            pltpu.VMEM((DP, 1664), BF), pltpu.VMEM((TOK, D), F32), pltpu.VMEM((TOK, D), BF),
            pltpu.VMEM((TOK, DP), BF), pltpu.VMEM((640, D), BF), pltpu.VMEM((128, D), BF),
            pltpu.SemaphoreType.DMA((40,)),
        ],
        compiler_params=params(60),
        cost_estimate=cost(10 * 10**9, [*args, *outs]),
    )(*args)


class Lockstep:
    def __init__(self):
        self.last = ()

    def tie(self, *values):
        tied = lax.optimization_barrier((*values, *self.last))
        self.last = tied
        return tied[: len(values)]

    def after(self, *values):
        self.last = (*self.last, *values)

    def __call__(self, values, pairs, late=(), late_pairs=(), beside=tuple):
        tied = lax.optimization_barrier((*values, *self.last))
        sent = [send(v, p) for v, p in zip(tied, pairs)]
        sent += [send(v, p) for v, p in zip(late, late_pairs)]
        sent += beside()
        self.last = lax.optimization_barrier(tuple(sent))
        return list(self.last)

    def gather(self, blocks, axes, more=(), more_pairs=()):
        values = [b for b in blocks for _ in range(3)]
        pairs = [STRAIGHT[a][n] for a in axes for n in (1, 2, 3)]
        got = self([*values, *more], [*pairs, *more_pairs])
        rings = [[b, *got[3 * i : 3 * i + 3]] for i, b in enumerate(blocks)]
        return rings, got[3 * len(blocks) :]

    def scatter(self, makers, axes, table, late=(), late_pairs=()):
        values = [make(s).astype(BF) for make in makers for s in (1, 2, 3)]
        pairs = [table[a][4 - s] for a in axes for s in (1, 2, 3)]
        got = self(values, pairs, late, late_pairs)
        sums = [
            sum([g.astype(F32) for g in got[3 * i : 3 * i + 3]], make(0).astype(F32))
            for i, make in enumerate(makers)
        ]
        return sums, got[3 * len(makers) :]


def place(blocks, at, sign):
    out = jnp.zeros((4, *blocks[0].shape), blocks[0].dtype)
    for step, block in enumerate(blocks):
        out = lax.dynamic_update_index_in_dim(out, block, (at - sign * step) % 4, 0)
    return out


def row_tables(segment_row):
    places = jnp.arange(TOK, dtype=jnp.int32)
    same_doc = segment_row[:, None] == segment_row[None, :]
    starts = jnp.min(jnp.where(same_doc, places[None, :], TOK), axis=1)
    offsets = (places - starts).astype(F32)
    lane = jnp.arange(128, dtype=jnp.int32)
    frequency = jnp.exp((lane % 32).astype(F32) * (-2.0 * math.log(THETA) / HEAD))
    angles = offsets[:, None] * frequency[None, :]
    side = jnp.where(lane % 64 < 32, -1.0, 1.0)
    allowed = same_doc & (places[:, None] >= places[None, :])
    return jnp.cos(angles), jnp.sin(angles) * side, jnp.where(allowed, 0.0, -1e30).astype(F32)


def body(
    tokens, segments, attn_gain, w_query, w_key, w_value, w_out, mlp_gain, w_gate, w_up, w_down,
    cotangent,
):
    core = lax.axis_index("core")
    at = {
        "x": lax.axis_index("x"),
        "y": lax.axis_index("y"),
        "z": lax.axis_index("z_hi") * 2 + lax.axis_index("z_lo"),
    }
    sign = 1 - 2 * core
    first = core == 0

    which = jnp.reshape(core, (1,)).astype(jnp.int32)
    kept, given, traded = halves(
        which, w_gate, w_up, w_query, w_key, w_value, attn_gain.reshape(1, 9),
        mlp_gain.reshape(1, 9), w_out, w_down,
    )
    step = Lockstep()
    given, traded, seg_other = step(
        [given, traded, segments.astype(F32)], [CORES, TRADE, CORES]
    )
    rows = jnp.concatenate([jnp.where(first, kept, given), jnp.where(first, given, kept)], axis=0)


    order_a, order_b, order_c = ("x", "z", "y"), ("y", "x", "z"), ("z", "y", "x")

    def natural(order):
        k = jnp.arange(D, dtype=jnp.int32)
        r, t = k % 18, k // 18
        c = {}
        for level, axis in enumerate(order):
            c[axis] = (at[axis] - (sign if level > 0 else 1) * ((t // 4**level) % 4)) % 4
        chip = (((c["z"] // 2) * 4 + c["x"]) * 2 + c["z"] % 2) * 4 + c["y"]
        return chip * 18 + r

    one, two, three = zip(order_a, order_b, order_c)
    z_rows = jnp.concatenate([rows[:, 3072:], jnp.zeros((18, 62), BF), traded], axis=1)
    got = step([z_rows] * 3, [STRAIGHT["z"][n] for n in (1, 2, 3)])
    z_at = jnp.reshape(at["z"], (1,)).astype(jnp.int32)
    w_attn, down = spread(z_at, z_rows, *got)
    w_attn = lax.all_gather(
        w_attn, AXES, axis=0, tiled=True, axis_index_groups=LINES["y", "x"]
    )
    (ha, hb), _ = step.gather([rows[:, :1536], rows[:, 1536:3072]], one[:2])
    rows_a, rows_b = natural(order_a), natural(order_b)

    k = jnp.arange(DP, dtype=jnp.int32)
    outer, inner, r, s = k // 320, (k // 80) % 4, (k % 80) % 18, (k % 80) // 18
    x_at, y_at = jnp.where(first, outer, inner), jnp.where(first, inner, outer)
    z = (at["z"] - s) % 4
    source = (((z // 2 * 4 + x_at) * 2 + z % 2) * 4 + y_at) * 18 + r
    source = jnp.where(s < 4, source, -1)
    e = ((x_at * 2 + z % 2) * 4 + y_at) * 2 + z // 2
    to_left = jnp.where((r < 9) & (s < 4), e * 9 + r, -1)
    to_right = jnp.where((r >= 9) & (s < 4), e * 9 + r - 9, -1)
    rows_a, rows_b, source = (i[None, :] for i in (rows_a, rows_b, source))
    ring = [RINGS[a] for a in two]
    held = [[stack_rows(ha), stack_rows(hb), down.reshape(96, D)]]
    *arrived, tok_other = step([*held[-1], tokens], [*ring, CORES])
    held.append(arrived)
    (w_attn,) = step.tie(w_attn)
    w_attn = lax.all_gather(
        w_attn, AXES, axis=0, tiled=True, axis_index_groups=LINES["x", "y"]
    )
    *arrived, cot_other = step([*held[-1], cotangent], [*ring, CORES])
    held.append(arrived)
    seg_other = seg_other.astype(jnp.int32)
    tables = [row_tables(segments[0]), row_tables(seg_other[0])]
    cos, sin, bias = (jnp.concatenate(t, axis=0) for t in zip(*tables))

    held.append(step(held[-1], ring))
    ha, hb, hc = zip(*held)
    ring = [RINGS[a] for a in three[:2]]
    down = place([h.reshape(2, 48, D) for h in hc], at["y"], sign)
    down = jnp.transpose(down, (1, 0, 2, 3)).reshape(384, D)
    held = [[jnp.concatenate(ha, axis=0), jnp.concatenate(hb, axis=0)]]
    wd = lax.all_gather(down, "x", axis=0, tiled=True)
    held.append(step(held[-1], ring))
    (w_attn,) = step.tie(w_attn)
    normed_p, turned, k_lo, k_hi, v_lo, v_hi, w_o, gains = attention_heads(
        tokens, tok_other, w_attn, source, to_left[None, :], to_right[None, :], cos, sin
    )
    probs, mixed, part, part_low = attention_forward(turned, k_lo, k_hi, v_lo, v_hi, w_o, bias)
    *arrived, part_low = step(held[-1], ring, beside=lambda: (part_low,))
    held.append(arrived)
    rows = middle_rows(gains, rows_a, rows_b, tokens, tok_other, part, swap(part_low))
    *arrived, middle, n2_a, n2_b, two_at, two_bt = step(held[-1], ring, beside=lambda: rows)
    held.append(arrived)
    ha, hb = zip(*held)

    act, d_gate, d_up, *grads = feed_forward(
        n2_a, n2_b, two_at, two_bt, cotangent, cot_other, *ha, *hb, wd
    )
    kept = (two_at, two_bt, d_gate, d_up)
    g_down = lax.psum_scatter(grads[6], "x", scatter_dimension=0, tiled=True)

    mlp_row, d_two = feed_back(rows_a, rows_b, middle, d_gate, d_up, *ha, *hb)
    *arrived, d_two = step([grads[0], grads[3]], ring, beside=lambda: (d_two,))
    sums = added([grads[1], grads[4]], arrived)
    d_middle, part_own, part_send, g_attn = attention_back(
        gains, mlp_row, source, to_left[None, :], to_right[None, :], middle, d_two, swap(d_two),
        cotangent, cot_other, w_o, probs, turned, k_lo, k_hi, v_lo, v_hi, cos, sin, tokens,
        tok_other, w_attn, normed_p, mixed,
    )
    *kept, act, part_send = lax.optimization_barrier((*kept, act, part_send))
    *arrived, part_send, g_attn = step(sums, ring, beside=lambda: (part_send, g_attn))
    sums = added([grads[2], grads[5]], arrived)
    out_own, out_send = feed_out(middle, act, wd)
    *arrived, part_other, out_send = step(
        [*sums, part_send], [*ring, CORES], beside=lambda: (out_send,)
    )
    g_gate, g_up = added(feed_grads(0, *kept), arrived)
    g_attn_x = lax.psum_scatter(
        g_attn, AXES, scatter_dimension=0, tiled=True, axis_index_groups=LINES["x", "y"]
    )
    g_attn = lax.psum_scatter(
        g_attn_x, AXES, scatter_dimension=0, tiled=True, axis_index_groups=LINES["y", "x"]
    )

    d_normed = part_own + part_other.astype(F32)
    x_own = tokens.astype(F32)
    r_own = lax.rsqrt(jnp.mean(x_own * x_own, axis=-1, keepdims=True) + EPS)
    e1 = d_normed * gains[0]
    grad_input = d_middle + r_own * (
        e1 - x_own * r_own * r_own * jnp.mean(x_own * e1, axis=-1, keepdims=True)
    )

    def rows_of(held, n):
        return lambda s: held[n * s : n * s + n]

    def y_block(s):
        down = g_down.reshape(2, 4, 48, D)
        return lax.dynamic_index_in_dim(down, (at["y"] - sign * s) % 4, 1, False).reshape(96, D)

    (g_up,), (out_other,) = step.scatter(
        [rows_of(g_up, 72)], two[1:2], SIGNED, [out_send], [CORES]
    )
    output = (out_own + out_other.astype(F32)).astype(BF)
    step.after(g_attn_x)
    (g_gate, g_down), _ = step.scatter(
        [rows_of(g_gate, 72), y_block], (two[0], two[2]), SIGNED
    )
    own, *packed = pack(z_at, g_attn, g_down.astype(BF).reshape(4, 24, D))
    (g_gate, g_up), got = step.scatter(
        [rows_of(g_gate, 18), rows_of(g_up, 18)], one[:2], STRAIGHT,
        packed, [STRAIGHT["z"][4 - s] for s in (1, 2, 3)],
    )
    g_z = sum([g.astype(F32) for g in got], own.astype(F32))

    g_rows = jnp.concatenate([g_gate, g_up, g_z[:, :962]], axis=1)
    mine = jnp.where(first, g_rows[:9], g_rows[9:])
    theirs = jnp.where(first, g_rows[9:], g_rows[:9]).astype(BF)
    theirs, g_od = step([theirs, g_z[:, 1024:].astype(BF)], [CORES, TRADE])
    g_g, g_u, g_q, g_k, g_v, g_o, g_d, g_gains = whole(which, mine, theirs, g_od)
    return (
        output, grad_input, g_gains[0], g_q, g_k, g_v, g_o, g_gains[1], g_g, g_u, g_d,
    )


def solution(mesh):
    fine = Mesh(mesh.devices.reshape(SHAPE), AXES)
    rows, vector = P(AXES, None), P(AXES)
    return jax.shard_map(
        body,
        mesh=fine,
        in_specs=(rows, rows, vector, rows, rows, rows, rows, vector, rows, rows, rows, rows),
        out_specs=(rows, rows, vector, rows, rows, rows, rows, vector, rows, rows, rows),
        check_vma=False,
    )
```
